32 devices in a mesh: obj: 8 (over z, y), blk: 4 (over x, core).
Axes of the slice: x: 2, y: 2, z: 4, core: 2. Of those that a mesh axis runs over, the one named last changes fastest.
Arguments:
- tokens: bfloat16 [8, 3072, 512], P('obj', 'blk'), may hold values from -6 to 6
- context: bfloat16 [8, 581, 384], P('obj'), may hold values from -6 to 6
- camera_groups: int32 [8], P('obj'), may hold values from 0 to 7
- camera_table: bfloat16 [8, 1024], replicated, may hold values from -6 to 6
- cross_query: bfloat16 [512, 512], replicated, may hold values from -0.25 to 0.25
- cross_kv: bfloat16 [384, 1024], replicated, may hold values from -0.3125 to 0.3125
- cross_out: bfloat16 [512, 512], replicated, may hold values from -4 to 4
- self_qkv: bfloat16 [512, 1536], replicated, may hold values from -0.25 to 0.25
- self_out: bfloat16 [512, 512], replicated, may hold values from -6 to 6
- mlp_up: bfloat16 [512, 2048], replicated, may hold values from -0.25 to 0.25
- mlp_down: bfloat16 [2048, 512], replicated, may hold values from -0.125 to 0.125
- norm_gain: bfloat16 [3, 512], replicated, may hold values from 0.25 to 1.75
- norm_bias: bfloat16 [3, 512], replicated, may hold values from -4 to 4
- mod_weight: bfloat16 [3, 1024, 1024], replicated, may hold values from -0.09375 to 0.09375
- mod_bias: bfloat16 [3, 1024], replicated, may hold values from -4 to 4
- cotangent: bfloat16 [8, 3072, 512], P('obj', 'blk'), may hold values from -6 to 6
Outputs:
- mixed: bfloat16 [8, 3072, 512], P('obj', 'blk')
- tokens_grad: float32 [8, 3072, 512], P('obj', 'blk')
- context_grad: float32 [8, 581, 384], P('obj')
- cross_query_grad: float32 [512, 512], P(None, 'blk')
- cross_kv_grad: float32 [384, 1024], P(None, 'blk')
- cross_out_grad: float32 [512, 512], P(None, 'blk')
- self_qkv_grad: float32 [512, 1536], P(None, 'blk')
- self_out_grad: float32 [512, 512], P(None, 'blk')
- mlp_up_grad: float32 [512, 2048], P(None, 'blk')
- mlp_down_grad: float32 [2048, 512], P(None, 'blk')
- norm_gain_grad: float32 [3, 512], P(None, 'blk')
- norm_bias_grad: float32 [3, 512], P(None, 'blk')
- mod_weight_grad: float32 [3, 1024, 1024], P(None, None, 'blk')
- mod_bias_grad: float32 [3, 1024], P(None, 'blk')
The draws below stay inside these ranges and needn't reach their ends.
All inputs are finite; a program needn't handle non-finite values.
Results may differ from the reference program's by a relative error of at most 0.02.
Values may be sent and summed in bfloat16 or wider, within the bound.
A program may use at most 320 MiB of HBM per device.

```python
import math
import jax
import jax.numpy as jnp
from jax import lax

D = 512
HEADS = 8
FF = 2048
CTXW = 384
CAM = 1024
CTX = 581
OBJ_LEN = 3072
GROUPS = 8
HEAD_DIM = 64
OBJECTS = 8


def set_ends(drawn, rng, least, top_value):
    longest = drawn.shape.index(max(drawn.shape))
    spots = []
    for shift in (0, 1):
        where = [jax.random.randint(jax.random.fold_in(rng, axis), (), 0, length) for axis, length in enumerate(drawn.shape)]
        where[longest] = (where[longest] + shift) % drawn.shape[longest]
        spots.append(tuple(where))
    return drawn.at[spots[0]].set(least).at[spots[1]].set(top_value)


def steps_of(own_key, dims, shards, smallest, top_value):
    gain = 1.0
    for axis_at, shards_of in shards:
        steps = jax.random.uniform(jax.random.fold_in(jax.random.fold_in(own_key, 6), axis_at), (shards_of,), jnp.float32, smallest / len(shards), top_value / len(shards))
        gain = gain * jnp.repeat(jnp.exp(steps), dims[axis_at] // shards_of).reshape((-1,) + (1,) * (len(dims) - 1 - axis_at))
    return gain


def bell_draw(stream_key, shape, width, reach, cuts=(), held_as=jnp.bfloat16):
    loudness = steps_of(stream_key, shape, cuts, -0.22, 0.18) if cuts else 1.0
    values = jax.random.normal(stream_key, shape, jnp.float32) * width * loudness
    return jnp.minimum(jnp.maximum(values, -reach), reach).astype(held_as)


def setup_inputs(seed: int = 0) -> dict:
    key_of = jax.random.split(jax.random.key(seed), 17)
    tokens = bell_draw(key_of[0], (OBJECTS, OBJ_LEN, D), 1.0, 6.0, ((0, 8), (1, 4)))
    context = bell_draw(key_of[1], (OBJECTS, CTX, CTXW), 1.0, 6.0, ((0, 8),))
    camera_groups = set_ends(jax.random.randint(key_of[2], (OBJECTS,), 0, GROUPS), jax.random.fold_in(key_of[2], 1), 0, GROUPS - 1).astype(jnp.int32)
    camera_table = bell_draw(key_of[3], (GROUPS, CAM), 1.0, 6.0)
    cross_query = bell_draw(key_of[4], (D, D), D ** -0.5, 0.25)
    cross_kv = bell_draw(key_of[5], (CTXW, 2 * D), CTXW ** -0.5, 0.3125)
    cross_out = bell_draw(key_of[6], (D, D), 2 ** -0.5, 4.0)
    self_qkv = bell_draw(key_of[7], (D, 3 * D), D ** -0.5, 0.25)
    self_out = bell_draw(key_of[8], (D, D), 1 ** -0.5, 6.0)
    mlp_up = bell_draw(key_of[9], (D, FF), D ** -0.5, 0.25)
    mlp_down = bell_draw(key_of[10], (FF, D), FF ** -0.5, 0.125)
    norm_gain = jnp.clip(1.0 + 0.15 * jax.random.normal(key_of[11], (3, D), jnp.float32), 0.25, 1.75).astype(jnp.bfloat16)
    norm_bias = bell_draw(key_of[12], (3, D), 0.3, 4.0)
    mod_weight = bell_draw(key_of[13], (3, CAM, 2 * D), (4 * CAM) ** -0.5, 0.09375)
    mod_bias = bell_draw(key_of[14], (3, 2 * D), 0.3, 4.0)
    cotangent = bell_draw(key_of[15], (OBJECTS, OBJ_LEN, D), 1.0, 6.0, ((0, 8), (1, 4)))
    return dict(tokens=tokens, context=context, camera_groups=camera_groups, camera_table=camera_table, cross_query=cross_query, cross_kv=cross_kv, cross_out=cross_out, self_qkv=self_qkv, self_out=self_out, mlp_up=mlp_up, mlp_down=mlp_down, norm_gain=norm_gain, norm_bias=norm_bias, mod_weight=mod_weight, mod_bias=mod_bias, cotangent=cotangent)


@jax.custom_vjp
def low(v):
    return lax.optimization_barrier(v.astype(jnp.bfloat16)).astype(jnp.float32)

@jax.custom_vjp
def low_back(v):
    return v

def low_keep(v):
    return (low(v), None)

def low_pass(kept, grad):
    return (grad,)

def back_keep(v):
    return (v, None)

def back_low(kept, grad):
    return (low(grad),)
low.defvjp(low_keep, low_pass)
low_back.defvjp(back_keep, back_low)
epsilon = 1e-06
highest = lax.Precision.HIGHEST

def product(left, right):
    return jnp.dot(left, right, precision=highest, preferred_element_type=jnp.float32)

def modulate(inputs, gain_row, offset, shift_row, scale_row):
    center = inputs - lax.optimization_barrier(jnp.mean(inputs, -1, keepdims=True))
    normed = center * lax.rsqrt(lax.optimization_barrier(jnp.mean(center * center, -1, keepdims=True)) + epsilon)
    return (normed * gain_row + offset) * (1.0 + scale_row) + shift_row

def attend(queries, key_rows, values):
    row_count = queries.shape[0]
    height = math.gcd(row_count, 512)
    key_heads = key_rows.reshape(-1, HEADS, HEAD_DIM)
    value_heads = values.reshape(-1, HEADS, HEAD_DIM)
    factor = HEAD_DIM ** (-0.5)

    def query_block(query_rows):
        query_heads = query_rows.reshape(height, HEADS, HEAD_DIM)
        scores = low_back(jnp.einsum('qhd,khd->hqk', query_heads, key_heads, precision=highest) * factor)
        weights = jnp.exp(scores - lax.optimization_barrier(jnp.max(scores, -1, keepdims=True)))
        summed = lax.optimization_barrier(jnp.sum(weights, -1, keepdims=True))
        merged = jnp.einsum('hqk,khd->hqd', low(weights), value_heads, precision=highest) / summed
        return jnp.transpose(merged, (1, 0, 2)).reshape(height, D)
    blocks = lax.map(jax.checkpoint(query_block), queries.reshape(row_count // height, height, D))
    return blocks.reshape(row_count, D)

def layer_forward(params, tokens, context, camera):
    cross_query, cross_kv, cross_out, self_qkv, self_out, mlp_up, mlp_down, norm_gain, norm_bias, mod_weight, mod_bias = params
    lifted = low(jax.nn.silu(camera))
    modulations = [product(lifted[None, :], mod_weight[position])[0] + mod_bias[position] for position in range(3)]

    def norm_at(inputs, position):
        return modulate(inputs, norm_gain[position], norm_bias[position], modulations[position][:D], modulations[position][D:])
    first_in = low(norm_at(tokens, 0))
    cross_q = low(low_back(product(first_in, cross_query)))
    cross_pair = low(low_back(product(low(context), cross_kv)))
    cross_att = low_back(attend(cross_q, cross_pair[:, :D], cross_pair[:, D:]))
    after_one = tokens + low_back(product(low(cross_att), cross_out))
    second_in = low(norm_at(after_one, 1))
    joint_rows = low(low_back(product(second_in, self_qkv)))
    self_att = low_back(attend(joint_rows[:, :D], joint_rows[:, D:2 * D], joint_rows[:, 2 * D:]))
    after_two = after_one + low_back(product(low(self_att), self_out))
    third_in = low(norm_at(after_two, 2))
    hidden = low_back(product(third_in, mlp_up))
    return after_two + low_back(product(low(jax.nn.gelu(hidden)), mlp_down))

def reference(tokens, context, camera_groups, camera_table, cross_query, cross_kv, cross_out, self_qkv, self_out, mlp_up, mlp_down, norm_gain, norm_bias, mod_weight, mod_bias, cotangent):
    params = tuple((weight.astype(jnp.float32) for weight in (cross_query, cross_kv, cross_out, self_qkv, self_out, mlp_up, mlp_down, norm_gain, norm_bias, mod_weight, mod_bias)))
    cameras = camera_table.astype(jnp.float32)[camera_groups]

    def per_object(running, object_item):
        token_rows, context_rows, camera_row, cotangent_rows = object_item

        def forward(weights, inputs, memory):
            return layer_forward(weights, inputs, memory, camera_row)
        output, pullback = jax.vjp(forward, params, token_rows, context_rows)
        gradients, token_grad, memory_grad = pullback(cotangent_rows)
        running = jax.tree.map(jnp.add, running, gradients)
        return (running, (output.astype(jnp.bfloat16), token_grad, memory_grad))
    zero_grads = jax.tree.map(jnp.zeros_like, params)
    totals, outputs = lax.scan(per_object, zero_grads, (tokens.astype(jnp.float32), context.astype(jnp.float32), cameras, cotangent.astype(jnp.float32)))
    mixed, tokens_grad, context_grad = outputs
    return (mixed, tokens_grad, context_grad, totals[0], totals[1], totals[2], totals[3], totals[4], totals[5], totals[6], totals[7], totals[8], totals[9], totals[10])
```

```python
import functools

import jax
import jax.numpy as jnp
from jax import lax
from jax.experimental import pallas as pl
from jax.experimental.pallas import tpu as pltpu
from jax.sharding import PartitionSpec as P

D = 512
HEADS = 8
HEAD_DIM = 64
PAIRS = HEADS // 2
WIDE = 2 * HEAD_DIM
LOG2E = 1.4426950408889634
LN2 = 0.6931471805599453
QUERY_FACTOR = LOG2E * HEAD_DIM ** (-0.5)
SCORE_FACTOR = HEAD_DIM ** (-0.5)
SAFE_SQUARE = 60.0 ** 2
EPSILON = 1e-06
GELU_A = 0.7978845608028654
GELU_B = 0.044715
MIB = 2**20

f32 = jnp.float32
bf16 = jnp.bfloat16
VMEM = pltpu.VMEM


def nn(a, b):
    return lax.dot_general(a, b, (((1,), (0,)), ((), ())), preferred_element_type=f32)


def nt(a, b):
    return lax.dot_general(a, b, (((1,), (1,)), ((), ())), preferred_element_type=f32)


def tn(a, b):
    return lax.dot_general(a, b, (((0,), (0,)), ((), ())), preferred_element_type=f32)


def whole():
    return pl.BlockSpec(memory_space=VMEM)


def params(mib=60):
    return pltpu.CompilerParams(vmem_limit_bytes=mib * MIB)


def lower_half(shape):
    return lax.broadcasted_iota(jnp.int32, shape, 1) % WIDE < HEAD_DIM


def own_half(shape, odd):
    lower = lower_half(shape)
    return jnp.logical_not(lower) if odd else lower


def normalize(x):
    center = x - jnp.mean(x, -1, keepdims=True)
    inverse = lax.rsqrt(jnp.mean(center * center, -1, keepdims=True) + EPSILON)
    return center * inverse, inverse


def modulate(x, gain, bias, shift, scale):
    normed, _ = normalize(x)
    return (normed * gain + bias) * (1.0 + scale) + shift


def modulate_back(g, x, gain, bias, scale):
    normed, inverse = normalize(x)
    affine = normed * gain + bias
    shift_grad = jnp.sum(g, 0, keepdims=True)
    scale_grad = jnp.sum(g * affine, 0, keepdims=True)
    a = g * (1.0 + scale)
    gain_grad = jnp.sum(a * normed, 0, keepdims=True)
    bias_grad = jnp.sum(a, 0, keepdims=True)
    n = a * gain
    back = inverse * (
        n - jnp.mean(n, -1, keepdims=True) - normed * jnp.mean(n * normed, -1, keepdims=True)
    )
    return back, jnp.concatenate([shift_grad, scale_grad, gain_grad, bias_grad], 0)


def norm_rows(gain_ref, bias_ref, mod_ref, j):
    gain = gain_ref[j : j + 1, :].astype(f32)
    bias = bias_ref[j : j + 1, :].astype(f32)
    shift = mod_ref[j : j + 1, :D]
    scale = mod_ref[j : j + 1, D:]
    return gain, bias, shift, scale


def head_sums(values, sign):
    rows = lax.broadcasted_iota(jnp.int32, (WIDE, WIDE), 0)
    cols = lax.broadcasted_iota(jnp.int32, (WIDE, WIDE), 1)
    block = jnp.where((rows < HEAD_DIM) != (cols < HEAD_DIM), sign, 0.0).astype(bf16)
    high = values.astype(bf16)
    low = (values - high.astype(f32)).astype(bf16)
    return nn(high, block) + nn(low, block)


def delta_lanes(product):
    parts = []
    for p in range(PAIRS):
        total = head_sums(product[:, p * WIDE : (p + 1) * WIDE], -1.0)
        high = total.astype(bf16).astype(f32)
        low = total - high
        lane = lax.broadcasted_iota(jnp.int32, total.shape, 1) % HEAD_DIM
        parts.append(jnp.where(lane == 0, high, jnp.where(lane == 1, low, 0.0)).astype(bf16))
    return jnp.concatenate(parts, 1)


def bounded(q, k):
    ok = None
    for p in range(PAIRS):
        cols = slice(p * WIDE, (p + 1) * WIDE)
        qp = q[:, cols].astype(f32)
        kp = k[:, cols].astype(f32)
        q_top = jnp.max(head_sums(qp * qp, 1.0))
        k_top = jnp.max(head_sums(kp * kp, 1.0))
        here = q_top * k_top < SAFE_SQUARE
        ok = here if ok is None else jnp.logical_and(ok, here)
    return ok


def attend_pair(safe, q_pair, k_pair, v_pair, w_ref, rows, real_keys):
    keys = k_pair.shape[0]
    count = q_pair.shape[0]
    outs = []
    for odd in (0, 1):
        own_k = own_half(k_pair.shape, odd)
        k_h = jnp.where(own_k, k_pair, jnp.zeros_like(k_pair))
        v_h = value_rows(v_pair, odd, real_keys)

        def blocks(shifted):
            parts = []
            for r in range(0, count, rows):
                s = nt(q_pair[r : r + rows], k_h)
                if shifted:
                    s = s - jnp.max(s, -1, keepdims=True)
                w = jnp.exp2(s).astype(bf16)
                w_ref[odd, r : r + rows, :] = w
                parts.append(nn(w, v_h))
            return jnp.concatenate(parts, 0)

        outs.append(lax.cond(safe, lambda: blocks(False), lambda: blocks(True)))
    lower = lower_half(outs[0].shape)
    merged = jnp.where(lower, outs[0], outs[1])
    sums = pltpu.roll(jnp.where(lower, outs[1], outs[0]), HEAD_DIM, 1)
    inverse = 1.0 / sums
    return merged * inverse, inverse


def value_rows(v_pair, odd, real_keys):
    own = own_half(v_pair.shape, odd)
    v_h = jnp.where(own, v_pair, jnp.ones_like(v_pair))
    if real_keys < v_pair.shape[0]:
        row = lax.broadcasted_iota(jnp.int32, v_pair.shape, 0)
        v_h = jnp.where(row < real_keys, v_h, jnp.zeros_like(v_h))
    return v_h


def attend_back_pair(do_pair, x_pair, do_t, q_t, k_pair, v_pair, w_of, chunk, real_keys, dkt_ref, dvt_ref):
    keys = k_pair.shape[0]
    dq = None
    for odd in (0, 1):
        own_q = own_half(do_pair.shape, odd)
        left = jnp.where(own_q, do_pair, x_pair)
        own_k = own_half(k_pair.shape, odd)
        k_h = jnp.where(own_k, k_pair, jnp.zeros_like(k_pair))
        v_h = value_rows(v_pair, odd, real_keys)
        head = slice(odd * HEAD_DIM, (odd + 1) * HEAD_DIM)
        for c in range(0, keys, chunk):
            cols = slice(c, c + chunk)
            w = w_of(odd, cols)
            dp = nt(left, v_h[cols])
            ds = (w.astype(f32) * dp).astype(bf16)
            part = nn(ds, k_h[cols])
            dq = part if dq is None else dq + part
            dkt_ref[head, cols] = (nn(q_t[head], ds) * LN2).astype(dkt_ref.dtype)
            dvt_ref[head, cols] = nn(do_t[head], w).astype(dvt_ref.dtype)
    return dq * SCORE_FACTOR


def cross_kernel(
    context_count, tokens, context, wq, wkv, wo, gain, bias, mod,
    second_in, after_one, q_out, pair_out, w_out, att_out, inv_out,
):
    x = tokens[...].astype(f32)
    first_in = modulate(x, *norm_rows(gain, bias, mod, 0)).astype(bf16)
    q = (nn(first_in, wq[...]) * QUERY_FACTOR).astype(bf16)
    pair = nn(context[...], wkv[...]).astype(bf16)
    q_out[...] = q
    pair_out[...] = pair
    safe = bounded(q, pair[:, :D])
    rows = min(256, q.shape[0])
    for p in range(PAIRS):
        cols = slice(p * WIDE, (p + 1) * WIDE)
        vcols = slice(D + p * WIDE, D + (p + 1) * WIDE)
        att, inverse = attend_pair(
            safe, q[:, cols], pair[:, cols], pair[:, vcols],
            w_out.at[2 * p : 2 * p + 2], rows, context_count,
        )
        att_out[:, cols] = att
        inv_out[:, cols] = inverse
    one = x + nn(att_out[...].astype(bf16), wo[...])
    after_one[...] = one
    second_in[...] = modulate(one, *norm_rows(gain, bias, mod, 1)).astype(bf16)


def self_kernel(own_in, all_in, wqkv, w_out, att_out, inv_out, q_out, kv_out, safe_ref):
    length = all_in.shape[0]
    g = pl.program_id(0)

    @pl.when(g == 0)
    def _():
        q_out[...] = (nn(own_in[...], wqkv[:, :D]) * QUERY_FACTOR).astype(bf16)
        step = 768 if length % 768 == 0 else length
        for r in range(0, length, step):
            kv_out[r : r + step, :] = nn(all_in[r : r + step, :], wqkv[:, D:]).astype(bf16)
        ok = bounded(q_out[...], kv_out[:, :D])
        safe_ref[0] = ok.astype(jnp.int32)

    cols = pl.ds(pl.multiple_of(g * WIDE, WIDE), WIDE)
    vcols = pl.ds(pl.multiple_of(D + g * WIDE, WIDE), WIDE)
    att, inverse = attend_pair(
        safe_ref[0] == 1, q_out[:, cols], kv_out[:, cols], kv_out[:, vcols],
        w_out, min(256, own_in.shape[0]), length,
    )
    att_out[:, cols] = att
    inv_out[:, cols] = inverse


def slabs(out_ref, base, grad):
    parts = out_ref.shape[0]
    rows, columns = grad.shape
    each = columns // parts
    lanes = out_ref.shape[2]
    for b in range(parts):
        for i in range(each // lanes):
            start = b * each + i * lanes
            out_ref[b, base + i * rows : base + (i + 1) * rows, :] = grad[
                :, start : start + lanes
            ].astype(out_ref.dtype)


def mlp_kernel(
    self_att, after_one, inv, cotangent, wo, up, down, gain, bias, mod,
    mixed, grad_two, do_out, x_out, modes, g_out,
):
    self_low = self_att[...].astype(bf16)
    two = after_one[...] + nn(self_low, wo[...])
    rows3 = norm_rows(gain, bias, mod, 2)
    third_in = modulate(two, *rows3).astype(bf16)
    cot = cotangent[...]
    final = two
    norm_grad = jnp.zeros_like(two)
    ff = up.shape[1]
    step = 512
    up_base = D * (D // g_out.shape[0] // g_out.shape[2])
    for f in range(0, ff, step):
        hidden = nn(third_in, up[:, f : f + step])
        square = hidden * hidden
        inner = GELU_A * hidden * (1.0 + GELU_B * square)
        t = jnp.tanh(inner)
        half = 0.5 * (1.0 + t)
        active = (hidden * half).astype(bf16)
        slope = half + 0.5 * hidden * (1.0 - t * t) * (GELU_A * (1.0 + 3.0 * GELU_B * square))
        final = final + nn(active, down[f : f + step, :])
        hidden_grad = (nt(cot, down[f : f + step, :]) * slope).astype(bf16)
        norm_grad = norm_grad + nt(hidden_grad, up[:, f : f + step])
        up_part = tn(third_in, hidden_grad)
        down_part = tn(active, cot)
        parts, _, lanes = g_out.shape
        each = ff // parts
        for i in range(step // lanes):
            col = f + i * lanes
            b, inside = col // each, col % each // lanes
            base = up_base + inside * D
            g_out[b, base : base + D, :] = up_part[:, i * lanes : (i + 1) * lanes].astype(bf16)
        down_base = up_base + D * (each // lanes)
        for b in range(parts):
            for i in range(D // parts // lanes):
                start = b * (D // parts) + i * lanes
                base = down_base + i * ff + f
                g_out[b, base : base + step, :] = down_part[:, start : start + lanes].astype(bf16)
    mixed[...] = final.astype(bf16)
    back, sums = modulate_back(norm_grad, two, rows3[0], rows3[1], rows3[3])
    modes[...] = sums
    grad = cot.astype(f32) + back
    grad_two[...] = grad
    self_grad = grad.astype(bf16)
    slabs(g_out, 0, tn(self_low, self_grad))
    do = (nt(self_grad, wo[...]) * inv[...]).astype(bf16)
    do_out[...] = do
    x_out[...] = delta_lanes(do.astype(f32) * self_att[...])


def self_back_kernel(do, x, q, kv, w, dq_out, dkvt_out, do_t, q_t):
    g = pl.program_id(0)

    @pl.when(g == 0)
    def _():
        do_t[...] = do[...].T
        q_t[...] = q[...].T

    length = kv.shape[0]
    cols = pl.ds(pl.multiple_of(g * WIDE, WIDE), WIDE)
    vcols = pl.ds(pl.multiple_of(D + g * WIDE, WIDE), WIDE)
    dq = attend_back_pair(
        do[:, cols], x[:, cols], do_t[cols, :], q_t[cols, :], kv[:, cols], kv[:, vcols],
        lambda odd, c: w[odd, :, c], 512, length, dkvt_out.at[cols, :], dkvt_out.at[vcols, :],
    )
    dq_out[:, cols] = dq.astype(bf16)


def joint_back_kernel(all_in, own_in, dq, dkvt, wqkv, part_out, own_part, g_out):
    length = all_in.shape[0]
    step = 512
    for c in range(0, length, step):
        part_out[c : c + step, :] = tn(dkvt[:, c : c + step], wqkv_t(wqkv)).astype(bf16)
    own_part[...] = nt(dq[...], wqkv[:, :D])
    grad_q = tn(own_in[...], dq[...])
    grad_kv = nn(dkvt[...], all_in[...]).T
    slabs(g_out, 0, jnp.concatenate([grad_q, grad_kv], 1))


def wqkv_t(wqkv):
    return wqkv[:, D:].T


def cross_back_kernel(
    context_count, norm_part, own_part, grad_two, after_one, tokens, context, q, pair, w, att, inv,
    wq, wkv, wo, gain, bias, mod,
    tokens_grad, context_out, modes, g_out, dkvt,
):
    rows2 = norm_rows(gain, bias, mod, 1)
    back, sums_two = modulate_back(
        norm_part[...].astype(f32) + own_part[...], after_one[...], rows2[0], rows2[1], rows2[3]
    )
    grad_one = grad_two[...] + back
    cross_grad = grad_one.astype(bf16)
    out_rows = D * (D // g_out.shape[0] // g_out.shape[2])
    slabs(g_out, 0, tn(att[...].astype(bf16), cross_grad))
    do = (nt(cross_grad, wo[...]) * inv[...]).astype(bf16)
    x = delta_lanes(do.astype(f32) * att[...])
    do_t = do.T
    q_t = q[...].T
    parts = []
    for p in range(PAIRS):
        cols = slice(p * WIDE, (p + 1) * WIDE)
        vcols = slice(D + p * WIDE, D + (p + 1) * WIDE)
        dq = attend_back_pair(
            do[:, cols], x[:, cols], do_t[cols, :], q_t[cols, :], pair[:, cols], pair[:, vcols],
            lambda odd, c, p=p: w[2 * p + odd, :, c], pair.shape[0], context_count,
            dkvt.at[cols, :], dkvt.at[vcols, :],
        )
        parts.append(dq.astype(bf16))
    dq = jnp.concatenate(parts, 1)
    first = tokens[...].astype(f32)
    rows1 = norm_rows(gain, bias, mod, 0)
    first_in = modulate(first, *rows1).astype(bf16)
    slabs(g_out, out_rows, tn(first_in, dq))
    back, sums_one = modulate_back(nt(dq, wq[...]), first, rows1[0], rows1[1], rows1[3])
    tokens_grad[...] = grad_one + back
    modes[...] = jnp.concatenate([sums_one, sums_two], 0)
    real = lax.broadcasted_iota(jnp.int32, dkvt.shape, 1) < context_count
    kept = jnp.where(real, dkvt[...], jnp.zeros_like(dkvt))
    slabs(g_out, 2 * out_rows, nn(kept, context[...]).T)
    context_out[...] = tn(dkvt[...], wkv[...].T).astype(bf16)


def shape(dims, dtype):
    return jax.ShapeDtypeStruct(tuple(dims), dtype)


def body(
    tokens, context, camera_groups, camera_table, cross_query, cross_kv, cross_out, self_qkv,
    self_out, mlp_up, mlp_down, norm_gain, norm_bias, mod_weight, mod_bias, cotangent,
):
    parts = lax.axis_size("blk")
    tokens = tokens[0]
    cotangent = cotangent[0]
    context_count = context.shape[1]
    rows = tokens.shape[0]
    length = rows * parts
    ff = mlp_up.shape[1]
    cam_width = mod_weight.shape[1]
    ctx_width = context.shape[2]
    padded = -(-context_count // 128) * 128
    context_rows = jnp.pad(context[0], ((0, padded - context_count), (0, 0)), mode="edge")

    picked = (
        camera_groups[:, None] == jnp.arange(camera_table.shape[0], dtype=jnp.int32)[None, :]
    ).astype(bf16)
    camera = jnp.dot(picked, camera_table, preferred_element_type=f32)
    lifted = jax.nn.silu(camera).astype(bf16)
    mod = (
        jnp.einsum("oc,jcm->ojm", lifted, mod_weight, preferred_element_type=f32)
        + mod_bias.astype(f32)
    )[0]

    second_in, after_one, cross_q, cross_pair, cross_w, cross_att, cross_inv = pl.pallas_call(
        functools.partial(cross_kernel, context_count),
        out_shape=[
            shape((rows, D), bf16), shape((rows, D), f32), shape((rows, D), bf16),
            shape((padded, 2 * D), bf16), shape((HEADS, rows, padded), bf16),
            shape((rows, D), f32), shape((rows, D), f32),
        ],
        in_specs=[whole()] * 8,
        out_specs=[whole()] * 7,
        compiler_params=params(),
        name="cross_forward",
    )(tokens, context_rows, cross_query, cross_kv, cross_out, norm_gain, norm_bias, mod)

    all_in = lax.all_gather(second_in, "blk", axis=0, tiled=True)

    full = lambda *dims: pl.BlockSpec(dims, lambda g: (0,) * len(dims))
    self_w, self_att, self_inv, self_q, self_kv = pl.pallas_call(
        self_kernel,
        grid=(PAIRS,),
        out_shape=[
            shape((HEADS, rows, length), bf16), shape((rows, D), f32), shape((rows, D), f32),
            shape((rows, D), bf16), shape((length, 2 * D), bf16),
        ],
        in_specs=[full(rows, D), full(length, D), full(D, 3 * D)],
        out_specs=[
            pl.BlockSpec((2, rows, length), lambda g: (g, 0, 0)),
            full(rows, D), full(rows, D), full(rows, D), full(length, 2 * D),
        ],
        scratch_shapes=[pltpu.SMEM((1,), jnp.int32)],
        compiler_params=params(),
        name="self_forward",
    )(second_in, all_in, self_qkv)

    each = D // parts
    lanes = min(128, each)
    tall = lambda columns, depth: depth * (columns // parts // lanes)
    early = tall(D, D) + tall(ff, D) + tall(D, ff)
    mixed, grad_two, self_do, self_x, modes_three, g_early = pl.pallas_call(
        mlp_kernel,
        out_shape=[
            shape((rows, D), bf16), shape((rows, D), f32), shape((rows, D), bf16),
            shape((rows, D), bf16), shape((4, D), f32), shape((parts, early, lanes), bf16),
        ],
        in_specs=[whole()] * 10,
        out_specs=[whole()] * 6,
        compiler_params=params(),
        name="feed_forward",
    )(self_att, after_one, self_inv, cotangent, self_out, mlp_up, mlp_down, norm_gain, norm_bias, mod)

    dq, dkvt = pl.pallas_call(
        self_back_kernel,
        grid=(PAIRS,),
        out_shape=[shape((rows, D), bf16), shape((2 * D, length), bf16)],
        in_specs=[
            full(rows, D), full(rows, D), full(rows, D), full(length, 2 * D),
            pl.BlockSpec((2, rows, length), lambda g: (g, 0, 0)),
        ],
        out_specs=[full(rows, D), full(2 * D, length)],
        scratch_shapes=[VMEM((D, rows), bf16), VMEM((D, rows), bf16)],
        compiler_params=params(),
        name="self_backward",
    )(self_do, self_x, self_q, self_kv, self_w)

    middle = tall(3 * D, D)
    norm_parts, own_part, g_middle = pl.pallas_call(
        joint_back_kernel,
        out_shape=[
            shape((length, D), bf16), shape((rows, D), f32), shape((parts, middle, lanes), bf16),
        ],
        in_specs=[whole()] * 5,
        out_specs=[whole()] * 3,
        compiler_params=params(),
        name="joint_backward",
    )(all_in, second_in, dq, dkvt, self_qkv)

    norm_part = lax.psum_scatter(norm_parts, "blk", scatter_dimension=0, tiled=True)

    late = 2 * tall(D, D) + tall(2 * D, ctx_width)
    tokens_grad, context_part, modes_low, g_late = pl.pallas_call(
        functools.partial(cross_back_kernel, context_count),
        out_shape=[
            shape((rows, D), f32), shape((padded, ctx_width), bf16), shape((8, D), f32),
            shape((parts, late, lanes), bf16),
        ],
        in_specs=[whole()] * 17,
        out_specs=[whole()] * 4,
        scratch_shapes=[VMEM((2 * D, padded), bf16)],
        compiler_params=params(),
        name="cross_backward",
    )(
        norm_part, own_part, grad_two, after_one, tokens, context_rows, cross_q, cross_pair, cross_w,
        cross_att, cross_inv, cross_query, cross_kv, cross_out, norm_gain, norm_bias, mod,
    )

    def reduced(g):
        part = lax.psum_scatter(g, "blk", scatter_dimension=0, tiled=True)
        return lax.psum(part, "obj")[0]

    early_sum = reduced(g_early)
    middle_sum = reduced(g_middle)
    late_sum = reduced(g_late)
    context_grad = lax.psum(context_part, "blk").astype(f32)[:context_count]

    def unslab(total, base, columns, depth):
        count = columns // parts // lanes
        pieces = [total[base + i * depth : base + (i + 1) * depth] for i in range(count)]
        return jnp.concatenate(pieces, 1).astype(f32)

    so = tall(D, D)
    self_out_grad = unslab(early_sum, 0, D, D)
    mlp_up_grad = unslab(early_sum, so, ff, D)
    mlp_down_grad = unslab(early_sum, so + tall(ff, D), D, ff)
    self_qkv_grad = unslab(middle_sum, 0, 3 * D, D)
    cross_out_grad = unslab(late_sum, 0, D, D)
    cross_query_grad = unslab(late_sum, so, D, D)
    cross_kv_grad = unslab(late_sum, 2 * so, 2 * D, ctx_width)

    small = jnp.concatenate([modes_low, modes_three], 0).reshape(3, 4, D)
    object_sums = lax.psum(small, "blk")
    everywhere = lax.all_gather(object_sums, "obj")
    lifted_all = lax.all_gather(lifted[0], "obj").astype(f32)
    mode_all = everywhere[:, :, :2].reshape(-1, 3, 2 * D)
    place = lax.axis_index("blk")
    width = 2 * D // parts
    mode_here = lax.dynamic_slice_in_dim(mode_all, place * width, width, 2)
    mod_weight_grad = jnp.einsum(
        "oc,ojm->jcm", lifted_all, mode_here, precision=lax.Precision.HIGHEST
    )
    mod_bias_grad = jnp.sum(mode_here, 0)
    norms = lax.dynamic_slice_in_dim(jnp.sum(everywhere[:, :, 2:], 0), place * each, each, 2)
    return (
        mixed[None], tokens_grad[None], context_grad[None], cross_query_grad, cross_kv_grad,
        cross_out_grad, self_qkv_grad, self_out_grad, mlp_up_grad, mlp_down_grad,
        norms[:, 0], norms[:, 1], mod_weight_grad, mod_bias_grad,
    )


def solution(mesh):
    rows = P("obj", "blk", None)
    columns = P(None, "blk")
    return jax.shard_map(
        body,
        mesh=mesh,
        in_specs=(rows, P("obj", None, None), P("obj")) + (P(),) * 12 + (rows,),
        out_specs=(rows, rows, P("obj", None, None)) + (columns,) * 9
        + (P(None, None, "blk"), columns),
        check_vma=False,
    )
```

```python
import functools
import math

import jax
import jax.numpy as jnp
from jax import lax
from jax.experimental import pallas as pl
from jax.experimental.pallas import tpu as pltpu
from jax.sharding import PartitionSpec as P

D = 512
HEADS = 8
HEAD_DIM = 64
PAIRS = HEADS // 2
WIDE = 2 * HEAD_DIM
LOG2E = 1.4426950408889634
LN2 = 0.6931471805599453
QUERY_FACTOR = LOG2E * HEAD_DIM ** (-0.5)
SCORE_FACTOR = HEAD_DIM ** (-0.5)
SAFE_SQUARE = 60.0 ** 2
EPSILON = 1e-06
GELU_A = 0.7978845608028654
GELU_B = 0.044715
MIB = 2**20

f32 = jnp.float32
bf16 = jnp.bfloat16
VMEM = pltpu.VMEM


def nn(a, b):
    return lax.dot_general(a, b, (((1,), (0,)), ((), ())), preferred_element_type=f32)


def nt(a, b):
    return lax.dot_general(a, b, (((1,), (1,)), ((), ())), preferred_element_type=f32)


def tn(a, b):
    return lax.dot_general(a, b, (((0,), (0,)), ((), ())), preferred_element_type=f32)


def whole():
    return pl.BlockSpec(memory_space=VMEM)


def params(mib=60):
    return pltpu.CompilerParams(vmem_limit_bytes=mib * MIB)


def lower_half(shape):
    return lax.broadcasted_iota(jnp.int32, shape, 1) % WIDE < HEAD_DIM


def own_half(shape, odd):
    lower = lower_half(shape)
    return jnp.logical_not(lower) if odd else lower


def normalize(x):
    center = x - jnp.mean(x, -1, keepdims=True)
    inverse = lax.rsqrt(jnp.mean(center * center, -1, keepdims=True) + EPSILON)
    return center * inverse, inverse


def modulate(x, gain, bias, shift, scale):
    normed, _ = normalize(x)
    return (normed * gain + bias) * (1.0 + scale) + shift


def modulate_back(g, x, gain, bias, scale):
    normed, inverse = normalize(x)
    affine = normed * gain + bias
    shift_grad = jnp.sum(g, 0, keepdims=True)
    scale_grad = jnp.sum(g * affine, 0, keepdims=True)
    a = g * (1.0 + scale)
    gain_grad = jnp.sum(a * normed, 0, keepdims=True)
    bias_grad = jnp.sum(a, 0, keepdims=True)
    n = a * gain
    back = inverse * (
        n - jnp.mean(n, -1, keepdims=True) - normed * jnp.mean(n * normed, -1, keepdims=True)
    )
    return back, jnp.concatenate([shift_grad, scale_grad, gain_grad, bias_grad], 0)


def norm_rows(gain_ref, bias_ref, mod_ref, j):
    gain = gain_ref[j : j + 1, :].astype(f32)
    bias = bias_ref[j : j + 1, :].astype(f32)
    shift = mod_ref[j : j + 1, :D]
    scale = mod_ref[j : j + 1, D:]
    return gain, bias, shift, scale


def head_sums(values, sign):
    rows = lax.broadcasted_iota(jnp.int32, (WIDE, WIDE), 0)
    cols = lax.broadcasted_iota(jnp.int32, (WIDE, WIDE), 1)
    block = jnp.where((rows < HEAD_DIM) != (cols < HEAD_DIM), sign, 0.0).astype(bf16)
    high = values.astype(bf16)
    low = (values - high.astype(f32)).astype(bf16)
    return nn(high, block) + nn(low, block)


def delta_lanes(product):
    parts = []
    for p in range(PAIRS):
        total = head_sums(product[:, p * WIDE : (p + 1) * WIDE], -1.0)
        high = total.astype(bf16).astype(f32)
        low = total - high
        lane = lax.broadcasted_iota(jnp.int32, total.shape, 1) % HEAD_DIM
        parts.append(jnp.where(lane == 0, high, jnp.where(lane == 1, low, 0.0)).astype(bf16))
    return jnp.concatenate(parts, 1)


def norm_top(x):
    rows = lax.broadcasted_iota(jnp.int32, (WIDE, WIDE), 0)
    cols = lax.broadcasted_iota(jnp.int32, (WIDE, WIDE), 1)
    block = jnp.where((rows < HEAD_DIM) == (cols < HEAD_DIM), 1.0, 0.0).astype(bf16)
    top = None
    for p in range(PAIRS):
        part = x[:, p * WIDE : (p + 1) * WIDE].astype(f32)
        here = jnp.max(nn((part * part).astype(bf16), block), 0, keepdims=True)
        top = here if top is None else jnp.maximum(top, here)
    return jnp.max(top)


def bounded(q, k):
    return norm_top(q) * norm_top(k) < SAFE_SQUARE


def pair_columns(head, offset=0):
    return pl.ds(pl.multiple_of(offset + head // 2 * WIDE, WIDE), WIDE)


def head_rows(head, offset=0):
    return pl.ds(pl.multiple_of(offset + head * HEAD_DIM, HEAD_DIM), HEAD_DIM)


def owned(shape, head):
    lane = lax.broadcasted_iota(jnp.int32, shape, 1)
    return lane // HEAD_DIM == head % 2


def key_rows(kv, head):
    k = kv[:, pair_columns(head)]
    return jnp.where(owned(k.shape, head), k, jnp.zeros_like(k))


def value_rows(kv, head, real_keys):
    v = kv[:, pair_columns(head, D)]
    v = jnp.where(owned(v.shape, head), v, jnp.ones_like(v))
    if real_keys < v.shape[0]:
        row = lax.broadcasted_iota(jnp.int32, v.shape, 0)
        v = jnp.where(row < real_keys, v, jnp.zeros_like(v))
    return v


def attend(head, safe, q, kv, w_ref, acc, top, real_keys):
    k = key_rows(kv, head)
    v = value_rows(kv, head, real_keys)
    count = q.shape[0]
    step = min(256, count)

    def blocks(shifted):
        for r in range(0, count, step):
            rows = slice(r, r + step)
            s = nt(q[rows, pair_columns(head)], k)
            if shifted:
                most = jnp.max(s, -1, keepdims=True)
                s = s - most
                top[rows, :] = jnp.broadcast_to(most, (step, WIDE))
            else:
                top[rows, :] = jnp.zeros((step, WIDE), f32)
            w = jnp.exp2(s).astype(bf16)
            w_ref[0, rows, :] = w
            acc[rows, :] = nn(w, v)

    @pl.when(safe)
    def _():
        blocks(False)

    @pl.when(jnp.logical_not(safe))
    def _():
        blocks(True)


def attend_back(head, do, x, do_t, q_t, kv, w_ref, dq, dkvt, real_keys, chunk):
    left = jnp.where(owned((do.shape[0], WIDE), head), do[:, pair_columns(head)], x[:, pair_columns(head)])
    k = key_rows(kv, head)
    v = value_rows(kv, head, real_keys)
    keys = k.shape[0]
    chunk = chunk if keys % chunk == 0 else keys
    total = None
    for c in range(0, keys, chunk):
        cols = slice(c, c + chunk)
        w = w_ref[0, :, cols]
        dp = nt(left, v[cols])
        ds = (w.astype(f32) * dp).astype(bf16)
        part = nn(ds, k[cols])
        total = part if total is None else total + part
        dkvt[head_rows(head), cols] = (nn(q_t[head_rows(head), :], ds) * LN2).astype(bf16)
        dkvt[head_rows(head, D), cols] = nn(do_t[head_rows(head), :], w).astype(bf16)
    total = total * SCORE_FACTOR

    @pl.when(head % 2 == 0)
    def _():
        dq[:, pair_columns(head)] = total.astype(dq.dtype)

    @pl.when(head % 2 == 1)
    def _():
        dq[:, pair_columns(head)] = (dq[:, pair_columns(head)].astype(f32) + total).astype(dq.dtype)


def put_head(ref, head, value):
    cols = pair_columns(head)
    ref[:, cols] = jnp.where(owned(value.shape, head), value, ref[:, cols])


def cross_kernel(
    context_count, tokens, context, wq, wkv, wo, gain, bias, mod,
    second_in, after_one, q_out, pair_out, w_out, att_out, inv_out, acc, top, safe_ref,
):
    h = pl.program_id(0)

    @pl.when(h == 0)
    def _():
        first_in = modulate(tokens[...].astype(f32), *norm_rows(gain, bias, mod, 0)).astype(bf16)
        q_out[...] = (nn(first_in, wq[...]) * QUERY_FACTOR).astype(bf16)
        pair_out[...] = nn(context[...], wkv[...]).astype(bf16)
        safe_ref[0] = bounded(q_out[...], pair_out[:, :D]).astype(jnp.int32)

    attend(h, safe_ref[0] == 1, q_out, pair_out, w_out, acc, top, context_count)
    inverse = 1.0 / pltpu.roll(acc[...], HEAD_DIM, 1)
    put_head(att_out, h, acc[...] * inverse)
    put_head(inv_out, h, inverse)

    @pl.when(h == HEADS - 1)
    def _():
        one = tokens[...].astype(f32) + nn(att_out[...].astype(bf16), wo[...])
        after_one[...] = one
        second_in[...] = modulate(one, *norm_rows(gain, bias, mod, 1)).astype(bf16)


def project_keys(blocks, wqkv, kv):
    for i, block in enumerate(blocks):
        rows = block.shape[0]
        kv[i * rows : (i + 1) * rows, :] = nn(block[...], wqkv[:, D:]).astype(bf16)


def near_kernel(own, sibling, wqkv, w_out, q_out, kv_out, sum_out, att_out, top_out, acc, top, safe_ref):
    h = pl.program_id(0)

    @pl.when(h == 0)
    def _():
        q_out[...] = (nn(own[...], wqkv[:, :D]) * QUERY_FACTOR).astype(bf16)
        project_keys([own, sibling], wqkv, kv_out)
        safe_ref[0] = bounded(q_out[...], kv_out[:, :D]).astype(jnp.int32)

    attend(h, safe_ref[0] == 1, q_out, kv_out, w_out, acc, top, kv_out.shape[0])
    put_head(att_out, h, acc[...])
    put_head(sum_out, h, pltpu.roll(acc[...], HEAD_DIM, 1))
    put_head(top_out, h, top[...])


def far_kernel(count, *refs):
    blocks = refs[:count]
    (wqkv, q, sum_near, att_near, top_near,
     w_out, kv_out, att_out, inv_near, inv_far, acc, top, safe_ref) = refs[count:]
    h = pl.program_id(0)

    @pl.when(h == 0)
    def _():
        project_keys(blocks, wqkv, kv_out)
        safe_ref[0] = bounded(q[...], kv_out[:, :D]).astype(jnp.int32)

    attend(h, safe_ref[0] == 1, q, kv_out, w_out, acc, top, kv_out.shape[0])
    cols = pair_columns(h)
    most = jnp.maximum(top[...], top_near[:, cols])
    near = jnp.exp2(top_near[:, cols] - most)
    far = jnp.exp2(top[...] - most)
    inverse = 1.0 / (sum_near[:, cols] * near + pltpu.roll(acc[...], HEAD_DIM, 1) * far)
    put_head(att_out, h, (att_near[:, cols] * near + acc[...] * far) * inverse)
    put_head(inv_near, h, near * inverse)
    put_head(inv_far, h, far * inverse)


def slab_rows(depth, columns, parts):
    return depth * columns // parts // WIDE


def padded_rows(rows, objects):
    unit = 16 * objects
    return -(-rows // unit) * unit


def slab_pieces(depth, each):
    lanes = math.gcd(each, WIDE)
    deep = depth * lanes // WIDE
    return [
        (i * deep, k * lanes, k * deep, i * lanes, deep, lanes)
        for i in range(each // lanes)
        for k in range(WIDE // lanes)
    ]


def slabs(out_ref, base, grad):
    parts = out_ref.shape[0]
    depth, columns = grad.shape
    each = columns // parts
    grad = grad.astype(out_ref.dtype)
    for b in range(parts):
        for to_row, to_lane, row, col, deep, lanes in slab_pieces(depth, each):
            start = b * each + col
            out_ref[b, base + to_row : base + to_row + deep, to_lane : to_lane + lanes] = grad[
                row : row + deep, start : start + lanes
            ]


def clear_tail(out_ref, used):
    if used < out_ref.shape[1]:
        rest = out_ref.shape[1] - used
        out_ref[:, used:, :] = jnp.zeros((out_ref.shape[0], rest, WIDE), out_ref.dtype)


def mlp_kernel(
    self_att, after_one, inv_near, inv_far, cotangent, wo, up, down, gain, bias, mod,
    mixed, grad_two, do_near, x_near, do_far, x_far, modes, g_out,
):
    self_low = self_att[...].astype(bf16)
    two = after_one[...] + nn(self_low, wo[...])
    rows3 = norm_rows(gain, bias, mod, 2)
    third_in = modulate(two, *rows3).astype(bf16)
    cot = cotangent[...]
    final = two
    norm_grad = jnp.zeros_like(two)
    ff = up.shape[1]
    step = 512
    up_base = slab_rows(D, D, g_out.shape[0])
    down_base = up_base + slab_rows(D, ff, g_out.shape[0])
    for f in range(0, ff, step):
        hidden = nn(third_in, up[:, f : f + step])
        square = hidden * hidden
        inner = GELU_A * hidden * (1.0 + GELU_B * square)
        t = jnp.tanh(inner)
        half = 0.5 * (1.0 + t)
        active = (hidden * half).astype(bf16)
        slope = half + 0.5 * hidden * (1.0 - t * t) * (GELU_A * (1.0 + 3.0 * GELU_B * square))
        final = final + nn(active, down[f : f + step, :])
        hidden_grad = (nt(cot, down[f : f + step, :]) * slope).astype(bf16)
        norm_grad = norm_grad + nt(hidden_grad, up[:, f : f + step])
        up_part = tn(third_in, hidden_grad)
        down_part = tn(active, cot)
        parts = g_out.shape[0]
        each = ff // parts
        for i in range(step // WIDE):
            col = f + i * WIDE
            base = up_base + col % each // WIDE * D
            g_out[col // each, base : base + D, :] = up_part[:, i * WIDE : (i + 1) * WIDE].astype(bf16)
        each = D // parts
        fold = max(1, WIDE // each)
        deep, lanes = ff // fold, min(each, WIDE)
        at = slice(f // deep * lanes, f // deep * lanes + lanes)
        down_part = down_part.astype(bf16)
        for b in range(parts):
            for i in range(max(1, each // WIDE)):
                start = b * each + i * WIDE
                base = down_base + i * ff + f % deep
                g_out[b, base : base + step, at] = down_part[:, start : start + lanes]
    clear_tail(g_out, down_base + slab_rows(ff, D, g_out.shape[0]))
    mixed[...] = final.astype(bf16)
    back, sums = modulate_back(norm_grad, two, rows3[0], rows3[1], rows3[3])
    modes[...] = sums
    grad = cot.astype(f32) + back
    grad_two[...] = grad
    self_grad = grad.astype(bf16)
    slabs(g_out, 0, tn(self_low, self_grad))
    att_grad = nt(self_grad, wo[...])
    for inv, do_out, x_out in ((inv_near, do_near, x_near), (inv_far, do_far, x_far)):
        do = (att_grad * inv[...]).astype(bf16)
        do_out[...] = do
        x_out[...] = delta_lanes(do.astype(f32) * self_att[...])


def project_back(dkvt, wqkv, part_out):
    count, rows, _ = part_out.shape
    for b in range(count):
        part = nn(wqkv[:, D:], dkvt[:, b * rows : (b + 1) * rows])
        part_out[b] = part.astype(bf16).T


class Mover:
    def __init__(self, send, recv):
        self.send, self.recv = send, recv
        self.copies = []
        place, obj = lax.axis_index("blk"), lax.axis_index("obj")
        self.chips = lax.axis_size("blk") // 2
        self.columns = lax.axis_size("obj") // 2
        self.core, self.chip = lax.rem(place, 2), place // 2
        self.side, self.column = lax.rem(obj, 2), obj // 2
        self.sibling = {"blk": self.chip * 2 + 1 - self.core}
        self.chip_ids = [lax.rem(self.chip + d, self.chips) for d in range(1, self.chips)]
        self.chip_peers = [{"blk": c * 2 + self.core} for c in self.chip_ids]
        self.across = {"obj": self.column * 2 + 1 - self.side}
        self.column_ids = [lax.rem(self.column + d, self.columns) for d in range(1, self.columns)]
        self.column_peers = [{"obj": c * 2 + self.side} for c in self.column_ids]

    def barrier(self):
        everyone = [self.sibling, self.across] + self.chip_peers + self.column_peers
        semaphore = pltpu.get_barrier_semaphore()
        for target in everyone:
            pl.semaphore_signal(semaphore, inc=1, device_id=target, device_id_type=pl.DeviceIdType.MESH)
        pl.semaphore_wait(semaphore, len(everyone))

    def copy(self, src, dst, target):
        at = len(self.copies)
        made = pltpu.make_async_remote_copy(
            src_ref=src, dst_ref=dst, send_sem=self.send.at[at], recv_sem=self.recv.at[at],
            device_id=target, device_id_type=pl.DeviceIdType.MESH,
        )
        self.copies.append(made)
        return made

    def drain(self):
        for made in self.copies:
            made.wait_send()


def begin(copies):
    for made in copies:
        made.start()


def arrive(copies):
    for made in copies:
        made.wait_recv()


def added(*values):
    total = values[0].astype(f32)
    for value in values[1:]:
        total = total + value.astype(f32)
    return total.astype(bf16)


def cut(rows, objects):
    unit = 16 * objects
    first = (rows // unit + 1) // 2 * unit
    return first, rows - first


class Gather:
    @staticmethod
    def scratch(chips, rows, objects, lanes):
        first, second = cut(rows, objects)
        return [
            VMEM((chips, rows, lanes), bf16), VMEM((chips, rows, lanes), bf16),
            VMEM((max(chips - 1, 1), first, lanes), bf16), VMEM((2, first // 2, lanes), bf16), VMEM((first // 2, lanes), bf16),
            VMEM((chips, second // 2, lanes), bf16), VMEM((chips, second // 2, lanes), bf16),
            VMEM((max(chips - 1, 1), second // 2, lanes), bf16),
        ]

    @staticmethod
    def copies(chips):
        return 2 * chips + 2 * (chips - 1) + 1 + chips

    def __init__(self, mover, g, scratch, out_first, out_second):
        self.mover, self.g = mover, g
        self.half, self.mine, self.far0, self.flat0, self.across0, self.across1, self.mine1, self.far1 = scratch
        self.out0, self.out1 = out_first, out_second
        first, half1 = self.far0.shape[1], self.mine1.shape[1]
        m, chips = mover, mover.chips
        self.rows = (slice(0, first), slice(first, first + 2 * half1))
        other = 1 - m.core
        self.core = [
            [m.copy(g.at[2 * j + other, rows], self.half.at[j, rows], m.sibling) for j in range(chips)]
            for rows in self.rows
        ]
        self.chip0 = [
            m.copy(self.mine.at[c, self.rows[0]], self.far0.at[d], peer)
            for d, (c, peer) in enumerate(zip(m.chip_ids, m.chip_peers))
        ]
        self.side0 = [m.copy(self.flat0.at[1 - m.side], self.across0, m.across)]
        away = pl.ds(pl.multiple_of(first + (1 - m.side) * half1, 16), half1)
        self.kept = pl.ds(pl.multiple_of(first + m.side * half1, 16), half1)
        self.side1 = [m.copy(self.mine.at[j, away], self.across1.at[j], m.across) for j in range(chips)]
        self.chip1 = [
            m.copy(self.mine1.at[c], self.far1.at[d], peer)
            for d, (c, peer) in enumerate(zip(m.chip_ids, m.chip_peers))
        ]

    def step0(self):
        begin(self.core[0] + self.core[1])

    def step1(self):
        for group, after in ((0, self.chip0), (1, self.side1)):
            arrive(self.core[group])
            rows = self.rows[group]
            for j in range(self.mover.chips):
                self.mine[j, rows] = added(self.g[2 * j + self.mover.core, rows], self.half[j, rows])
            begin(after)

    def step2(self):
        m = self.mover
        arrive(self.chip0)
        total = added(self.mine[m.chip, self.rows[0]], *[self.far0[d] for d in range(m.chips - 1)])
        self.flat0[...] = total.reshape(self.flat0.shape)
        begin(self.side0)
        arrive(self.side1)
        for j in range(m.chips):
            self.mine1[j] = added(self.mine[j, self.kept], self.across1[j])
        begin(self.chip1)

    def step3(self):
        m = self.mover
        arrive(self.side0)
        self.out0[...] = added(self.flat0[m.side], self.across0[...])
        arrive(self.chip1)
        self.out1[...] = added(self.mine1[m.chip], *[self.far1[d] for d in range(m.chips - 1)])


class Spread:
    @staticmethod
    def scratch(objects, half, lanes):
        columns = objects // 2
        return VMEM((max(columns - 1, 1), half // columns, lanes), bf16)

    @staticmethod
    def copies(objects):
        return 2 * (objects // 2 - 1) + 1

    def __init__(self, mover, half, taken, out):
        m = mover
        self.mover, self.half, self.taken, self.out = mover, half, taken, out
        piece = taken.shape[1]
        self.piece = pl.ds(pl.multiple_of(m.column * piece, 16), piece)
        self.sums = [
            m.copy(half.at[pl.ds(pl.multiple_of(c * piece, 16), piece)], taken.at[d], peer)
            for d, (c, peer) in enumerate(zip(m.column_ids, m.column_peers))
        ]
        own = out.at[m.side, m.column]
        self.shares = [m.copy(own, own, peer) for peer in m.column_peers]
        self.sides = [m.copy(out.at[m.side], out.at[m.side], m.across)]

    def step0(self):
        begin(self.sums)

    def step1(self):
        arrive(self.sums)
        m = self.mover
        self.out[m.side, m.column] = added(
            self.half[self.piece], *[self.taken[d] for d in range(m.columns - 1)]
        )
        begin(self.shares)

    def step2(self):
        arrive(self.shares)
        begin(self.sides)

    def step3(self):
        arrive(self.sides)


def far_back_kernel(do, x, q, kv, w, wqkv, g, dq_out, dkvt, part_out, half0, half1, do_t, q_t, *scratch):
    h = pl.program_id(0)
    mover = Mover(*scratch[-2:])
    gather = Gather(mover, g, scratch[:-2], half0, half1)

    @pl.when(h == 0)
    def _():
        mover.barrier()
        gather.step0()
        do_t[...] = do[...].T
        q_t[...] = q[...].T

    @pl.when(h == 1)
    def _():
        gather.step1()

    @pl.when(h == 5)
    def _():
        gather.step2()

    attend_back(h, do, x, do_t, q_t, kv, w, dq_out, dkvt, kv.shape[0], 512)

    @pl.when(h == HEADS - 1)
    def _():
        project_back(dkvt, wqkv, part_out)
        gather.step3()
        mover.drain()


def near_back_kernel(count, do, x, q, kv, w, wqkv, dq_far, dkvt_far, far_parts, half0, half1, own, sibling, *refs):
    blocks = refs[:count]
    (norm_grad, g_out, out0, out1, dq, dkvt, do_t, q_t, parts, from_sibling, chip_sums, from_chips, near_sibling,
     taken0, taken1, sums0, sums1, send, recv) = refs[count:]
    h = pl.program_id(0)
    m = Mover(send, recv)
    spreads = [Spread(m, half0, taken0, sums0), Spread(m, half1, taken1, sums1)]
    chips = m.chips
    far_core = [m.copy(far_parts.at[2 * d + 1], from_sibling.at[d], m.sibling) for d in range(chips - 1)]
    back = [{"blk": lax.rem(m.chip + chips - d, chips) * 2 + m.core} for d in range(1, chips)]
    far_chip = [m.copy(chip_sums.at[d], from_chips.at[d], back[d]) for d in range(chips - 1)]
    near_core = [m.copy(parts.at[1], near_sibling, m.sibling)]

    @pl.when(h == 0)
    def _():
        m.barrier()
        begin(far_core)
        for spread in spreads:
            spread.step0()
        do_t[...] = do[...].T
        q_t[...] = q[...].T

    @pl.when(h == 1)
    def _():
        arrive(far_core)
        for d in range(chips - 1):
            chip_sums[d] = added(far_parts[2 * d], from_sibling[d])
        begin(far_chip)

    @pl.when(h == 3)
    def _():
        for spread in spreads:
            spread.step1()

    @pl.when(h == 5)
    def _():
        spreads[0].step2()

    @pl.when(h == 6)
    def _():
        spreads[1].step2()

    attend_back(h, do, x, do_t, q_t, kv, w, dq, dkvt, kv.shape[0], 512)

    @pl.when(h == HEADS - 1)
    def _():
        project_back(dkvt, wqkv, parts)
        begin(near_core)
        dq_low = (dq[...] + dq_far[...]).astype(bf16)
        rows = own.shape[0]
        grad = nn(dkvt[:, :rows], own[...]) + nn(dkvt[:, rows:], sibling[...])
        for i, block in enumerate(blocks):
            grad = grad + nn(dkvt_far[:, i * rows : (i + 1) * rows], block[...])
        slabs(g_out, 0, jnp.concatenate([tn(own[...], dq_low), grad.T], 1))
        total = nt(dq_low, wqkv[:, :D]) + parts[0].astype(f32)
        arrive(far_chip)
        for d in range(chips - 1):
            total = total + from_chips[d].astype(f32)
        arrive(near_core)
        norm_grad[...] = total + near_sibling[...].astype(f32)
        for spread, out in zip(spreads, (out0, out1)):
            spread.step3()
            out[...] = spread.out[...]
        m.drain()


def cross_back_kernel(
    context_count, norm_grad, grad_two, after_one, tokens, context, q, pair, w, att, inv,
    wq, wkv, wo, gain, bias, mod, g_middle, modes_three, lifted,
    tokens_grad, ctx_result, small_result, mid0, mid1, late0, late1,
    dkvt, do, x, do_t, q_t, dq, g_mid, g_late, small, ctx,
    ctx_half, ctx_mine, ctx_far, small_half, small_mine, small_far, *rest
):
    h = pl.program_id(0)
    mid_scratch, late_scratch = rest[0:8], rest[8:16]
    mid_half0, mid_half1, late_half0, late_half1 = rest[16:20]
    mid_taken0, mid_taken1, late_taken0, late_taken1 = rest[20:24]
    mid_sums0, mid_sums1, late_sums0, late_sums1, ctx_out, small_out = rest[24:30]
    m = Mover(*rest[30:32])
    chips = m.chips
    mid = Gather(m, g_mid, mid_scratch, mid_half0, mid_half1)
    mid_spread = [Spread(m, mid_half0, mid_taken0, mid_sums0), Spread(m, mid_half1, mid_taken1, mid_sums1)]
    late = Gather(m, g_late, late_scratch, late_half0, late_half1)
    late_spread = [Spread(m, late_half0, late_taken0, late_sums0), Spread(m, late_half1, late_taken1, late_sums1)]
    ctx_rows = ctx.shape[0] // 2
    ctx_own = pl.ds(pl.multiple_of(m.core * ctx_rows, 16), ctx_rows)
    ctx_other = pl.ds(pl.multiple_of((1 - m.core) * ctx_rows, 16), ctx_rows)
    ctx_core = [m.copy(ctx.at[ctx_other], ctx_half, m.sibling)]
    ctx_chip = [m.copy(ctx_mine, ctx_far.at[d], m.chip_peers[d]) for d in range(chips - 1)]
    ctx_back = [m.copy(ctx_out.at[ctx_own], ctx_out.at[ctx_own], m.sibling)]
    small_core = [m.copy(small, small_half, m.sibling)]
    small_chip = [m.copy(small_mine, small_far.at[d], m.chip_peers[d]) for d in range(chips - 1)]
    own_small = small_out.at[m.column, m.side]
    small_side = [m.copy(own_small, own_small, m.across)]
    small_column = [m.copy(small_out.at[m.column], small_out.at[m.column], peer) for peer in m.column_peers]
    middle_rows = g_middle.shape[1]
    late_base = slab_rows(D, D, g_late.shape[0])

    @pl.when(h == 0)
    def _():
        m.barrier()
        g_mid[:, :middle_rows, :] = g_middle[...]
        rows = norm_rows(gain, bias, mod, 1)
        back, sums = modulate_back(norm_grad[...], after_one[...], rows[0], rows[1], rows[3])
        grad_one = grad_two[...] + back
        tokens_grad[...] = grad_one
        small[4:8, :] = sums
        small[8:12, :] = modes_three[...]
        small[12:14, :] = lifted[...]
        small[14:16, :] = jnp.zeros((2, D), f32)
        cross_grad = grad_one.astype(bf16)
        slabs(g_mid, middle_rows, tn(att[...].astype(bf16), cross_grad))
        clear_tail(g_mid, middle_rows + slab_rows(D, D, g_mid.shape[0]))
        mid.step0()
        do[...] = (nt(cross_grad, wo[...]) * inv[...]).astype(bf16)
        x[...] = delta_lanes(do[...].astype(f32) * att[...])
        do_t[...] = do[...].T
        q_t[...] = q[...].T

    @pl.when(h == 1)
    def _():
        mid.step1()

    @pl.when(h == 4)
    def _():
        mid.step2()

    @pl.when(h == 6)
    def _():
        mid.step3()
        for spread in mid_spread:
            spread.step0()

    attend_back(h, do, x, do_t, q_t, pair, w, dq, dkvt, context_count, pair.shape[0])

    @pl.when(h == HEADS - 1)
    def _():
        dq_low = dq[...].astype(bf16)
        first = tokens[...].astype(f32)
        rows = norm_rows(gain, bias, mod, 0)
        first_in = modulate(first, *rows).astype(bf16)
        slabs(g_late, 0, tn(first_in, dq_low))
        real = lax.broadcasted_iota(jnp.int32, dkvt.shape, 1) < context_count
        kept = jnp.where(real, dkvt[...], jnp.zeros_like(dkvt))
        slabs(g_late, late_base, nn(kept, context[...]).T)
        clear_tail(g_late, late_base + slab_rows(context.shape[1], 2 * D, g_late.shape[0]))
        late.step0()
        ctx[...] = tn(dkvt[...], wkv[...].T).astype(bf16)
        begin(ctx_core)
        for spread in mid_spread:
            spread.step1()
        back, sums = modulate_back(nt(dq_low, wq[...]), first, rows[0], rows[1], rows[3])
        small[0:4, :] = sums
        begin(small_core)
        late.step1()
        arrive(ctx_core)
        ctx_mine[...] = added(ctx[ctx_own], ctx_half[...])
        begin(ctx_chip)
        arrive(small_core)
        small_mine[...] = small[...] + small_half[...]
        begin(small_chip)
        tokens_grad[...] = tokens_grad[...] + back
        for spread in mid_spread:
            spread.step2()
        late.step2()
        arrive(small_chip)
        total = small_mine[...]
        for d in range(chips - 1):
            total = total + small_far[d]
        small_out[m.column, m.side] = total
        begin(small_side)
        late.step3()
        for spread in late_spread:
            spread.step0()
        arrive(ctx_chip)
        ctx_out[ctx_own] = added(ctx_mine[...], *[ctx_far[d] for d in range(chips - 1)])
        begin(ctx_back)
        arrive(small_side)
        begin(small_column)
        for spread in late_spread:
            spread.step1()
        for spread in late_spread:
            spread.step2()
        for spread, out in zip(mid_spread, (mid0, mid1)):
            spread.step3()
            out[...] = spread.out[...]
        arrive(ctx_back)
        ctx_result[...] = ctx_out[...]
        arrive(small_column)
        small_result[...] = small_out[...]
        for spread, out in zip(late_spread, (late0, late1)):
            spread.step3()
            out[...] = spread.out[...]
        m.drain()


def finish_kernel(parts, early0, early1, mid0, mid1, late0, late1, small, so, up, down, qkv, co, cq, ckv, gains, biases, modw, modb, mode):
    place = lax.axis_index("blk")
    objects = small.shape[0]
    width = 2 * D // parts
    each = D // parts

    def put(out, total, base):
        depth, columns = out.shape
        for to_row, to_lane, row, col, deep, lanes in slab_pieces(depth, columns):
            out[row : row + deep, col : col + lanes] = total[
                base + to_row : base + to_row + deep, to_lane : to_lane + lanes
            ].astype(f32)
        return base + slab_rows(depth, columns, 1)

    early = jnp.concatenate([early0[...], early1[...]], 0)
    base = put(so, early, 0)
    base = put(up, early, base)
    put(down, early, base)
    middle = jnp.concatenate([mid0[...], mid1[...]], 0)
    base = put(qkv, middle, 0)
    put(co, middle, base)
    late = jnp.concatenate([late0[...], late1[...]], 0)
    base = put(cq, late, 0)
    put(ckv, late, base)
    lifted = jnp.concatenate([small[:, 12, :], small[:, 13, :]], 1)
    summed = jnp.sum(small[...], 0)
    for b in range(parts):
        @pl.when(place == b)
        def _():
            row, col = b * width // D, b * width % D
            for j in range(3):
                mode[j] = small[:, 4 * j + row, col : col + width]
                gains[j : j + 1, :] = summed[4 * j + 2 : 4 * j + 3, b * each : (b + 1) * each]
                biases[j : j + 1, :] = summed[4 * j + 3 : 4 * j + 4, b * each : (b + 1) * each]
    for j in range(3):
        modw[j] = lax.dot_general(
            lifted, mode[j], (((0,), (0,)), ((), ())), precision=lax.Precision.HIGHEST, preferred_element_type=f32
        )
        modb[j : j + 1, :] = jnp.sum(mode[j], 0, keepdims=True)


def shape(dims, dtype):
    return jax.ShapeDtypeStruct(tuple(dims), dtype)


def body(
    tokens, context, camera_groups, camera_table, cross_query, cross_kv, cross_out, self_qkv,
    self_out, mlp_up, mlp_down, norm_gain, norm_bias, mod_weight, mod_bias, cotangent,
):
    parts = lax.axis_size("blk")
    tokens = tokens[0]
    cotangent = cotangent[0]
    context_count = context.shape[1]
    rows = tokens.shape[0]
    length = rows * parts
    ff = mlp_up.shape[1]
    cam_width = mod_weight.shape[1]
    ctx_width = context.shape[2]
    padded = -(-context_count // 128) * 128
    context_rows = jnp.pad(context[0], ((0, padded - context_count), (0, 0)), mode="edge")

    picked = (
        camera_groups[:, None] == jnp.arange(camera_table.shape[0], dtype=jnp.int32)[None, :]
    ).astype(bf16)
    camera = jnp.dot(picked, camera_table, preferred_element_type=f32)
    lifted = jax.nn.silu(camera).astype(bf16)
    mod = (
        jnp.einsum("oc,jcm->ojm", lifted, mod_weight, preferred_element_type=f32)
        + mod_bias.astype(f32)
    )[0]

    def near_hop(block):
        return lax.ppermute(block, "blk", [(i, i ^ 1) for i in range(parts)])

    def chip_hop(block, distance):
        route = [(i, (i // 2 + distance) % chips * 2 + i % 2) for i in range(parts)]
        return lax.ppermute(block, "blk", route)

    chips = parts // 2
    objects = lax.axis_size("obj")
    full = lambda *dims: pl.BlockSpec(dims, lambda h: (0,) * len(dims))
    head = lambda keys: pl.BlockSpec((1, rows, keys), lambda h: (h, 0, 0))
    row_full = full(rows, D)
    row_f32, row_bf16 = shape((rows, D), f32), shape((rows, D), bf16)
    per_head = [VMEM((rows, WIDE), f32), VMEM((rows, WIDE), f32), pltpu.SMEM((1,), jnp.int32)]
    transposed = [VMEM((D, rows), bf16), VMEM((D, rows), bf16)]
    norm_full = [full(3, D), full(3, D), full(3, 2 * D)]

    def call(kernel, name, us, outs, ins, out_specs, scratch=(), collective_id=None, **more):
        return pl.pallas_call(
            kernel, name=name, out_shape=outs, in_specs=ins, out_specs=out_specs, scratch_shapes=list(scratch),
            cost_estimate=pl.CostEstimate(flops=int(us * 1.1e9), bytes_accessed=int(us * 3.6e6), transcendentals=0),
            compiler_params=params() if collective_id is None else pltpu.CompilerParams(
                vmem_limit_bytes=60 * MIB, collective_id=collective_id, has_side_effects=True
            ), **more,
        )

    second_in, after_one, cross_q, cross_pair, cross_w, cross_att, cross_inv = call(
        functools.partial(cross_kernel, context_count), "cross_forward", 15,
        [row_bf16, row_f32, row_bf16, shape((padded, 2 * D), bf16), shape((HEADS, rows, padded), bf16), row_f32, row_f32],
        [row_full, full(padded, ctx_width), full(D, D), full(ctx_width, 2 * D), full(D, D)] + norm_full,
        [row_full, row_full, row_full, full(padded, 2 * D), head(padded), row_full, row_full],
        per_head, grid=(HEADS,),
    )(tokens, context_rows, cross_query, cross_kv, cross_out, norm_gain, norm_bias, mod)

    sibling_in = near_hop(second_in)
    to_chips, sibling_in = lax.optimization_barrier((second_in, sibling_in))
    chip_in = [chip_hop(to_chips, d) for d in range(1, chips)]
    near_keys, far_keys = 2 * rows, 2 * rows * (chips - 1)
    near_w, self_q, near_kv, near_sum, near_att, near_top = call(
        near_kernel, "near_forward", 16,
        [shape((HEADS, rows, near_keys), bf16), row_bf16, shape((near_keys, 2 * D), bf16), row_f32, row_f32, row_f32],
        [row_full, row_full, full(D, 3 * D)],
        [head(near_keys), row_full, full(near_keys, 2 * D), row_full, row_full, row_full],
        per_head, grid=(HEADS,),
    )(second_in, sibling_in, self_qkv)
    chip_in, near_kv = lax.optimization_barrier((chip_in, near_kv))
    far_in = []
    for block in chip_in:
        far_in += [block, near_hop(block)]
    count = len(far_in)
    far_w, far_kv, self_att, near_inv, far_inv = call(
        functools.partial(far_kernel, count), "far_forward", 16,
        [shape((HEADS, rows, far_keys), bf16), shape((far_keys, 2 * D), bf16), row_f32, row_f32, row_f32],
        [row_full] * count + [full(D, 3 * D)] + [row_full] * 4,
        [head(far_keys), full(far_keys, 2 * D), row_full, row_full, row_full],
        per_head, grid=(HEADS,),
    )(*far_in, self_qkv, self_q, near_sum, near_att, near_top)

    lanes = WIDE
    tall = lambda columns, depth: slab_rows(depth, columns, parts)
    early = padded_rows(tall(D, D) + tall(ff, D) + tall(D, ff), objects)
    mixed, grad_two, near_do, near_x, far_do, far_x, modes_three, g_early = call(
        mlp_kernel, "feed_forward", 20,
        [row_bf16, row_f32, row_bf16, row_bf16, row_bf16, row_bf16, shape((4, D), f32), shape((parts, early, lanes), bf16)],
        [whole()] * 11, [whole()] * 8,
    )(self_att, after_one, near_inv, far_inv, cotangent, self_out, mlp_up, mlp_down, norm_gain, norm_bias, mod)

    unit = objects // 2
    moving = lambda copies: [pltpu.SemaphoreType.DMA((copies,)), pltpu.SemaphoreType.DMA((copies,))]
    halves = lambda rows: [shape((n // 2, lanes), bf16) for n in cut(rows, objects)]
    half_vmem = lambda rows: [VMEM((n // 2, lanes), bf16) for n in cut(rows, objects)]
    spread_outs = lambda rows: [shape((2, unit, n // objects, lanes), bf16) for n in cut(rows, objects)]
    taken = lambda rows: [Spread.scratch(objects, n // 2, lanes) for n in cut(rows, objects)]
    in_vmem = lambda shapes: [VMEM(item.shape, item.dtype) for item in shapes]
    once = lambda *dims: pl.BlockSpec(dims, lambda h: (0,) * len(dims), pipeline_mode=pl.Buffered(1))
    like = lambda shapes: [once(*item.shape) for item in shapes]
    row_once = once(rows, D)

    half_shapes = halves(early)
    far_dq, far_dkvt, far_parts, half0, half1 = call(
        far_back_kernel, "far_backward", 25,
        [row_f32, shape((2 * D, far_keys), bf16), shape((count, rows, D), bf16)] + half_shapes,
        [row_once, row_once, row_once, once(far_keys, 2 * D), head(far_keys), once(D, 3 * D), once(parts, early, lanes)],
        [row_once, once(2 * D, far_keys), once(count, rows, D)] + like(half_shapes),
        transposed + Gather.scratch(chips, early, objects, lanes) + moving(Gather.copies(chips)), grid=(HEADS,),
        collective_id=0,
    )(far_do, far_x, self_q, far_kv, far_w, self_qkv, g_early)

    middle = tall(3 * D, D)
    spread_shapes = spread_outs(early)
    hops = VMEM((chips - 1, rows, D), bf16)
    norm_grad, g_middle, early0, early1 = call(
        functools.partial(near_back_kernel, count), "near_backward", 30,
        [row_f32, shape((parts, middle, lanes), bf16)] + spread_shapes,
        [row_once, row_once, row_once, once(near_keys, 2 * D), head(near_keys), once(D, 3 * D),
         row_once, once(2 * D, far_keys), once(count, rows, D)] + like(half_shapes) + [row_once] * (2 + count),
        [row_once, once(parts, middle, lanes)] + like(spread_shapes),
        [VMEM((rows, D), f32), VMEM((2 * D, near_keys), bf16)] + transposed
        + [VMEM((2, rows, D), bf16), hops, hops, hops, VMEM((rows, D), bf16)] + taken(early) + in_vmem(spread_shapes)
        + moving(2 * (chips - 1) + 1 + 2 * Spread.copies(objects)),
        grid=(HEADS,), collective_id=1,
    )(near_do, near_x, self_q, near_kv, near_w, self_qkv, far_dq, far_dkvt, far_parts, half0, half1,
      second_in, sibling_in, *far_in)

    late = padded_rows(tall(D, D) + tall(2 * D, ctx_width), objects)
    mid = padded_rows(middle + tall(D, D), objects)
    lifted_rows = lifted.astype(f32).reshape(2, D) * (1.0 / parts)
    mid_shapes, late_shapes = spread_outs(mid), spread_outs(late)
    ctx_half = VMEM((padded // 2, ctx_width), bf16)
    small_vmem = VMEM((16, D), f32)
    tokens_grad, context_sum, small_all, mid0, mid1, late0, late1 = call(
        functools.partial(cross_back_kernel, context_count), "cross_backward", 20,
        [row_f32, shape((padded, ctx_width), bf16), shape((unit, 2, 16, D), f32)] + mid_shapes + late_shapes,
        [row_once] * 4 + [once(padded, ctx_width), row_once, once(padded, 2 * D), head(padded), row_once, row_once,
         once(D, D), once(ctx_width, 2 * D), once(D, D)] + norm_full + [once(parts, middle, lanes), full(4, D), full(2, D)],
        [row_once, once(padded, ctx_width), once(unit, 2, 16, D)] + like(mid_shapes) + like(late_shapes),
        [VMEM((2 * D, padded), bf16), VMEM((rows, D), bf16), VMEM((rows, D), bf16)] + transposed + [VMEM((rows, D), f32)]
        + [VMEM((parts, mid, lanes), bf16), VMEM((parts, late, lanes), bf16), small_vmem, VMEM((padded, ctx_width), bf16)]
        + [ctx_half, ctx_half, VMEM((chips - 1, padded // 2, ctx_width), bf16)]
        + [small_vmem, small_vmem, VMEM((chips - 1, 16, D), f32)]
        + Gather.scratch(chips, mid, objects, lanes) + Gather.scratch(chips, late, objects, lanes)
        + half_vmem(mid) + half_vmem(late) + taken(mid) + taken(late) + in_vmem(mid_shapes) + in_vmem(late_shapes)
        + [VMEM((padded, ctx_width), bf16), VMEM((unit, 2, 16, D), f32)]
        + moving(2 * Gather.copies(chips) + 4 * Spread.copies(objects) + 2 + chips - 1 + 2 + chips - 1 + unit - 1),
        grid=(HEADS,), collective_id=2,
    )(
        norm_grad, grad_two, after_one, tokens, context_rows, cross_q, cross_pair, cross_w,
        cross_att, cross_inv, cross_query, cross_kv, cross_out, norm_gain, norm_bias, mod, g_middle, modes_three,
        lifted_rows,
    )
    context_grad = context_sum[:context_count].astype(f32)

    width = 2 * D // parts
    grads = lambda depth, columns: shape((depth, columns // parts), f32)
    so, up, down, qkv, co, cq, ckv, gains, biases, modw, modb = pl.pallas_call(
        functools.partial(finish_kernel, parts),
        name="finish",
        out_shape=[
            grads(D, D), grads(D, ff), grads(ff, D), grads(D, 3 * D), grads(D, D), grads(D, D), grads(ctx_width, 2 * D),
            grads(3, D), grads(3, D), shape((3, cam_width, width), f32), grads(3, 2 * D),
        ],
        in_specs=[whole()] * 7,
        out_specs=[whole()] * 11,
        scratch_shapes=[VMEM((3, objects, width), f32)],
        compiler_params=params(),
    )(*[v.reshape(-1, lanes) for v in (early0, early1, mid0, mid1, late0, late1)], small_all.reshape(objects, 16, D))
    return (
        mixed[None], tokens_grad[None], context_grad[None], cq, ckv, co, qkv, so, up, down, gains, biases, modw, modb,
    )


def solution(mesh):
    rows = P("obj", "blk", None)
    columns = P(None, "blk")
    return jax.shard_map(
        body,
        mesh=mesh,
        in_specs=(rows, P("obj", None, None), P("obj")) + (P(),) * 12 + (rows,),
        out_specs=(rows, rows, P("obj", None, None)) + (columns,) * 9
        + (P(None, None, "blk"), columns),
        check_vma=False,
    )
```

```python
import functools
import math

import jax
import jax.numpy as jnp
from jax import lax
from jax.experimental import pallas as pl
from jax.experimental.pallas import tpu as pltpu
from jax.sharding import PartitionSpec as P

D = 512
HEADS = 8
HEAD_DIM = 64
PAIRS = HEADS // 2
WIDE = 2 * HEAD_DIM
LOG2E = 1.4426950408889634
LN2 = 0.6931471805599453
QUERY_FACTOR = LOG2E * HEAD_DIM ** (-0.5)
SCORE_FACTOR = HEAD_DIM ** (-0.5)
SAFE_SQUARE = 60.0 ** 2
EPSILON = 1e-06
GELU_A = 0.7978845608028654
GELU_B = 0.044715
MIB = 2**20

f32 = jnp.float32
bf16 = jnp.bfloat16
VMEM = pltpu.VMEM


def nn(a, b):
    return lax.dot_general(a, b, (((1,), (0,)), ((), ())), preferred_element_type=f32)


def nt(a, b):
    return lax.dot_general(a, b, (((1,), (1,)), ((), ())), preferred_element_type=f32)


def tn(a, b):
    return lax.dot_general(a, b, (((0,), (0,)), ((), ())), preferred_element_type=f32)


def whole():
    return pl.BlockSpec(memory_space=VMEM)


def params(mib=60):
    return pltpu.CompilerParams(vmem_limit_bytes=mib * MIB)


def lower_half(shape):
    return lax.broadcasted_iota(jnp.int32, shape, 1) % WIDE < HEAD_DIM


def own_half(shape, odd):
    lower = lower_half(shape)
    return jnp.logical_not(lower) if odd else lower


def normalize(x):
    center = x - jnp.mean(x, -1, keepdims=True)
    inverse = lax.rsqrt(jnp.mean(center * center, -1, keepdims=True) + EPSILON)
    return center * inverse, inverse


def modulate(x, gain, bias, shift, scale):
    normed, _ = normalize(x)
    return (normed * gain + bias) * (1.0 + scale) + shift


def modulate_back(g, x, gain, bias, scale):
    normed, inverse = normalize(x)
    affine = normed * gain + bias
    shift_grad = jnp.sum(g, 0, keepdims=True)
    scale_grad = jnp.sum(g * affine, 0, keepdims=True)
    a = g * (1.0 + scale)
    gain_grad = jnp.sum(a * normed, 0, keepdims=True)
    bias_grad = jnp.sum(a, 0, keepdims=True)
    n = a * gain
    back = inverse * (
        n - jnp.mean(n, -1, keepdims=True) - normed * jnp.mean(n * normed, -1, keepdims=True)
    )
    return back, jnp.concatenate([shift_grad, scale_grad, gain_grad, bias_grad], 0)


def norm_rows(gain_ref, bias_ref, mod_ref, j):
    gain = gain_ref[j : j + 1, :].astype(f32)
    bias = bias_ref[j : j + 1, :].astype(f32)
    shift = mod_ref[j : j + 1, :D]
    scale = mod_ref[j : j + 1, D:]
    return gain, bias, shift, scale


def head_sums(values, sign):
    rows = lax.broadcasted_iota(jnp.int32, (WIDE, WIDE), 0)
    cols = lax.broadcasted_iota(jnp.int32, (WIDE, WIDE), 1)
    block = jnp.where((rows < HEAD_DIM) != (cols < HEAD_DIM), sign, 0.0).astype(bf16)
    high = values.astype(bf16)
    low = (values - high.astype(f32)).astype(bf16)
    return nn(high, block) + nn(low, block)


def delta_lanes(product):
    parts = []
    for p in range(PAIRS):
        total = head_sums(product[:, p * WIDE : (p + 1) * WIDE], -1.0)
        high = total.astype(bf16).astype(f32)
        low = total - high
        lane = lax.broadcasted_iota(jnp.int32, total.shape, 1) % HEAD_DIM
        parts.append(jnp.where(lane == 0, high, jnp.where(lane == 1, low, 0.0)).astype(bf16))
    return jnp.concatenate(parts, 1)


def norm_top(x):
    rows = lax.broadcasted_iota(jnp.int32, (WIDE, WIDE), 0)
    cols = lax.broadcasted_iota(jnp.int32, (WIDE, WIDE), 1)
    block = jnp.where((rows < HEAD_DIM) == (cols < HEAD_DIM), 1.0, 0.0).astype(bf16)
    top = None
    for p in range(PAIRS):
        part = x[:, p * WIDE : (p + 1) * WIDE].astype(f32)
        here = jnp.max(nn((part * part).astype(bf16), block), 0, keepdims=True)
        top = here if top is None else jnp.maximum(top, here)
    return jnp.max(top)


def bounded(q, k):
    return norm_top(q) * norm_top(k) < SAFE_SQUARE


def pair_columns(head, offset=0):
    return pl.ds(pl.multiple_of(offset + head // 2 * WIDE, WIDE), WIDE)


def head_rows(head, offset=0):
    return pl.ds(pl.multiple_of(offset + head * HEAD_DIM, HEAD_DIM), HEAD_DIM)


def owned(shape, head):
    lane = lax.broadcasted_iota(jnp.int32, shape, 1)
    return lane // HEAD_DIM == head % 2


def key_rows(kv, head):
    k = kv[:, pair_columns(head)]
    return jnp.where(owned(k.shape, head), k, jnp.zeros_like(k))


def value_rows(kv, head, real_keys):
    v = kv[:, pair_columns(head, D)]
    v = jnp.where(owned(v.shape, head), v, jnp.ones_like(v))
    if real_keys < v.shape[0]:
        row = lax.broadcasted_iota(jnp.int32, v.shape, 0)
        v = jnp.where(row < real_keys, v, jnp.zeros_like(v))
    return v


def attend(head, safe, q, kv, w_ref, acc, top, real_keys):
    k = key_rows(kv, head)
    v = value_rows(kv, head, real_keys)
    count = q.shape[0]
    step = min(256, count)

    def blocks(shifted):
        for r in range(0, count, step):
            rows = slice(r, r + step)
            s = nt(q[rows, pair_columns(head)], k)
            if shifted:
                most = jnp.max(s, -1, keepdims=True)
                s = s - most
                top[rows, :] = jnp.broadcast_to(most, (step, WIDE))
            else:
                top[rows, :] = jnp.zeros((step, WIDE), f32)
            w = jnp.exp2(s).astype(bf16)
            w_ref[0, rows, :] = w
            acc[rows, :] = nn(w, v)

    @pl.when(safe)
    def _():
        blocks(False)

    @pl.when(jnp.logical_not(safe))
    def _():
        blocks(True)


def attend_back(head, do, x, do_t, q_t, kv, w_ref, dq, dkvt, real_keys, chunk):
    left = jnp.where(owned((do.shape[0], WIDE), head), do[:, pair_columns(head)], x[:, pair_columns(head)])
    k = key_rows(kv, head)
    v = value_rows(kv, head, real_keys)
    keys = k.shape[0]
    chunk = chunk if keys % chunk == 0 else keys
    total = None
    for c in range(0, keys, chunk):
        cols = slice(c, c + chunk)
        w = w_ref[0, :, cols]
        dp = nt(left, v[cols])
        ds = (w.astype(f32) * dp).astype(bf16)
        part = nn(ds, k[cols])
        total = part if total is None else total + part
        dkvt[head_rows(head), cols] = (nn(q_t[head_rows(head), :], ds) * LN2).astype(bf16)
        dkvt[head_rows(head, D), cols] = nn(do_t[head_rows(head), :], w).astype(bf16)
    total = total * SCORE_FACTOR

    dq[:, pair_columns(head)] += total


def put_head(ref, head, value):
    cols = pair_columns(head)
    ref[:, cols] = jnp.where(owned(value.shape, head), value, ref[:, cols])


def cross_kernel(
    context_count, tokens, context, wq, wkv, wo, gain, bias, mod,
    second_in, after_one, q_out, pair_out, w_out, att_out, inv_out, acc, top, safe_ref,
):
    h = pl.program_id(0)

    @pl.when(h == 0)
    def _():
        first_in = modulate(tokens[...].astype(f32), *norm_rows(gain, bias, mod, 0)).astype(bf16)
        q_out[...] = (nn(first_in, wq[...]) * QUERY_FACTOR).astype(bf16)
        pair_out[...] = nn(context[...], wkv[...]).astype(bf16)
        safe_ref[0] = bounded(q_out[...], pair_out[:, :D]).astype(jnp.int32)

    attend(h, safe_ref[0] == 1, q_out, pair_out, w_out, acc, top, context_count)
    inverse = 1.0 / pltpu.roll(acc[...], HEAD_DIM, 1)
    put_head(att_out, h, acc[...] * inverse)
    put_head(inv_out, h, inverse)

    @pl.when(h == HEADS - 1)
    def _():
        one = tokens[...].astype(f32) + nn(att_out[...].astype(bf16), wo[...])
        after_one[...] = one
        second_in[...] = modulate(one, *norm_rows(gain, bias, mod, 1)).astype(bf16)


def project_keys(blocks, wqkv, kv):
    for i, block in enumerate(blocks):
        rows = block.shape[0]
        kv[i * rows : (i + 1) * rows, :] = nn(block[...], wqkv[:, D:]).astype(bf16)


def near_kernel(own, sibling, wqkv, w_out, q_out, kv_out, sum_out, att_out, top_out, acc, top, safe_ref):
    h = pl.program_id(0)

    @pl.when(h == 0)
    def _():
        q_out[...] = (nn(own[...], wqkv[:, :D]) * QUERY_FACTOR).astype(bf16)
        project_keys([own, sibling], wqkv, kv_out)
        safe_ref[0] = bounded(q_out[...], kv_out[:, :D]).astype(jnp.int32)

    attend(h, safe_ref[0] == 1, q_out, kv_out, w_out, acc, top, kv_out.shape[0])
    put_head(att_out, h, acc[...])
    put_head(sum_out, h, pltpu.roll(acc[...], HEAD_DIM, 1))
    put_head(top_out, h, top[...])


def far_kernel(count, *refs):
    blocks = refs[:count]
    (wqkv, q, sum_near, att_near, top_near,
     w_out, kv_out, att_out, inv_near, inv_far, acc, top, safe_ref) = refs[count:]
    h = pl.program_id(0)

    @pl.when(h == 0)
    def _():
        project_keys(blocks, wqkv, kv_out)
        safe_ref[0] = bounded(q[...], kv_out[:, :D]).astype(jnp.int32)

    attend(h, safe_ref[0] == 1, q, kv_out, w_out, acc, top, kv_out.shape[0])
    cols = pair_columns(h)
    most = jnp.maximum(top[...], top_near[:, cols])
    near = jnp.exp2(top_near[:, cols] - most)
    far = jnp.exp2(top[...] - most)
    inverse = 1.0 / (sum_near[:, cols] * near + pltpu.roll(acc[...], HEAD_DIM, 1) * far)
    put_head(att_out, h, (att_near[:, cols] * near + acc[...] * far) * inverse)
    put_head(inv_near, h, near * inverse)
    put_head(inv_far, h, far * inverse)


def slab_rows(depth, columns, parts):
    return depth * columns // parts // WIDE


def padded_rows(rows, objects):
    unit = 16 * objects
    return -(-rows // unit) * unit


def slab_pieces(depth, each):
    lanes = math.gcd(each, WIDE)
    deep = depth * lanes // WIDE
    return [
        (i * deep, k * lanes, k * deep, i * lanes, deep, lanes)
        for i in range(each // lanes)
        for k in range(WIDE // lanes)
    ]


def slabs(out_ref, base, grad):
    parts = out_ref.shape[0]
    depth, columns = grad.shape
    each = columns // parts
    grad = grad.astype(out_ref.dtype)
    for b in range(parts):
        for to_row, to_lane, row, col, deep, lanes in slab_pieces(depth, each):
            start = b * each + col
            out_ref[b, base + to_row : base + to_row + deep, to_lane : to_lane + lanes] = grad[
                row : row + deep, start : start + lanes
            ]


def clear_tail(out_ref, used):
    if used < out_ref.shape[1]:
        rest = out_ref.shape[1] - used
        out_ref[:, used:, :] = jnp.zeros((out_ref.shape[0], rest, WIDE), out_ref.dtype)


def mlp_kernel(
    self_att, after_one, inv_near, inv_far, cotangent, wo, up, down, gain, bias, mod,
    mixed, grad_two, do_near, x_near, do_far, x_far, modes, g_out,
):
    self_low = self_att[...].astype(bf16)
    two = after_one[...] + nn(self_low, wo[...])
    rows3 = norm_rows(gain, bias, mod, 2)
    third_in = modulate(two, *rows3).astype(bf16)
    cot = cotangent[...]
    final = two
    norm_grad = jnp.zeros_like(two)
    ff = up.shape[1]
    step = 512
    up_base = slab_rows(D, D, g_out.shape[0])
    down_base = up_base + slab_rows(D, ff, g_out.shape[0])
    for f in range(0, ff, step):
        hidden = nn(third_in, up[:, f : f + step])
        square = hidden * hidden
        inner = GELU_A * hidden * (1.0 + GELU_B * square)
        t = jnp.tanh(inner)
        half = 0.5 * (1.0 + t)
        active = (hidden * half).astype(bf16)
        slope = half + 0.5 * hidden * (1.0 - t * t) * (GELU_A * (1.0 + 3.0 * GELU_B * square))
        final = final + nn(active, down[f : f + step, :])
        hidden_grad = (nt(cot, down[f : f + step, :]) * slope).astype(bf16)
        norm_grad = norm_grad + nt(hidden_grad, up[:, f : f + step])
        up_part = tn(third_in, hidden_grad)
        down_part = tn(active, cot)
        parts = g_out.shape[0]
        each = ff // parts
        for i in range(step // WIDE):
            col = f + i * WIDE
            base = up_base + col % each // WIDE * D
            g_out[col // each, base : base + D, :] = up_part[:, i * WIDE : (i + 1) * WIDE].astype(bf16)
        each = D // parts
        fold = max(1, WIDE // each)
        deep, lanes = ff // fold, min(each, WIDE)
        at = slice(f // deep * lanes, f // deep * lanes + lanes)
        down_part = down_part.astype(bf16)
        for b in range(parts):
            for i in range(max(1, each // WIDE)):
                start = b * each + i * WIDE
                base = down_base + i * ff + f % deep
                g_out[b, base : base + step, at] = down_part[:, start : start + lanes]
    clear_tail(g_out, down_base + slab_rows(ff, D, g_out.shape[0]))
    mixed[...] = final.astype(bf16)
    back, sums = modulate_back(norm_grad, two, rows3[0], rows3[1], rows3[3])
    modes[...] = sums
    grad = cot.astype(f32) + back
    grad_two[...] = grad
    self_grad = grad.astype(bf16)
    slabs(g_out, 0, tn(self_low, self_grad))
    att_grad = nt(self_grad, wo[...])
    for inv, do_out, x_out in ((inv_near, do_near, x_near), (inv_far, do_far, x_far)):
        do = (att_grad * inv[...]).astype(bf16)
        do_out[...] = do
        x_out[...] = delta_lanes(do.astype(f32) * self_att[...])


def project_back(dkvt, wqkv, part_out):
    count, rows, _ = part_out.shape
    for b in range(count):
        part = nn(wqkv[:, D:], dkvt[:, b * rows : (b + 1) * rows])
        part_out[b] = part.astype(bf16).T


class Mover:
    def __init__(self, send, recv):
        self.send, self.recv = send, recv
        self.copies = []
        place, obj = lax.axis_index("blk"), lax.axis_index("obj")
        self.chips = lax.axis_size("blk") // 2
        self.columns = lax.axis_size("obj") // 2
        self.core, self.chip = lax.rem(place, 2), place // 2
        self.side, self.column = lax.rem(obj, 2), obj // 2
        self.sibling = {"blk": self.chip * 2 + 1 - self.core}
        self.chip_ids = [lax.rem(self.chip + d, self.chips) for d in range(1, self.chips)]
        self.chip_peers = [{"blk": c * 2 + self.core} for c in self.chip_ids]
        self.across = {"obj": self.column * 2 + 1 - self.side}
        self.column_ids = [lax.rem(self.column + d, self.columns) for d in range(1, self.columns)]
        self.column_peers = [{"obj": c * 2 + self.side} for c in self.column_ids]

    def barrier(self):
        everyone = [self.sibling, self.across] + self.chip_peers + self.column_peers
        semaphore = pltpu.get_barrier_semaphore()
        for target in everyone:
            pl.semaphore_signal(semaphore, inc=1, device_id=target, device_id_type=pl.DeviceIdType.MESH)
        pl.semaphore_wait(semaphore, len(everyone))

    def copy(self, src, dst, target):
        at = len(self.copies)
        made = pltpu.make_async_remote_copy(
            src_ref=src, dst_ref=dst, send_sem=self.send.at[at], recv_sem=self.recv.at[at],
            device_id=target, device_id_type=pl.DeviceIdType.MESH,
        )
        self.copies.append(made)
        return made

    def drain(self):
        for made in self.copies:
            made.wait_send()


def begin(copies):
    for made in copies:
        made.start()


def arrive(copies):
    for made in copies:
        made.wait_recv()


def added(*values):
    total = values[0].astype(f32)
    for value in values[1:]:
        total = total + value.astype(f32)
    return total.astype(bf16)


def cut(rows, objects):
    unit = 16 * objects
    first = (rows // unit + 1) // 2 * unit
    return first, rows - first


class Gather:
    @staticmethod
    def scratch(chips, rows, objects, lanes):
        first, second = cut(rows, objects)
        return [
            VMEM((chips, rows, lanes), bf16),
            VMEM((max(chips - 1, 1), first, lanes), bf16), VMEM((2, first // 2, lanes), bf16), VMEM((first // 2, lanes), bf16),
            VMEM((chips, second // 2, lanes), bf16), VMEM((chips, second // 2, lanes), bf16),
            VMEM((max(chips - 1, 1), second // 2, lanes), bf16),
        ]

    @staticmethod
    def copies(chips):
        return 2 * chips + 2 * (chips - 1) + 1 + chips

    def __init__(self, mover, g, scratch, out_first, out_second):
        self.mover, self.g = mover, g
        self.mine, self.far0, self.flat0, self.across0, self.across1, self.mine1, self.far1 = scratch
        self.out0, self.out1 = out_first, out_second
        first, half1 = self.far0.shape[1], self.mine1.shape[1]
        m, chips = mover, mover.chips
        self.rows = (slice(0, first), slice(first, first + 2 * half1))
        other = 1 - m.core
        self.core = [
            [m.copy(g.at[2 * j + other, rows], self.mine.at[j, rows], m.sibling) for j in range(chips)]
            for rows in self.rows
        ]
        self.chip0 = [
            m.copy(self.mine.at[c, self.rows[0]], self.far0.at[d], peer)
            for d, (c, peer) in enumerate(zip(m.chip_ids, m.chip_peers))
        ]
        self.side0 = [m.copy(self.flat0.at[1 - m.side], self.across0, m.across)]
        away = pl.ds(pl.multiple_of(first + (1 - m.side) * half1, 16), half1)
        self.kept = pl.ds(pl.multiple_of(first + m.side * half1, 16), half1)
        self.side1 = [m.copy(self.mine.at[j, away], self.across1.at[j], m.across) for j in range(chips)]
        self.chip1 = [
            m.copy(self.mine1.at[c], self.far1.at[d], peer)
            for d, (c, peer) in enumerate(zip(m.chip_ids, m.chip_peers))
        ]

    def step0(self):
        begin(self.core[0] + self.core[1])

    def step1(self):
        for group, after in ((0, self.chip0), (1, self.side1)):
            arrive(self.core[group])
            rows = self.rows[group]
            for j in range(self.mover.chips):
                self.mine[j, rows] = added(self.g[2 * j + self.mover.core, rows], self.mine[j, rows])
            begin(after)

    def step2(self):
        m = self.mover
        arrive(self.chip0)
        total = added(self.mine[m.chip, self.rows[0]], *[self.far0[d] for d in range(m.chips - 1)])
        self.flat0[...] = total.reshape(self.flat0.shape)
        begin(self.side0)
        arrive(self.side1)
        for j in range(m.chips):
            self.mine1[j] = added(self.mine[j, self.kept], self.across1[j])
        begin(self.chip1)

    def step3(self):
        m = self.mover
        arrive(self.side0)
        self.out0[...] = added(self.flat0[m.side], self.across0[...])
        arrive(self.chip1)
        self.out1[...] = added(self.mine1[m.chip], *[self.far1[d] for d in range(m.chips - 1)])


class Spread:
    @staticmethod
    def scratch(objects, half, lanes):
        columns = objects // 2
        return VMEM((max(columns - 1, 1), half // columns, lanes), bf16)

    @staticmethod
    def copies(objects):
        return 2 * (objects // 2 - 1) + 1

    def __init__(self, mover, half, taken, out):
        m = mover
        self.mover, self.half, self.taken, self.out = mover, half, taken, out
        piece = taken.shape[1]
        self.piece = pl.ds(pl.multiple_of(m.column * piece, 16), piece)
        self.sums = [
            m.copy(half.at[pl.ds(pl.multiple_of(c * piece, 16), piece)], taken.at[d], peer)
            for d, (c, peer) in enumerate(zip(m.column_ids, m.column_peers))
        ]
        own = out.at[m.side, m.column]
        self.shares = [m.copy(own, own, peer) for peer in m.column_peers]
        self.sides = [m.copy(out.at[m.side], out.at[m.side], m.across)]

    def step0(self):
        begin(self.sums)

    def step1(self):
        arrive(self.sums)
        m = self.mover
        self.out[m.side, m.column] = added(
            self.half[self.piece], *[self.taken[d] for d in range(m.columns - 1)]
        )
        begin(self.shares)

    def step2(self):
        arrive(self.shares)
        begin(self.sides)

    def step3(self):
        arrive(self.sides)


def self_back_kernel(
    count, do_far, x_far, do_near, x_near, q, kv_far, kv_near, w_far, w_near, wqkv, g_early, own, sibling, *refs
):
    blocks = refs[:count]
    (norm_grad, g_out, out0, out1, dq, dkvt_far, dkvt_near, do_far_t, do_near_t, q_t, far_parts, near_parts,
     from_sibling, chip_sums, from_chips, near_sibling, half0, half1, taken0, taken1, sums0, sums1) = refs[count : count + 22]
    gather_scratch, moving = refs[count + 22 : -2], refs[-2:]
    h = pl.program_id(0)
    m = Mover(*moving)
    gather = Gather(m, g_early, gather_scratch, half0, half1)
    spreads = [Spread(m, half0, taken0, sums0), Spread(m, half1, taken1, sums1)]
    chips = m.chips
    far_core = [m.copy(far_parts.at[2 * d + 1], from_sibling.at[d], m.sibling) for d in range(chips - 1)]
    back = [{"blk": lax.rem(m.chip + chips - d, chips) * 2 + m.core} for d in range(1, chips)]
    far_chip = [m.copy(chip_sums.at[d], from_chips.at[d], back[d]) for d in range(chips - 1)]
    near_core = [m.copy(near_parts.at[1], near_sibling, m.sibling)]

    @pl.when(h == 0)
    def _():
        m.barrier()
        gather.step0()
        do_far_t[...] = do_far[...].T
        do_near_t[...] = do_near[...].T
        q_t[...] = q[...].T
        dq[...] = jnp.zeros_like(dq)

    @pl.when(h == 1)
    def _():
        gather.step1()

    @pl.when(h == 6)
    def _():
        gather.step2()

    @pl.when(h == HEADS)
    def _():
        project_back(dkvt_far, wqkv, far_parts)
        begin(far_core)
        gather.step3()
        for spread in spreads:
            spread.step0()

    @pl.when(h == HEADS + 1)
    def _():
        arrive(far_core)
        for d in range(chips - 1):
            chip_sums[d] = added(far_parts[2 * d], from_sibling[d])
        begin(far_chip)

    @pl.when(h == HEADS + 4)
    def _():
        spreads[0].step1()

    @pl.when(h == HEADS + 5)
    def _():
        spreads[1].step1()

    @pl.when(h == HEADS + 7)
    def _():
        spreads[0].step2()

    @pl.when(h < HEADS)
    def _():
        attend_back(h, do_far, x_far, do_far_t, q_t, kv_far, w_far, dq, dkvt_far, kv_far.shape[0], 512)

    @pl.when(h >= HEADS)
    def _():
        attend_back(h - HEADS, do_near, x_near, do_near_t, q_t, kv_near, w_near, dq, dkvt_near, kv_near.shape[0], 512)

    @pl.when(h == 2 * HEADS - 1)
    def _():
        project_back(dkvt_near, wqkv, near_parts)
        begin(near_core)
        dq_low = dq[...].astype(bf16)
        rows = own.shape[0]
        grad = nn(dkvt_near[:, :rows], own[...]) + nn(dkvt_near[:, rows:], sibling[...])
        spreads[1].step2()
        for i, block in enumerate(blocks):
            grad = grad + nn(dkvt_far[:, i * rows : (i + 1) * rows], block[...])
        slabs(g_out, 0, jnp.concatenate([tn(own[...], dq_low), grad.T], 1))
        total = nt(dq_low, wqkv[:, :D]) + near_parts[0].astype(f32)
        arrive(far_chip)
        for d in range(chips - 1):
            total = total + from_chips[d].astype(f32)
        arrive(near_core)
        norm_grad[...] = total + near_sibling[...].astype(f32)
        for spread, out in zip(spreads, (out0, out1)):
            spread.step3()
            out[...] = spread.out[...]
        m.drain()


def cross_back_kernel(
    context_count, norm_grad, grad_two, after_one, tokens, context, q, pair, w, att, inv,
    wq, wkv, wo, gain, bias, mod, g_middle, modes_three, lifted,
    tokens_grad, ctx_result, small_result, mid0, mid1, late0, late1,
    dkvt, do, x, do_t, q_t, dq, g_mid, g_late, small, ctx,
    ctx_half, ctx_mine, ctx_far, small_half, small_mine, small_far, *rest
):
    h = pl.program_id(0)
    mid_scratch, late_scratch, rest = rest[0:7], rest[7:14], rest[14:]
    mid_half0, mid_half1, late_half0, late_half1 = rest[0:4]
    mid_taken0, mid_taken1, late_taken0, late_taken1 = rest[4:8]
    mid_sums0, mid_sums1, late_sums0, late_sums1, ctx_out, small_out = rest[8:14]
    m = Mover(*rest[14:16])
    chips = m.chips
    mid = Gather(m, g_mid, mid_scratch, mid_half0, mid_half1)
    mid_spread = [Spread(m, mid_half0, mid_taken0, mid_sums0), Spread(m, mid_half1, mid_taken1, mid_sums1)]
    late = Gather(m, g_late, late_scratch, late_half0, late_half1)
    late_spread = [Spread(m, late_half0, late_taken0, late_sums0), Spread(m, late_half1, late_taken1, late_sums1)]
    ctx_rows = ctx.shape[0] // 2
    ctx_own = pl.ds(pl.multiple_of(m.core * ctx_rows, 16), ctx_rows)
    ctx_other = pl.ds(pl.multiple_of((1 - m.core) * ctx_rows, 16), ctx_rows)
    ctx_core = [m.copy(ctx.at[ctx_other], ctx_half, m.sibling)]
    ctx_chip = [m.copy(ctx_mine, ctx_far.at[d], m.chip_peers[d]) for d in range(chips - 1)]
    ctx_back = [m.copy(ctx_out.at[ctx_own], ctx_out.at[ctx_own], m.sibling)]
    small_core = [m.copy(small, small_half, m.sibling)]
    small_chip = [m.copy(small_mine, small_far.at[d], m.chip_peers[d]) for d in range(chips - 1)]
    own_small = small_out.at[m.column, m.side]
    small_side = [m.copy(own_small, own_small, m.across)]
    small_column = [m.copy(small_out.at[m.column], small_out.at[m.column], peer) for peer in m.column_peers]
    middle_rows = g_middle.shape[1]
    late_base = slab_rows(D, D, g_late.shape[0])

    @pl.when(h == 0)
    def _():
        m.barrier()
        g_mid[:, :middle_rows, :] = g_middle[...]
        rows = norm_rows(gain, bias, mod, 1)
        back, sums = modulate_back(norm_grad[...], after_one[...], rows[0], rows[1], rows[3])
        grad_one = grad_two[...] + back
        tokens_grad[...] = grad_one
        small[4:8, :] = sums
        small[8:12, :] = modes_three[...]
        small[12:14, :] = lifted[...]
        small[14:16, :] = jnp.zeros((2, D), f32)
        cross_grad = grad_one.astype(bf16)
        slabs(g_mid, middle_rows, tn(att[...].astype(bf16), cross_grad))
        clear_tail(g_mid, middle_rows + slab_rows(D, D, g_mid.shape[0]))
        mid.step0()
        do[...] = (nt(cross_grad, wo[...]) * inv[...]).astype(bf16)
        x[...] = delta_lanes(do[...].astype(f32) * att[...])
        do_t[...] = do[...].T
        q_t[...] = q[...].T
        dq[...] = jnp.zeros_like(dq)

    @pl.when(h == 1)
    def _():
        mid.step1()

    @pl.when(h == 4)
    def _():
        mid.step2()

    @pl.when(h == 6)
    def _():
        mid.step3()
        for spread in mid_spread:
            spread.step0()

    attend_back(h, do, x, do_t, q_t, pair, w, dq, dkvt, context_count, pair.shape[0])

    @pl.when(h == HEADS - 1)
    def _():
        dq_low = dq[...].astype(bf16)
        first = tokens[...].astype(f32)
        rows = norm_rows(gain, bias, mod, 0)
        first_in = modulate(first, *rows).astype(bf16)
        slabs(g_late, 0, tn(first_in, dq_low))
        real = lax.broadcasted_iota(jnp.int32, dkvt.shape, 1) < context_count
        kept = jnp.where(real, dkvt[...], jnp.zeros_like(dkvt))
        slabs(g_late, late_base, nn(kept, context[...]).T)
        clear_tail(g_late, late_base + slab_rows(context.shape[1], 2 * D, g_late.shape[0]))
        late.step0()
        ctx[...] = tn(dkvt[...], wkv[...].T).astype(bf16)
        begin(ctx_core)
        for spread in mid_spread:
            spread.step1()
        back, sums = modulate_back(nt(dq_low, wq[...]), first, rows[0], rows[1], rows[3])
        small[0:4, :] = sums
        begin(small_core)
        late.step1()
        arrive(ctx_core)
        ctx_mine[...] = added(ctx[ctx_own], ctx_half[...])
        begin(ctx_chip)
        arrive(small_core)
        small_mine[...] = small[...] + small_half[...]
        begin(small_chip)
        tokens_grad[...] = tokens_grad[...] + back
        for spread in mid_spread:
            spread.step2()
        late.step2()
        arrive(small_chip)
        total = small_mine[...]
        for d in range(chips - 1):
            total = total + small_far[d]
        small_out[m.column, m.side] = total
        begin(small_side)
        late.step3()
        for spread in late_spread:
            spread.step0()
        arrive(ctx_chip)
        ctx_out[ctx_own] = added(ctx_mine[...], *[ctx_far[d] for d in range(chips - 1)])
        begin(ctx_back)
        arrive(small_side)
        begin(small_column)
        for spread in late_spread:
            spread.step1()
        for spread in late_spread:
            spread.step2()
        for spread, out in zip(mid_spread, (mid0, mid1)):
            spread.step3()
            out[...] = spread.out[...]
        arrive(ctx_back)
        ctx_result[...] = ctx_out[...]
        arrive(small_column)
        small_result[...] = small_out[...]
        for spread, out in zip(late_spread, (late0, late1)):
            spread.step3()
            out[...] = spread.out[...]
        m.drain()


def finish_kernel(parts, early0, early1, mid0, mid1, late0, late1, small, so, up, down, qkv, co, cq, ckv, gains, biases, modw, modb, mode):
    place = lax.axis_index("blk")
    objects = small.shape[0]
    width = 2 * D // parts
    each = D // parts

    def put(out, total, base):
        depth, columns = out.shape
        for to_row, to_lane, row, col, deep, lanes in slab_pieces(depth, columns):
            out[row : row + deep, col : col + lanes] = total[
                base + to_row : base + to_row + deep, to_lane : to_lane + lanes
            ].astype(f32)
        return base + slab_rows(depth, columns, 1)

    early = jnp.concatenate([early0[...], early1[...]], 0)
    base = put(so, early, 0)
    base = put(up, early, base)
    put(down, early, base)
    middle = jnp.concatenate([mid0[...], mid1[...]], 0)
    base = put(qkv, middle, 0)
    put(co, middle, base)
    late = jnp.concatenate([late0[...], late1[...]], 0)
    base = put(cq, late, 0)
    put(ckv, late, base)
    lifted = jnp.concatenate([small[:, 12, :], small[:, 13, :]], 1)
    summed = jnp.sum(small[...], 0)
    for b in range(parts):
        @pl.when(place == b)
        def _():
            row, col = b * width // D, b * width % D
            for j in range(3):
                mode[j] = small[:, 4 * j + row, col : col + width]
                gains[j : j + 1, :] = summed[4 * j + 2 : 4 * j + 3, b * each : (b + 1) * each]
                biases[j : j + 1, :] = summed[4 * j + 3 : 4 * j + 4, b * each : (b + 1) * each]
    for j in range(3):
        modw[j] = lax.dot_general(
            lifted, mode[j], (((0,), (0,)), ((), ())), precision=lax.Precision.HIGHEST, preferred_element_type=f32
        )
        modb[j : j + 1, :] = jnp.sum(mode[j], 0, keepdims=True)


def shape(dims, dtype):
    return jax.ShapeDtypeStruct(tuple(dims), dtype)


def body(
    tokens, context, camera_groups, camera_table, cross_query, cross_kv, cross_out, self_qkv,
    self_out, mlp_up, mlp_down, norm_gain, norm_bias, mod_weight, mod_bias, cotangent,
):
    parts = lax.axis_size("blk")
    tokens = tokens[0]
    cotangent = cotangent[0]
    context_count = context.shape[1]
    rows = tokens.shape[0]
    length = rows * parts
    ff = mlp_up.shape[1]
    cam_width = mod_weight.shape[1]
    ctx_width = context.shape[2]
    padded = -(-context_count // 128) * 128
    context_rows = jnp.pad(context[0], ((0, padded - context_count), (0, 0)), mode="edge")

    picked = (
        camera_groups[:, None] == jnp.arange(camera_table.shape[0], dtype=jnp.int32)[None, :]
    ).astype(bf16)
    camera = jnp.dot(picked, camera_table, preferred_element_type=f32)
    lifted = jax.nn.silu(camera).astype(bf16)
    mod = (
        jnp.einsum("oc,jcm->ojm", lifted, mod_weight, preferred_element_type=f32)
        + mod_bias.astype(f32)
    )[0]

    def near_hop(block):
        return lax.ppermute(block, "blk", [(i, i ^ 1) for i in range(parts)])

    def chip_hop(block, distance):
        route = [(i, (i // 2 + distance) % chips * 2 + i % 2) for i in range(parts)]
        return lax.ppermute(block, "blk", route)

    chips = parts // 2
    objects = lax.axis_size("obj")
    full = lambda *dims: pl.BlockSpec(dims, lambda h: (0,) * len(dims))
    head = lambda keys: pl.BlockSpec((1, rows, keys), lambda h: (h, 0, 0))
    row_full = full(rows, D)
    row_f32, row_bf16 = shape((rows, D), f32), shape((rows, D), bf16)
    per_head = [VMEM((rows, WIDE), f32), VMEM((rows, WIDE), f32), pltpu.SMEM((1,), jnp.int32)]
    transposed = [VMEM((D, rows), bf16), VMEM((D, rows), bf16)]
    norm_full = [full(3, D), full(3, D), full(3, 2 * D)]

    def call(kernel, name, us, outs, ins, out_specs, scratch=(), collective_id=None, **more):
        return pl.pallas_call(
            kernel, name=name, out_shape=outs, in_specs=ins, out_specs=out_specs, scratch_shapes=list(scratch),
            cost_estimate=pl.CostEstimate(flops=int(us * 1.1e9), bytes_accessed=int(us * 3.6e6), transcendentals=0),
            compiler_params=params() if collective_id is None else pltpu.CompilerParams(
                vmem_limit_bytes=62 * MIB, collective_id=collective_id, has_side_effects=True
            ), **more,
        )

    second_in, after_one, cross_q, cross_pair, cross_w, cross_att, cross_inv = call(
        functools.partial(cross_kernel, context_count), "cross_forward", 15,
        [row_bf16, row_f32, row_bf16, shape((padded, 2 * D), bf16), shape((HEADS, rows, padded), bf16), row_f32, row_f32],
        [row_full, full(padded, ctx_width), full(D, D), full(ctx_width, 2 * D), full(D, D)] + norm_full,
        [row_full, row_full, row_full, full(padded, 2 * D), head(padded), row_full, row_full],
        per_head, grid=(HEADS,),
    )(tokens, context_rows, cross_query, cross_kv, cross_out, norm_gain, norm_bias, mod)

    sibling_in = near_hop(second_in)
    to_chips, sibling_in = lax.optimization_barrier((second_in, sibling_in))
    chip_in = [chip_hop(to_chips, d) for d in range(1, chips)]
    near_keys, far_keys = 2 * rows, 2 * rows * (chips - 1)
    near_w, self_q, near_kv, near_sum, near_att, near_top = call(
        near_kernel, "near_forward", 16,
        [shape((HEADS, rows, near_keys), bf16), row_bf16, shape((near_keys, 2 * D), bf16), row_f32, row_f32, row_f32],
        [row_full, row_full, full(D, 3 * D)],
        [head(near_keys), row_full, full(near_keys, 2 * D), row_full, row_full, row_full],
        per_head, grid=(HEADS,),
    )(second_in, sibling_in, self_qkv)
    chip_in, near_kv = lax.optimization_barrier((chip_in, near_kv))
    far_in = []
    for block in chip_in:
        far_in += [block, near_hop(block)]
    count = len(far_in)
    far_w, far_kv, self_att, near_inv, far_inv = call(
        functools.partial(far_kernel, count), "far_forward", 16,
        [shape((HEADS, rows, far_keys), bf16), shape((far_keys, 2 * D), bf16), row_f32, row_f32, row_f32],
        [row_full] * count + [full(D, 3 * D)] + [row_full] * 4,
        [head(far_keys), full(far_keys, 2 * D), row_full, row_full, row_full],
        per_head, grid=(HEADS,),
    )(*far_in, self_qkv, self_q, near_sum, near_att, near_top)

    lanes = WIDE
    tall = lambda columns, depth: slab_rows(depth, columns, parts)
    early = padded_rows(tall(D, D) + tall(ff, D) + tall(D, ff), objects)
    mixed, grad_two, near_do, near_x, far_do, far_x, modes_three, g_early = call(
        mlp_kernel, "feed_forward", 20,
        [row_bf16, row_f32, row_bf16, row_bf16, row_bf16, row_bf16, shape((4, D), f32), shape((parts, early, lanes), bf16)],
        [whole()] * 11, [whole()] * 8,
    )(self_att, after_one, near_inv, far_inv, cotangent, self_out, mlp_up, mlp_down, norm_gain, norm_bias, mod)

    unit = objects // 2
    moving = lambda copies: [pltpu.SemaphoreType.DMA((copies,)), pltpu.SemaphoreType.DMA((copies,))]
    halves = lambda rows: [shape((n // 2, lanes), bf16) for n in cut(rows, objects)]
    half_vmem = lambda rows: [VMEM((n // 2, lanes), bf16) for n in cut(rows, objects)]
    spread_outs = lambda rows: [shape((2, unit, n // objects, lanes), bf16) for n in cut(rows, objects)]
    taken = lambda rows: [Spread.scratch(objects, n // 2, lanes) for n in cut(rows, objects)]
    in_vmem = lambda shapes: [VMEM(item.shape, item.dtype) for item in shapes]
    once = lambda *dims: pl.BlockSpec(dims, lambda h: (0,) * len(dims), pipeline_mode=pl.Buffered(1))
    like = lambda shapes: [once(*item.shape) for item in shapes]
    row_once = once(rows, D)

    middle = tall(3 * D, D)
    spread_shapes = spread_outs(early)
    hops = VMEM((chips - 1, rows, D), bf16)
    norm_grad, g_middle, early0, early1 = call(
        functools.partial(self_back_kernel, count), "self_backward", 60,
        [row_f32, shape((parts, middle, lanes), bf16)] + spread_shapes,
        [row_once] * 5 + [once(far_keys, 2 * D), once(near_keys, 2 * D),
         pl.BlockSpec((1, rows, far_keys), lambda h: (jnp.minimum(h, HEADS - 1), 0, 0)),
         pl.BlockSpec((1, rows, near_keys), lambda h: (jnp.maximum(h - HEADS, 0), 0, 0)),
         once(D, 3 * D), once(parts, early, lanes)] + [row_once] * (2 + count),
        [row_once, once(parts, middle, lanes)] + like(spread_shapes),
        [VMEM((rows, D), f32), VMEM((2 * D, far_keys), bf16), VMEM((2 * D, near_keys), bf16)]
        + [VMEM((D, rows), bf16)] * 3 + [VMEM((count, rows, D), bf16), VMEM((2, rows, D), bf16)]
        + [hops, hops, hops, VMEM((rows, D), bf16)] + half_vmem(early) + taken(early) + in_vmem(spread_shapes)
        + Gather.scratch(chips, early, objects, lanes)
        + moving(Gather.copies(chips) + 2 * (chips - 1) + 1 + 2 * Spread.copies(objects)),
        grid=(2 * HEADS,), collective_id=1,
    )(far_do, far_x, near_do, near_x, self_q, far_kv, near_kv, far_w, near_w, self_qkv, g_early,
      second_in, sibling_in, *far_in)

    late = padded_rows(tall(D, D) + tall(2 * D, ctx_width), objects)
    mid = padded_rows(middle + tall(D, D), objects)
    lifted_rows = lifted.astype(f32).reshape(2, D) * (1.0 / parts)
    mid_shapes, late_shapes = spread_outs(mid), spread_outs(late)
    ctx_half = VMEM((padded // 2, ctx_width), bf16)
    small_vmem = VMEM((16, D), f32)
    tokens_grad, context_sum, small_all, mid0, mid1, late0, late1 = call(
        functools.partial(cross_back_kernel, context_count), "cross_backward", 20,
        [row_f32, shape((padded, ctx_width), bf16), shape((unit, 2, 16, D), f32)] + mid_shapes + late_shapes,
        [row_once] * 4 + [once(padded, ctx_width), row_once, once(padded, 2 * D), head(padded), row_once, row_once,
         once(D, D), once(ctx_width, 2 * D), once(D, D)] + norm_full + [once(parts, middle, lanes), full(4, D), full(2, D)],
        [row_once, once(padded, ctx_width), once(unit, 2, 16, D)] + like(mid_shapes) + like(late_shapes),
        [VMEM((2 * D, padded), bf16), VMEM((rows, D), bf16), VMEM((rows, D), bf16)] + transposed + [VMEM((rows, D), f32)]
        + [VMEM((parts, mid, lanes), bf16), VMEM((parts, late, lanes), bf16), small_vmem, VMEM((padded, ctx_width), bf16)]
        + [ctx_half, ctx_half, VMEM((chips - 1, padded // 2, ctx_width), bf16)]
        + [small_vmem, small_vmem, VMEM((chips - 1, 16, D), f32)]
        + Gather.scratch(chips, mid, objects, lanes) + Gather.scratch(chips, late, objects, lanes)
        + half_vmem(mid) + half_vmem(late) + taken(mid) + taken(late) + in_vmem(mid_shapes) + in_vmem(late_shapes)
        + [VMEM((padded, ctx_width), bf16), VMEM((unit, 2, 16, D), f32)]
        + moving(2 * Gather.copies(chips) + 4 * Spread.copies(objects) + 2 + chips - 1 + 2 + chips - 1 + unit - 1),
        grid=(HEADS,), collective_id=2,
    )(
        norm_grad, grad_two, after_one, tokens, context_rows, cross_q, cross_pair, cross_w,
        cross_att, cross_inv, cross_query, cross_kv, cross_out, norm_gain, norm_bias, mod, g_middle, modes_three,
        lifted_rows,
    )
    context_grad = context_sum[:context_count].astype(f32)

    width = 2 * D // parts
    grads = lambda depth, columns: shape((depth, columns // parts), f32)
    so, up, down, qkv, co, cq, ckv, gains, biases, modw, modb = pl.pallas_call(
        functools.partial(finish_kernel, parts),
        name="finish",
        out_shape=[
            grads(D, D), grads(D, ff), grads(ff, D), grads(D, 3 * D), grads(D, D), grads(D, D), grads(ctx_width, 2 * D),
            grads(3, D), grads(3, D), shape((3, cam_width, width), f32), grads(3, 2 * D),
        ],
        in_specs=[whole()] * 7,
        out_specs=[whole()] * 11,
        scratch_shapes=[VMEM((3, objects, width), f32)],
        compiler_params=params(),
    )(*[v.reshape(-1, lanes) for v in (early0, early1, mid0, mid1, late0, late1)], small_all.reshape(objects, 16, D))
    return (
        mixed[None], tokens_grad[None], context_grad[None], cq, ckv, co, qkv, so, up, down, gains, biases, modw, modb,
    )


def solution(mesh):
    rows = P("obj", "blk", None)
    columns = P(None, "blk")
    return jax.shard_map(
        body,
        mesh=mesh,
        in_specs=(rows, P("obj", None, None), P("obj")) + (P(),) * 12 + (rows,),
        out_specs=(rows, rows, P("obj", None, None)) + (columns,) * 9
        + (P(None, None, "blk"), columns),
        check_vma=False,
    )
```

```python
import functools
import math

import jax
import jax.numpy as jnp
from jax import lax
from jax.experimental import pallas as pl
from jax.experimental.pallas import tpu as pltpu
from jax.sharding import PartitionSpec as P

D = 512
HEADS = 8
HEAD_DIM = 64
PAIRS = HEADS // 2
WIDE = 2 * HEAD_DIM
LOG2E = 1.4426950408889634
LN2 = 0.6931471805599453
QUERY_FACTOR = LOG2E * HEAD_DIM ** (-0.5)
SCORE_FACTOR = HEAD_DIM ** (-0.5)
SAFE_SQUARE = 60.0 ** 2
EPSILON = 1e-06
GELU_A = 0.7978845608028654
GELU_B = 0.044715
MIB = 2**20

f32 = jnp.float32
bf16 = jnp.bfloat16
VMEM = pltpu.VMEM


def nn(a, b):
    return lax.dot_general(a, b, (((1,), (0,)), ((), ())), preferred_element_type=f32)


def nt(a, b):
    return lax.dot_general(a, b, (((1,), (1,)), ((), ())), preferred_element_type=f32)


def tn(a, b):
    return lax.dot_general(a, b, (((0,), (0,)), ((), ())), preferred_element_type=f32)


def whole():
    return pl.BlockSpec(memory_space=VMEM)


def params(mib=60):
    return pltpu.CompilerParams(vmem_limit_bytes=mib * MIB)


def lower_half(shape):
    return lax.broadcasted_iota(jnp.int32, shape, 1) % WIDE < HEAD_DIM


def own_half(shape, odd):
    lower = lower_half(shape)
    return jnp.logical_not(lower) if odd else lower


def normalize(x):
    center = x - jnp.mean(x, -1, keepdims=True)
    inverse = lax.rsqrt(jnp.mean(center * center, -1, keepdims=True) + EPSILON)
    return center * inverse, inverse


def modulate(x, gain, bias, shift, scale):
    normed, _ = normalize(x)
    return (normed * gain + bias) * (1.0 + scale) + shift


def modulate_back(g, x, gain, bias, scale):
    normed, inverse = normalize(x)
    affine = normed * gain + bias
    shift_grad = jnp.sum(g, 0, keepdims=True)
    scale_grad = jnp.sum(g * affine, 0, keepdims=True)
    a = g * (1.0 + scale)
    gain_grad = jnp.sum(a * normed, 0, keepdims=True)
    bias_grad = jnp.sum(a, 0, keepdims=True)
    n = a * gain
    back = inverse * (
        n - jnp.mean(n, -1, keepdims=True) - normed * jnp.mean(n * normed, -1, keepdims=True)
    )
    return back, jnp.concatenate([shift_grad, scale_grad, gain_grad, bias_grad], 0)


def norm_rows(gain_ref, bias_ref, mod_ref, j):
    gain = gain_ref[j : j + 1, :].astype(f32)
    bias = bias_ref[j : j + 1, :].astype(f32)
    shift = mod_ref[j : j + 1, :D]
    scale = mod_ref[j : j + 1, D:]
    return gain, bias, shift, scale


def head_sums(values, sign):
    rows = lax.broadcasted_iota(jnp.int32, (WIDE, WIDE), 0)
    cols = lax.broadcasted_iota(jnp.int32, (WIDE, WIDE), 1)
    block = jnp.where((rows < HEAD_DIM) != (cols < HEAD_DIM), sign, 0.0).astype(bf16)
    high = values.astype(bf16)
    low = (values - high.astype(f32)).astype(bf16)
    return nn(high, block) + nn(low, block)


def delta_lanes(product):
    parts = []
    for p in range(PAIRS):
        total = head_sums(product[:, p * WIDE : (p + 1) * WIDE], -1.0)
        high = total.astype(bf16).astype(f32)
        low = total - high
        lane = lax.broadcasted_iota(jnp.int32, total.shape, 1) % HEAD_DIM
        parts.append(jnp.where(lane == 0, high, jnp.where(lane == 1, low, 0.0)).astype(bf16))
    return jnp.concatenate(parts, 1)


def norm_top(x):
    rows = lax.broadcasted_iota(jnp.int32, (WIDE, WIDE), 0)
    cols = lax.broadcasted_iota(jnp.int32, (WIDE, WIDE), 1)
    block = jnp.where((rows < HEAD_DIM) == (cols < HEAD_DIM), 1.0, 0.0).astype(bf16)
    top = None
    for p in range(PAIRS):
        part = x[:, p * WIDE : (p + 1) * WIDE].astype(f32)
        here = jnp.max(nn((part * part).astype(bf16), block), 0, keepdims=True)
        top = here if top is None else jnp.maximum(top, here)
    return jnp.max(top)


def bounded(q, k):
    return norm_top(q) * norm_top(k) < SAFE_SQUARE


def pair_columns(head, offset=0):
    return pl.ds(pl.multiple_of(offset + head // 2 * WIDE, WIDE), WIDE)


def head_rows(head, offset=0):
    return pl.ds(pl.multiple_of(offset + head * HEAD_DIM, HEAD_DIM), HEAD_DIM)


def owned(shape, head):
    lane = lax.broadcasted_iota(jnp.int32, shape, 1)
    return lane // HEAD_DIM == head % 2


def key_rows(kv, head):
    k = kv[:, pair_columns(head)]
    return jnp.where(owned(k.shape, head), k, jnp.zeros_like(k))


def value_rows(kv, head, real_keys):
    v = kv[:, pair_columns(head, D)]
    v = jnp.where(owned(v.shape, head), v, jnp.ones_like(v))
    if real_keys < v.shape[0]:
        row = lax.broadcasted_iota(jnp.int32, v.shape, 0)
        v = jnp.where(row < real_keys, v, jnp.zeros_like(v))
    return v


def attend(head, safe, q, kv, w_ref, acc, top, real_keys):
    count = q.shape[0]
    step = min(256, count)

    def blocks(shifted):
        k = key_rows(kv, head)
        v = value_rows(kv, head, real_keys)
        for r in range(0, count, step):
            rows = slice(r, r + step)
            s = nt(q[rows, pair_columns(head)], k)
            if shifted:
                most = jnp.max(s, -1, keepdims=True)
                s = s - most
            w = jnp.exp2(s).astype(bf16)
            w_ref[0, rows, :] = w
            acc[rows, :] = nn(w, v)
            if top is not None:
                top[rows, :] = jnp.broadcast_to(most, (step, WIDE)) if shifted else jnp.zeros((step, WIDE), f32)

    @pl.when(safe)
    def _():
        blocks(False)

    @pl.when(jnp.logical_not(safe))
    def _():
        blocks(True)


def paired(even, odd):
    lower = lower_half(even.shape)
    return jnp.where(lower, even, odd), pltpu.roll(jnp.where(lower, odd, even), HEAD_DIM, 1)


def attend_back(head, do, x, do_t, q_t, kv, w_ref, dq, dkvt, real_keys, chunk):
    left = jnp.where(owned((do.shape[0], WIDE), head), do[:, pair_columns(head)], x[:, pair_columns(head)])
    k = key_rows(kv, head)
    v = value_rows(kv, head, real_keys)
    keys = k.shape[0]
    chunk = chunk if keys % chunk == 0 else keys
    total = None
    for c in range(0, keys, chunk):
        cols = slice(c, c + chunk)
        w = w_ref[0, :, cols]
        dp = nt(left, v[cols])
        ds = (w.astype(f32) * dp).astype(bf16)
        part = nn(ds, k[cols])
        total = part if total is None else total + part
        dkvt[head_rows(head), cols] = (nn(q_t[head_rows(head), :], ds) * LN2).astype(bf16)
        dkvt[head_rows(head, D), cols] = nn(do_t[head_rows(head), :], w).astype(bf16)
    total = total * SCORE_FACTOR

    dq[:, pair_columns(head)] += total


def cross_kernel(
    context_count, tokens, context, wq, wkv, wo, gain, bias, mod,
    second_in, after_one, q_hbm, pair_hbm, w_out, att_out, inv_out, q, pair, att, acc, safe_ref, sems,
):
    h = pl.program_id(0)
    saves = [pltpu.make_async_copy(q, q_hbm, sems.at[0]), pltpu.make_async_copy(pair, pair_hbm, sems.at[1])]

    @pl.when(h == 0)
    def _():
        first_in = modulate(tokens[...].astype(f32), *norm_rows(gain, bias, mod, 0)).astype(bf16)
        q[...] = (nn(first_in, wq[...]) * QUERY_FACTOR).astype(bf16)
        pair[...] = nn(context[...], wkv[...]).astype(bf16)
        safe_ref[0] = bounded(q[...], pair[:, :D]).astype(jnp.int32)
        for save in saves:
            save.start()

    attend(h, safe_ref[0] == 1, q, pair, w_out, acc.at[h % 2], None, context_count)

    @pl.when(h % 2 == 1)
    def _():
        values, sums = paired(acc[0], acc[1])
        inverse = 1.0 / sums
        att_out[...] = values * inverse
        inv_out[...] = inverse
        att[:, pair_columns(h)] = att_out[...].astype(bf16)

    @pl.when(h == HEADS - 1)
    def _():
        one = tokens[...].astype(f32) + nn(att[...], wo[...])
        after_one[...] = one
        second_in[...] = modulate(one, *norm_rows(gain, bias, mod, 1)).astype(bf16)
        for save in saves:
            save.wait()


def project_keys(blocks, wqkv, kv):
    for i, block in enumerate(blocks):
        rows = block.shape[0]
        kv[i * rows : (i + 1) * rows, :] = nn(block[...], wqkv[:, D:]).astype(bf16)


def near_kernel(own, sibling, wqkv, w_out, q_hbm, kv_hbm, acc_out, top_out, q, kv, safe_ref, sems):
    h = pl.program_id(0)
    saves = [pltpu.make_async_copy(q, q_hbm, sems.at[0]), pltpu.make_async_copy(kv, kv_hbm, sems.at[1])]

    @pl.when(h == 0)
    def _():
        q[...] = (nn(own[...], wqkv[:, :D]) * QUERY_FACTOR).astype(bf16)
        project_keys([own, sibling], wqkv, kv)
        safe_ref[0] = bounded(q[...], kv[:, :D]).astype(jnp.int32)
        for save in saves:
            save.start()

    attend(h, safe_ref[0] == 1, q, kv, w_out, acc_out.at[0], top_out.at[0], kv.shape[0])

    @pl.when(h == HEADS - 1)
    def _():
        for save in saves:
            save.wait()


def far_kernel(count, *refs):
    blocks = refs[:count]
    wqkv, q, acc_near, top_near, w_out, kv_hbm, att_out, inv_near, inv_far, kv, acc, top, safe_ref, sems = refs[count:]
    h = pl.program_id(0)
    save = pltpu.make_async_copy(kv, kv_hbm, sems.at[0])

    @pl.when(h == 0)
    def _():
        project_keys(blocks, wqkv, kv)
        safe_ref[0] = bounded(q[...], kv[:, :D]).astype(jnp.int32)
        save.start()

    attend(h, safe_ref[0] == 1, q, kv, w_out, acc.at[h % 2], top.at[h % 2], kv.shape[0])

    @pl.when(h % 2 == 1)
    def _():
        lower = lower_half(acc_near.shape[1:])
        values_near, sums_near = paired(acc_near[0], acc_near[1])
        values_far, sums_far = paired(acc[0], acc[1])
        taken_near = jnp.where(lower, top_near[0], top_near[1])
        taken_far = jnp.where(lower, top[0], top[1])
        most = jnp.maximum(taken_near, taken_far)
        near = jnp.exp2(taken_near - most)
        far = jnp.exp2(taken_far - most)
        inverse = 1.0 / (sums_near * near + sums_far * far)
        near, far = near * inverse, far * inverse
        att_out[...] = values_near * near + values_far * far
        inv_near[...] = near
        inv_far[...] = far

    @pl.when(h == HEADS - 1)
    def _():
        save.wait()


def slab_rows(depth, columns, parts):
    return depth * columns // parts // WIDE


def padded_rows(rows, objects):
    unit = 16 * objects
    return max(2, -(-rows // unit)) * unit


def slab_pieces(depth, each):
    lanes = math.gcd(each, WIDE)
    deep = depth * lanes // WIDE
    return [
        (i * deep, k * lanes, k * deep, i * lanes, deep, lanes)
        for i in range(each // lanes)
        for k in range(WIDE // lanes)
    ]


def slabs(out_ref, base, grad):
    parts = out_ref.shape[0]
    depth, columns = grad.shape
    each = columns // parts
    grad = grad.astype(out_ref.dtype)
    for b in range(parts):
        for to_row, to_lane, row, col, deep, lanes in slab_pieces(depth, each):
            start = b * each + col
            out_ref[b, base + to_row : base + to_row + deep, to_lane : to_lane + lanes] = grad[
                row : row + deep, start : start + lanes
            ]


def loop(total, block, body):
    if total % block:
        block = total

    def turn(i, carry):
        body(pl.ds(pl.multiple_of(i * block, block), block))
        return carry

    lax.fori_loop(0, total // block, turn, 0)


def slabs_by_rows(out_ref, base, depth, columns, make, block=256):
    parts = out_ref.shape[0]
    each = columns // parts
    if each % WIDE:
        slabs(out_ref, base, make(pl.ds(0, depth)))
        return
    block = math.gcd(depth, block)

    def put(rows):
        grad = make(rows).astype(out_ref.dtype)
        for b in range(parts):
            for i in range(each // WIDE):
                start = b * each + i * WIDE
                at = pl.ds(pl.multiple_of(base + i * depth + rows.start, 16), block)
                out_ref[b, at, :] = grad[:, start : start + WIDE]

    loop(depth, block, put)


def clear_tail(out_ref, used):
    if used < out_ref.shape[1]:
        rest = out_ref.shape[1] - used
        out_ref[:, used:, :] = jnp.zeros((out_ref.shape[0], rest, WIDE), out_ref.dtype)


def mlp_kernel(
    self_att, after_one, wo, gain, bias, mod, up_hbm, cot_hbm, down_hbm, near_hbm, far_hbm,
    mixed, grad_two, do_near, x_near, do_far, x_far, modes, g_hbm,
    up, cotangent, down, inv_near, inv_far, g_out, two, final, norm_grad, third_in, active, hidden_grad,
    fetch_sems, save_sems,
):
    fetches = [
        Fetch([pair], fetch_sems.at[pl.ds(i, 1)])
        for i, pair in enumerate(
            [(up_hbm, up), (cot_hbm, cotangent), (down_hbm, down), (near_hbm, inv_near), (far_hbm, inv_far)]
        )
    ]
    for fetch in fetches:
        fetch.start()
    count = self_att.shape[0]
    ff = up.shape[1]
    parts = g_out.shape[0]
    rows3 = norm_rows(gain, bias, mod, 2)
    up_base = slab_rows(D, D, parts)
    down_base = up_base + slab_rows(D, ff, parts)

    def start(rows):
        value = after_one[rows, :] + nn(self_att[rows, :].astype(bf16), wo[...])
        two[rows, :] = value
        final[rows, :] = value
        third_in[rows, :] = modulate(value, *rows3).astype(bf16)
        norm_grad[rows, :] = jnp.zeros_like(value)

    loop(count, 384, start)
    for fetch in fetches[:3]:
        fetch.wait()
    step = active.shape[1]

    def columns_of(f, dynamic):
        cols = pl.ds(pl.multiple_of(f, step), step) if dynamic else slice(f, f + step)

        def rows_of(rows):
            hidden = nn(third_in[rows, :], up[:, cols])
            square = hidden * hidden
            t = jnp.tanh(GELU_A * hidden * (1.0 + GELU_B * square))
            half = 0.5 * (1.0 + t)
            low = (hidden * half).astype(bf16)
            slope = half + 0.5 * hidden * (1.0 - t * t) * (GELU_A * (1.0 + 3.0 * GELU_B * square))
            low_grad = (nt(cotangent[rows, :], down[cols, :]) * slope).astype(bf16)
            active[rows, :] = low
            hidden_grad[rows, :] = low_grad
            final[rows, :] += nn(low, down[cols, :])
            norm_grad[rows, :] += nt(low_grad, up[:, cols])

        loop(count, 768, rows_of)
        up_part = tn(third_in[...], hidden_grad[...]).astype(bf16)
        down_part = tn(active[...], cotangent[...]).astype(bf16)
        each = ff // parts
        for i in range(step // WIDE):
            col = f + i * WIDE
            base = up_base + col % each // WIDE * D
            at = pl.ds(pl.multiple_of(base, 16), D) if dynamic else slice(base, base + D)
            g_out[col // each, at, :] = up_part[:, i * WIDE : (i + 1) * WIDE]
        each = D // parts
        if dynamic:
            for b in range(parts):
                for i in range(each // WIDE):
                    start = b * each + i * WIDE
                    at = pl.ds(pl.multiple_of(down_base + i * ff + f, 16), step)
                    g_out[b, at, :] = down_part[:, start : start + WIDE]
            return
        for to_row, to_lane, row, col, deep, lanes in slab_pieces(ff, each):
            if row <= f < row + deep:
                at = down_base + to_row + f - row
                for b in range(parts):
                    g_out[b, at : at + step, to_lane : to_lane + lanes] = down_part[
                        :, b * each + col : b * each + col + lanes
                    ]

    if D // parts % WIDE == 0:
        def turn(i, carry):
            columns_of(i * step, True)
            return carry

        lax.fori_loop(0, ff // step, turn, 0)
    else:
        for f in range(0, ff, step):
            columns_of(f, False)
    clear_tail(g_out, down_base + slab_rows(ff, D, parts))
    saves = [
        pltpu.make_async_copy(g_out.at[:, rows], g_hbm.at[:, rows], save_sems.at[i])
        for i, rows in enumerate((slice(up_base, g_out.shape[1]), slice(0, up_base)))
    ]
    saves[0].start()
    for fetch in fetches[3:]:
        fetch.wait()
    modes[...] = jnp.zeros_like(modes)
    self_grad = third_in

    def end(rows):
        mixed[rows, :] = final[rows, :].astype(bf16)
        back, sums = modulate_back(norm_grad[rows, :], two[rows, :], rows3[0], rows3[1], rows3[3])
        modes[...] += sums
        grad = cotangent[rows, :].astype(f32) + back
        grad_two[rows, :] = grad
        low = grad.astype(bf16)
        self_grad[rows, :] = low
        att_grad = nt(low, wo[...])
        for inv, do_out, x_out in ((inv_near, do_near, x_near), (inv_far, do_far, x_far)):
            do = (att_grad * inv[rows, :]).astype(bf16)
            do_out[rows, :] = do
            x_out[rows, :] = delta_lanes(do.astype(f32) * self_att[rows, :])

    loop(count, 384, end)
    slabs_by_rows(g_out, 0, D, D, lambda rows: tn(self_att[:, rows].astype(bf16), self_grad[...]))
    saves[1].start()
    for save in saves:
        save.wait()


def project_back(dkvt, wqkv, part_out):
    count, rows, _ = part_out.shape
    for b in range(count):
        part = nn(wqkv[:, D:], dkvt[:, b * rows : (b + 1) * rows])
        part_out[b] = part.astype(bf16).T


class Mover:
    def __init__(self, send, recv):
        self.send, self.recv = send, recv
        self.copies = []
        place, obj = lax.axis_index("blk"), lax.axis_index("obj")
        self.chips = lax.axis_size("blk") // 2
        self.columns = lax.axis_size("obj") // 2
        self.core, self.chip = lax.rem(place, 2), place // 2
        self.side, self.column = lax.rem(obj, 2), obj // 2
        self.sibling = {"blk": self.chip * 2 + 1 - self.core}
        self.chip_ids = [lax.rem(self.chip + d, self.chips) for d in range(1, self.chips)]
        self.chip_peers = [{"blk": c * 2 + self.core} for c in self.chip_ids]
        self.across = {"obj": self.column * 2 + 1 - self.side}
        objects = lax.axis_size("obj")
        self.obj = obj
        self.object_ids = [lax.rem(obj + d, objects) for d in range(1, objects)]
        self.object_peers = [{"obj": o} for o in self.object_ids]
        self.column_ids = [lax.rem(self.column + d, self.columns) for d in range(1, self.columns)]
        self.column_peers = [{"obj": c * 2 + self.side} for c in self.column_ids]

    def barrier(self, all_objects=False):
        everyone = [self.sibling] + self.chip_peers
        everyone += self.object_peers if all_objects else [self.across] + self.column_peers
        semaphore = pltpu.get_barrier_semaphore()
        for target in everyone:
            pl.semaphore_signal(semaphore, inc=1, device_id=target, device_id_type=pl.DeviceIdType.MESH)
        pl.semaphore_wait(semaphore, len(everyone))

    def copy(self, src, dst, target):
        at = len(self.copies)
        made = pltpu.make_async_remote_copy(
            src_ref=src, dst_ref=dst, send_sem=self.send.at[at], recv_sem=self.recv.at[at],
            device_id=target, device_id_type=pl.DeviceIdType.MESH,
        )
        self.copies.append(made)
        return made

    def drain(self):
        for made in self.copies:
            made.wait_send()


def begin(copies):
    for made in copies:
        made.start()


def arrive(copies):
    for made in copies:
        made.wait_recv()


def added(*values):
    total = values[0].astype(f32)
    for value in values[1:]:
        total = total + value.astype(f32)
    return total.astype(bf16)


def cut(rows, objects):
    unit = 16 * objects
    first = (rows // unit + 1) // 2 * unit
    return first, rows - first


class Gather:
    @staticmethod
    def scratch(chips, rows, objects, lanes):
        first, second = cut(rows, objects)
        return [
            VMEM((chips, rows, lanes), bf16),
            VMEM((max(chips - 1, 1), first, lanes), bf16), VMEM((2, first // 2, lanes), bf16), VMEM((first // 2, lanes), bf16),
            VMEM((chips, second // 2, lanes), bf16), VMEM((chips, second // 2, lanes), bf16),
            VMEM((max(chips - 1, 1), second // 2, lanes), bf16),
        ]

    @staticmethod
    def copies(chips):
        return 2 * chips + 2 * (chips - 1) + 1 + chips

    def __init__(self, mover, g, scratch, out_first, out_second):
        self.mover, self.g = mover, g
        self.mine, self.far0, self.flat0, self.across0, self.across1, self.mine1, self.far1 = scratch
        self.out0, self.out1 = out_first, out_second
        first, half1 = self.far0.shape[1], self.mine1.shape[1]
        m, chips = mover, mover.chips
        self.rows = (slice(0, first), slice(first, first + 2 * half1))
        other = 1 - m.core
        self.core = [
            [m.copy(g.at[2 * j + other, rows], self.mine.at[j, rows], m.sibling) for j in range(chips)]
            for rows in self.rows
        ]
        self.chip0 = [
            m.copy(self.mine.at[c, self.rows[0]], self.far0.at[d], peer)
            for d, (c, peer) in enumerate(zip(m.chip_ids, m.chip_peers))
        ]
        self.side0 = [m.copy(self.flat0.at[1 - m.side], self.across0, m.across)]
        away = pl.ds(pl.multiple_of(first + (1 - m.side) * half1, 16), half1)
        self.kept = pl.ds(pl.multiple_of(first + m.side * half1, 16), half1)
        self.side1 = [m.copy(self.mine.at[j, away], self.across1.at[j], m.across) for j in range(chips)]
        self.chip1 = [
            m.copy(self.mine1.at[c], self.far1.at[d], peer)
            for d, (c, peer) in enumerate(zip(m.chip_ids, m.chip_peers))
        ]

    def step0(self):
        begin(self.core[0] + self.core[1])

    def step1(self):
        for group, after in ((0, self.chip0), (1, self.side1)):
            arrive(self.core[group])
            rows = self.rows[group]
            for j in range(self.mover.chips):
                self.mine[j, rows] = added(self.g[2 * j + self.mover.core, rows], self.mine[j, rows])
            begin(after)

    def step2(self):
        m = self.mover
        arrive(self.chip0)
        total = added(self.mine[m.chip, self.rows[0]], *[self.far0[d] for d in range(m.chips - 1)])
        self.flat0[...] = total.reshape(self.flat0.shape)
        begin(self.side0)
        arrive(self.side1)
        for j in range(m.chips):
            self.mine1[j] = added(self.mine[j, self.kept], self.across1[j])
        begin(self.chip1)

    def step3(self):
        m = self.mover
        arrive(self.side0)
        self.out0[...] = added(self.flat0[m.side], self.across0[...])
        arrive(self.chip1)
        self.out1[...] = added(self.mine1[m.chip], *[self.far1[d] for d in range(m.chips - 1)])


class Spread:
    @staticmethod
    def scratch(objects, half, lanes):
        columns = objects // 2
        return VMEM((max(columns - 1, 1), half // columns, lanes), bf16)

    @staticmethod
    def copies(objects):
        return 2 * (objects // 2 - 1)

    def __init__(self, mover, half, taken, out):
        m = mover
        self.mover, self.half, self.taken, self.out = mover, half, taken, out
        piece = taken.shape[1]
        self.piece = pl.ds(pl.multiple_of(m.column * piece, 16), piece)
        self.sums = [
            m.copy(half.at[pl.ds(pl.multiple_of(c * piece, 16), piece)], taken.at[d], peer)
            for d, (c, peer) in enumerate(zip(m.column_ids, m.column_peers))
        ]
        own = out.at[m.column]
        self.shares = [m.copy(own, own, peer) for peer in m.column_peers]

    def step0(self):
        begin(self.sums)

    def step1(self):
        arrive(self.sums)
        m = self.mover
        self.out[m.column] = added(self.half[self.piece], *[self.taken[d] for d in range(m.columns - 1)])
        begin(self.shares)

    def step2(self):
        arrive(self.shares)


class Cross:
    def __init__(self, mover, own, other):
        self.own, self.other = own, other
        self.copies = [mover.copy(own, other, mover.across)]

    def start(self):
        begin(self.copies)

    def wait(self):
        arrive(self.copies)


def put_sides(mover, own, other, out):
    out[mover.side] = own[...]
    out[1 - mover.side] = other[...]


class Fetch:
    def __init__(self, pairs, sems):
        self.copies = [pltpu.make_async_copy(src, dst, sems.at[i]) for i, (src, dst) in enumerate(pairs)]

    def start(self):
        begin(self.copies)

    def wait(self):
        for made in self.copies:
            made.wait()


def self_back_kernel(
    count, do_far, x_far, do_near, x_near, q, kv_far, kv_near_hbm, w_far, w_near, wqkv_hbm, g_early, *refs
):
    late_hbm = refs[: count + 2]
    (norm_grad, g_out, out0, out1, dq, dkvt_far, dkvt_near, do_far_t, do_near_t, q_t, far_parts, near_parts,
     from_sibling, chip_sums, from_chips, near_sibling, half0, half1, taken0, taken1, sums0, sums1,
     kv_near, wqkv) = refs[count + 2 : count + 26]
    late = refs[count + 26 : 2 * count + 28]
    own, sibling, blocks = late[0], late[1], late[2:]
    gather_scratch, sems, moving = refs[2 * count + 28 : -3], refs[-3], refs[-2:]
    h = pl.program_id(0)
    fetch = Fetch(list(zip((kv_near_hbm, wqkv_hbm) + tuple(late_hbm), (kv_near, wqkv) + tuple(late))), sems)
    m = Mover(*moving)
    gather = Gather(m, g_early, gather_scratch, half0, half1)
    spreads = [Spread(m, half0, taken0, sums0), Spread(m, half1, taken1, sums1)]
    chips = m.chips
    far_core = [m.copy(far_parts.at[2 * d + 1], from_sibling.at[d], m.sibling) for d in range(chips - 1)]
    back = [{"blk": lax.rem(m.chip + chips - d, chips) * 2 + m.core} for d in range(1, chips)]
    far_chip = [m.copy(chip_sums.at[d], from_chips.at[d], back[d]) for d in range(chips - 1)]
    near_core = [m.copy(near_parts.at[1], near_sibling, m.sibling)]

    @pl.when(h == 0)
    def _():
        m.barrier()
        gather.step0()
        fetch.start()
        do_far_t[...] = do_far[...].T
        q_t[...] = q[...].T
        dq[...] = jnp.zeros_like(dq)

    @pl.when(h == 1)
    def _():
        gather.step1()

    @pl.when(h == 6)
    def _():
        gather.step2()

    @pl.when(h == HEADS)
    def _():
        fetch.wait()
        project_back(dkvt_far, wqkv, far_parts)
        begin(far_core)
        gather.step3()
        for spread in spreads:
            spread.step0()
        do_near_t[...] = do_near[...].T

    @pl.when(h == HEADS + 1)
    def _():
        arrive(far_core)
        for d in range(chips - 1):
            chip_sums[d] = added(far_parts[2 * d], from_sibling[d])
        begin(far_chip)

    @pl.when(h == HEADS + 4)
    def _():
        spreads[0].step1()

    @pl.when(h == HEADS + 5)
    def _():
        spreads[1].step1()

    @pl.when(h < HEADS)
    def _():
        attend_back(h, do_far, x_far, do_far_t, q_t, kv_far, w_far, dq, dkvt_far, kv_far.shape[0], 512)

    @pl.when(h >= HEADS)
    def _():
        attend_back(h - HEADS, do_near, x_near, do_near_t, q_t, kv_near, w_near, dq, dkvt_near, kv_near.shape[0], 512)

    @pl.when(h == 2 * HEADS - 1)
    def _():
        project_back(dkvt_near, wqkv, near_parts)
        begin(near_core)
        dq_low = dq[...].astype(bf16)
        rows = own.shape[0]
        grad = nn(dkvt_near[:, :rows], own[...]) + nn(dkvt_near[:, rows:], sibling[...])
        for i, block in enumerate(blocks):
            grad = grad + nn(dkvt_far[:, i * rows : (i + 1) * rows], block[...])
        slabs(g_out, 0, jnp.concatenate([tn(own[...], dq_low), grad.T], 1))
        clear_tail(g_out, slab_rows(D, 3 * D, g_out.shape[0]))
        total = nt(dq_low, wqkv[:, :D]) + near_parts[0].astype(f32)
        arrive(far_chip)
        for d in range(chips - 1):
            total = total + from_chips[d].astype(f32)
        arrive(near_core)
        norm_grad[...] = total + near_sibling[...].astype(f32)
        for spread, out in zip(spreads, (out0, out1)):
            spread.step2()
            out[...] = spread.out[...]
        m.drain()


class Job:
    @staticmethod
    def scratch(chips, rows, objects, lanes):
        made = [VMEM((chips, rows, lanes), bf16), VMEM((max(chips - 1, 1), rows, lanes), bf16)]
        for n in cut(rows, objects):
            piece = n // objects
            made += [
                VMEM((objects, piece, lanes), bf16), VMEM((objects - 1, piece, lanes), bf16),
                VMEM((objects, piece, lanes), bf16),
            ]
        return made

    @staticmethod
    def copies(chips, objects):
        return 2 * (2 * chips - 1 + 2 * (objects - 1))

    def __init__(self, mover, g, scratch):
        m = mover
        self.mover, self.g = m, g
        self.mine, self.far = scratch[:2]
        self.groups = []
        start = 0
        for shard, taken, sums in (scratch[2:5], scratch[5:8]):
            objects, piece, _ = shard.shape
            rows = slice(start, start + objects * piece)
            start += objects * piece
            core = [m.copy(g.at[2 * j + 1 - m.core, rows], self.mine.at[j, rows], m.sibling) for j in range(m.chips)]
            chip = [
                m.copy(self.mine.at[c, rows], self.far.at[d, rows], peer)
                for d, (c, peer) in enumerate(zip(m.chip_ids, m.chip_peers))
            ]
            pieces = [
                m.copy(shard.at[o], taken.at[d], peer) for d, (o, peer) in enumerate(zip(m.object_ids, m.object_peers))
            ]
            shares = [m.copy(sums.at[m.obj], sums.at[m.obj], peer) for peer in m.object_peers]
            self.groups.append((rows, shard, taken, sums, core, chip, pieces, shares))

    def step0(self):
        for group in self.groups:
            begin(group[4])

    def step1(self):
        m = self.mover
        for rows, _, _, _, core, chip, _, _ in self.groups:
            arrive(core)
            for j in range(m.chips):
                self.mine[j, rows] = added(self.g[2 * j + m.core, rows], self.mine[j, rows])
            begin(chip)

    def step2(self):
        m = self.mover
        for rows, shard, _, _, _, chip, pieces, _ in self.groups:
            arrive(chip)
            total = added(self.mine[m.chip, rows], *[self.far[d, rows] for d in range(m.chips - 1)])
            shard[...] = total.reshape(shard.shape)
            begin(pieces)

    def step3(self):
        m = self.mover
        for _, shard, taken, sums, _, _, pieces, shares in self.groups:
            arrive(pieces)
            sums[m.obj] = added(shard[m.obj], *[taken[d] for d in range(taken.shape[0])])
            begin(shares)

    def finish(self, outs):
        for group, out in zip(self.groups, outs):
            arrive(group[7])
            out[...] = group[3][...]


def cross_back_kernel(
    context_count, norm_grad, grad_two, after_one, tokens, context, q, pair, w, att, inv,
    wq, wkv, wo, gain, bias, mod, g_middle, modes_three, lifted, own0, own1,
    tokens_grad, ctx_result, small_result, early0, early1, mid0, mid1, out0, out1, late0, late1,
    dkvt, do, x, do_t, q_t, dq, g_out, g_late, small, ctx,
    ctx_half, ctx_mine, ctx_far, small_half, small_mine, small_far, ctx_out, small_out, other0, other1, *rest
):
    h = pl.program_id(0)
    m = Mover(*rest[-2:])
    chips = m.chips
    middle = Job(m, g_middle, rest[0:8])
    outer = Job(m, g_out, rest[8:16])
    late = Job(m, g_late, rest[16:24])
    early = [Cross(m, own0, other0), Cross(m, own1, other1)]
    ctx_rows = ctx.shape[0] // 2
    ctx_own = pl.ds(pl.multiple_of(m.core * ctx_rows, 16), ctx_rows)
    ctx_other = pl.ds(pl.multiple_of((1 - m.core) * ctx_rows, 16), ctx_rows)
    ctx_core = [m.copy(ctx.at[ctx_other], ctx_half, m.sibling)]
    ctx_chip = [m.copy(ctx_mine, ctx_far.at[d], m.chip_peers[d]) for d in range(chips - 1)]
    ctx_back = [m.copy(ctx_out.at[ctx_own], ctx_out.at[ctx_own], m.sibling)]
    small_core = [m.copy(small, small_half, m.sibling)]
    small_chip = [m.copy(small_mine, small_far.at[d], m.chip_peers[d]) for d in range(chips - 1)]
    small_share = [m.copy(small_out.at[m.obj], small_out.at[m.obj], peer) for peer in m.object_peers]
    late_base = slab_rows(D, D, g_late.shape[0])

    @pl.when(h == 0)
    def _():
        m.barrier(True)
        middle.step0()
        rows = norm_rows(gain, bias, mod, 1)
        back, sums = modulate_back(norm_grad[...], after_one[...], rows[0], rows[1], rows[3])
        grad_one = grad_two[...] + back
        tokens_grad[...] = grad_one
        small[4:8, :] = sums
        small[8:12, :] = modes_three[...]
        small[12:14, :] = lifted[...]
        small[14:16, :] = jnp.zeros((2, D), f32)
        cross_grad = grad_one.astype(bf16)
        middle.step1()
        slabs(g_out, 0, tn(att[...].astype(bf16), cross_grad))
        clear_tail(g_out, slab_rows(D, D, g_out.shape[0]))
        outer.step0()
        do[...] = (nt(cross_grad, wo[...]) * inv[...]).astype(bf16)
        x[...] = delta_lanes(do[...].astype(f32) * att[...])
        do_t[...] = do[...].T
        q_t[...] = q[...].T
        dq[...] = jnp.zeros_like(dq)

    @pl.when(h == 1)
    def _():
        outer.step1()

    @pl.when(h == 3)
    def _():
        middle.step2()

    @pl.when(h == 4)
    def _():
        outer.step2()
        for cross in early:
            cross.start()

    @pl.when(h == 7)
    def _():
        middle.step3()

    attend_back(h, do, x, do_t, q_t, pair, w, dq, dkvt, context_count, pair.shape[0])

    @pl.when(h == HEADS - 1)
    def _():
        dq_low = dq[...].astype(bf16)
        first = tokens[...].astype(f32)
        rows = norm_rows(gain, bias, mod, 0)
        first_in = modulate(first, *rows).astype(bf16)
        slabs(g_late, 0, tn(first_in, dq_low))
        real = lax.broadcasted_iota(jnp.int32, dkvt.shape, 1) < context_count
        kept = jnp.where(real, dkvt[...], jnp.zeros_like(dkvt))
        slabs(g_late, late_base, nn(kept, context[...]).T)
        clear_tail(g_late, late_base + slab_rows(context.shape[1], 2 * D, g_late.shape[0]))
        late.step0()
        ctx[...] = tn(dkvt[...], wkv[...].T).astype(bf16)
        begin(ctx_core)
        late.step1()
        outer.step3()
        back, sums = modulate_back(nt(dq_low, wq[...]), first, rows[0], rows[1], rows[3])
        small[0:4, :] = sums
        begin(small_core)
        arrive(ctx_core)
        ctx_mine[...] = added(ctx[ctx_own], ctx_half[...])
        begin(ctx_chip)
        arrive(small_core)
        small_mine[...] = small[...] + small_half[...]
        begin(small_chip)
        late.step2()
        tokens_grad[...] = tokens_grad[...] + back
        arrive(small_chip)
        total = small_mine[...]
        for d in range(chips - 1):
            total = total + small_far[d]
        small_out[m.obj] = total
        begin(small_share)
        for cross, own, out in zip(early, (own0, own1), (early0, early1)):
            cross.wait()
            put_sides(m, own, cross.other, out)
        arrive(ctx_chip)
        ctx_out[ctx_own] = added(ctx_mine[...], *[ctx_far[d] for d in range(chips - 1)])
        begin(ctx_back)
        middle.finish((mid0, mid1))
        late.step3()
        outer.finish((out0, out1))
        arrive(ctx_back)
        ctx_result[...] = ctx_out[...]
        arrive(small_share)
        small_result[...] = small_out[...]
        late.finish((late0, late1))
        m.drain()


def finish_kernel(parts, early0, early1, mid0, mid1, out0, out1, late0, late1, small, so, up, down, qkv, co, cq, ckv, gains, biases, modw, modb, mode):
    place = lax.axis_index("blk")
    objects = small.shape[0]
    width = 2 * D // parts
    each = D // parts

    def put(out, total, base):
        depth, columns = out.shape
        for to_row, to_lane, row, col, deep, lanes in slab_pieces(depth, columns):
            out[row : row + deep, col : col + lanes] = total[
                base + to_row : base + to_row + deep, to_lane : to_lane + lanes
            ].astype(f32)
        return base + slab_rows(depth, columns, 1)

    early = jnp.concatenate([early0[...], early1[...]], 0)
    base = put(so, early, 0)
    base = put(up, early, base)
    put(down, early, base)
    put(qkv, jnp.concatenate([mid0[...], mid1[...]], 0), 0)
    put(co, jnp.concatenate([out0[...], out1[...]], 0), 0)
    late = jnp.concatenate([late0[...], late1[...]], 0)
    base = put(cq, late, 0)
    put(ckv, late, base)
    lifted = jnp.concatenate([small[:, 12, :], small[:, 13, :]], 1)
    summed = jnp.sum(small[...], 0)
    for b in range(parts):
        @pl.when(place == b)
        def _():
            row, col = b * width // D, b * width % D
            for j in range(3):
                mode[j] = small[:, 4 * j + row, col : col + width]
                gains[j : j + 1, :] = summed[4 * j + 2 : 4 * j + 3, b * each : (b + 1) * each]
                biases[j : j + 1, :] = summed[4 * j + 3 : 4 * j + 4, b * each : (b + 1) * each]
    for j in range(3):
        modw[j] = lax.dot_general(
            lifted, mode[j], (((0,), (0,)), ((), ())), precision=lax.Precision.HIGHEST, preferred_element_type=f32
        )
        modb[j : j + 1, :] = jnp.sum(mode[j], 0, keepdims=True)


def shape(dims, dtype):
    return jax.ShapeDtypeStruct(tuple(dims), dtype)


def body(
    tokens, context, camera_groups, camera_table, cross_query, cross_kv, cross_out, self_qkv,
    self_out, mlp_up, mlp_down, norm_gain, norm_bias, mod_weight, mod_bias, cotangent,
):
    parts = lax.axis_size("blk")
    tokens = tokens[0]
    cotangent = cotangent[0]
    context_count = context.shape[1]
    rows = tokens.shape[0]
    length = rows * parts
    ff = mlp_up.shape[1]
    cam_width = mod_weight.shape[1]
    ctx_width = context.shape[2]
    padded = -(-context_count // 128) * 128
    context_rows = jnp.pad(context[0], ((0, padded - context_count), (0, 0)), mode="edge")

    picked = (
        camera_groups[:, None] == jnp.arange(camera_table.shape[0], dtype=jnp.int32)[None, :]
    ).astype(bf16)
    camera = jnp.dot(picked, camera_table, preferred_element_type=f32)
    lifted = jax.nn.silu(camera).astype(bf16)
    mod = (
        jnp.einsum("oc,jcm->ojm", lifted, mod_weight, preferred_element_type=f32)
        + mod_bias.astype(f32)
    )[0]

    def near_hop(block):
        return lax.ppermute(block, "blk", [(i, i ^ 1) for i in range(parts)])

    def chip_hop(block, distance):
        route = [(i, (i // 2 + distance) % chips * 2 + i % 2) for i in range(parts)]
        return lax.ppermute(block, "blk", route)

    chips = parts // 2
    objects = lax.axis_size("obj")
    full = lambda *dims: pl.BlockSpec(dims, lambda h: (0,) * len(dims))
    head = lambda keys: pl.BlockSpec((1, rows, keys), lambda h: (h, 0, 0))
    row_full = full(rows, D)
    row_f32, row_bf16 = shape((rows, D), f32), shape((rows, D), bf16)
    two_heads = VMEM((2, rows, WIDE), f32)
    flag = pltpu.SMEM((1,), jnp.int32)
    anywhere = pl.BlockSpec(memory_space=pl.ANY)
    pair_block = pl.BlockSpec((rows, WIDE), lambda h: (0, h // 2))
    head_block = pl.BlockSpec((1, rows, WIDE), lambda h: (h, 0, 0))
    heads_block = pl.BlockSpec((2, rows, WIDE), lambda h: (h // 2, 0, 0))
    sums_f32 = shape((HEADS, rows, WIDE), f32)
    transposed = [VMEM((D, rows), bf16), VMEM((D, rows), bf16)]
    norm_full = [full(3, D), full(3, D), full(3, 2 * D)]

    def call(kernel, name, us, outs, ins, out_specs, scratch=(), collective_id=None, **more):
        return pl.pallas_call(
            kernel, name=name, out_shape=outs, in_specs=ins, out_specs=out_specs, scratch_shapes=list(scratch),
            cost_estimate=pl.CostEstimate(flops=int(us * 1.1e9), bytes_accessed=int(us * 3.6e6), transcendentals=0),
            compiler_params=params() if collective_id is None else pltpu.CompilerParams(
                vmem_limit_bytes=62 * MIB, collective_id=collective_id, has_side_effects=True
            ), **more,
        )

    second_in, after_one, cross_q, cross_pair, cross_w, cross_att, cross_inv = call(
        functools.partial(cross_kernel, context_count), "cross_forward", 15,
        [row_bf16, row_f32, row_bf16, shape((padded, 2 * D), bf16), shape((HEADS, rows, padded), bf16), row_f32, row_f32],
        [row_full, full(padded, ctx_width), full(D, D), full(ctx_width, 2 * D), full(D, D)] + norm_full,
        [row_full, row_full, anywhere, anywhere, head(padded), pair_block, pair_block],
        [VMEM((rows, D), bf16), VMEM((padded, 2 * D), bf16), VMEM((rows, D), bf16), two_heads, flag,
         pltpu.SemaphoreType.DMA((2,))], grid=(HEADS,),
    )(tokens, context_rows, cross_query, cross_kv, cross_out, norm_gain, norm_bias, mod)

    sibling_in = near_hop(second_in)
    to_chips, sibling_in = lax.optimization_barrier((second_in, sibling_in))
    chip_in = [chip_hop(to_chips, d) for d in range(1, chips)]
    near_keys, far_keys = 2 * rows, 2 * rows * (chips - 1)
    near_w, self_q, near_kv, near_acc, near_top = call(
        near_kernel, "near_forward", 16,
        [shape((HEADS, rows, near_keys), bf16), row_bf16, shape((near_keys, 2 * D), bf16), sums_f32, sums_f32],
        [row_full, row_full, full(D, 3 * D)],
        [head(near_keys), anywhere, anywhere, head_block, head_block],
        [VMEM((rows, D), bf16), VMEM((near_keys, 2 * D), bf16), flag, pltpu.SemaphoreType.DMA((2,))], grid=(HEADS,),
    )(second_in, sibling_in, self_qkv)
    chip_in, near_kv = lax.optimization_barrier((chip_in, near_kv))
    far_in = []
    for block in chip_in:
        far_in += [block, near_hop(block)]
    count = len(far_in)
    far_w, far_kv, self_att, near_inv, far_inv = call(
        functools.partial(far_kernel, count), "far_forward", 16,
        [shape((HEADS, rows, far_keys), bf16), shape((far_keys, 2 * D), bf16), row_f32, row_f32, row_f32],
        [row_full] * count + [full(D, 3 * D), row_full, heads_block, heads_block],
        [head(far_keys), anywhere, pair_block, pair_block, pair_block],
        [VMEM((far_keys, 2 * D), bf16), two_heads, two_heads, flag, pltpu.SemaphoreType.DMA((1,))], grid=(HEADS,),
    )(*far_in, self_qkv, self_q, near_acc, near_top)

    lanes = WIDE
    tall = lambda columns, depth: slab_rows(depth, columns, parts)
    early = padded_rows(tall(D, D) + tall(ff, D) + tall(D, ff), objects)
    mixed, grad_two, near_do, near_x, far_do, far_x, modes_three, g_early = call(
        mlp_kernel, "feed_forward", 20,
        [row_bf16, row_f32, row_bf16, row_bf16, row_bf16, row_bf16, shape((4, D), f32), shape((parts, early, lanes), bf16)],
        [whole()] * 6 + [anywhere] * 5, [whole()] * 7 + [anywhere],
        [VMEM((D, ff), bf16), VMEM((rows, D), bf16), VMEM((ff, D), bf16), VMEM((rows, D), f32), VMEM((rows, D), f32),
         VMEM((parts, early, lanes), bf16), VMEM((rows, D), f32), VMEM((rows, D), f32), VMEM((rows, D), f32),
         VMEM((rows, D), bf16), VMEM((rows, 512), bf16), VMEM((rows, 512), bf16),
         pltpu.SemaphoreType.DMA((5,)), pltpu.SemaphoreType.DMA((2,))],
    )(self_att, after_one, self_out, norm_gain, norm_bias, mod, mlp_up, cotangent, mlp_down, near_inv, far_inv)

    unit = objects // 2
    moving = lambda copies: [pltpu.SemaphoreType.DMA((copies,)), pltpu.SemaphoreType.DMA((copies,))]
    halves = lambda rows: [shape((n // 2, lanes), bf16) for n in cut(rows, objects)]
    half_vmem = lambda rows: [VMEM((n // 2, lanes), bf16) for n in cut(rows, objects)]
    spread_outs = lambda rows: [shape((2, unit, n // objects, lanes), bf16) for n in cut(rows, objects)]
    own_outs = lambda rows: [shape((unit, n // objects, lanes), bf16) for n in cut(rows, objects)]
    taken = lambda rows: [Spread.scratch(objects, n // 2, lanes) for n in cut(rows, objects)]
    in_vmem = lambda shapes: [VMEM(item.shape, item.dtype) for item in shapes]
    once = lambda *dims: pl.BlockSpec(dims, lambda h: (0,) * len(dims), pipeline_mode=pl.Buffered(1))
    like = lambda shapes: [once(*item.shape) for item in shapes]
    row_once = once(rows, D)

    middle = padded_rows(tall(3 * D, D), objects)
    own_shapes = own_outs(early)
    hops = VMEM((chips - 1, rows, D), bf16)
    row_vmem = VMEM((rows, D), bf16)
    norm_grad, g_middle, own0, own1 = call(
        functools.partial(self_back_kernel, count), "self_backward", 60,
        [row_f32, shape((parts, middle, lanes), bf16)] + own_shapes,
        [row_once] * 5 + [once(far_keys, 2 * D), anywhere,
         pl.BlockSpec((1, rows, far_keys), lambda h: (jnp.minimum(h, HEADS - 1), 0, 0)),
         pl.BlockSpec((1, rows, near_keys), lambda h: (jnp.maximum(h - HEADS, 0), 0, 0)),
         anywhere, once(parts, early, lanes)] + [anywhere] * (2 + count),
        [row_once, once(parts, middle, lanes)] + like(own_shapes),
        [VMEM((rows, D), f32), VMEM((2 * D, far_keys), bf16), VMEM((2 * D, near_keys), bf16)]
        + [VMEM((D, rows), bf16)] * 3 + [VMEM((count, rows, D), bf16), VMEM((2, rows, D), bf16)]
        + [hops, hops, hops, row_vmem] + half_vmem(early) + taken(early) + in_vmem(own_shapes)
        + [VMEM((near_keys, 2 * D), bf16), VMEM((D, 3 * D), bf16)] + [row_vmem] * (2 + count)
        + Gather.scratch(chips, early, objects, lanes) + [pltpu.SemaphoreType.DMA((count + 4,))]
        + moving(Gather.copies(chips) + 2 * (chips - 1) + 1 + 2 * Spread.copies(objects)),
        grid=(2 * HEADS,), collective_id=1,
    )(far_do, far_x, near_do, near_x, self_q, far_kv, near_kv, far_w, near_w, self_qkv, g_early,
      second_in, sibling_in, *far_in)

    outer = padded_rows(tall(D, D), objects)
    late = padded_rows(tall(D, D) + tall(2 * D, ctx_width), objects)
    lifted_rows = lifted.astype(f32).reshape(2, D) * (1.0 / parts)
    sums = spread_outs(early) + [
        shape((objects, n // objects, lanes), bf16) for total in (middle, outer, late) for n in cut(total, objects)
    ]
    ctx_half = VMEM((padded // 2, ctx_width), bf16)
    small_vmem = VMEM((16, D), f32)
    tokens_grad, context_sum, small_all, *sums = call(
        functools.partial(cross_back_kernel, context_count), "cross_backward", 20,
        [row_f32, shape((padded, ctx_width), bf16), shape((objects, 16, D), f32)] + sums,
        [row_once] * 4 + [once(padded, ctx_width), row_once, once(padded, 2 * D), head(padded), row_once, row_once,
         once(D, D), once(ctx_width, 2 * D), once(D, D)] + norm_full + [once(parts, middle, lanes), full(4, D), full(2, D)]
        + like(own_shapes),
        [row_once, once(padded, ctx_width), once(objects, 16, D)] + like(sums),
        [VMEM((2 * D, padded), bf16), row_vmem, row_vmem] + transposed + [VMEM((rows, D), f32)]
        + [VMEM((parts, outer, lanes), bf16), VMEM((parts, late, lanes), bf16), small_vmem, VMEM((padded, ctx_width), bf16)]
        + [ctx_half, ctx_half, VMEM((chips - 1, padded // 2, ctx_width), bf16)]
        + [small_vmem, small_vmem, VMEM((chips - 1, 16, D), f32)]
        + [VMEM((padded, ctx_width), bf16), VMEM((objects, 16, D), f32)] + in_vmem(own_shapes)
        + Job.scratch(chips, middle, objects, lanes) + Job.scratch(chips, outer, objects, lanes)
        + Job.scratch(chips, late, objects, lanes)
        + moving(3 * Job.copies(chips, objects) + 2 + chips + 1 + chips + objects - 1),
        grid=(HEADS,), collective_id=2,
    )(
        norm_grad, grad_two, after_one, tokens, context_rows, cross_q, cross_pair, cross_w,
        cross_att, cross_inv, cross_query, cross_kv, cross_out, norm_gain, norm_bias, mod, g_middle, modes_three,
        lifted_rows, own0, own1,
    )
    context_grad = context_sum[:context_count].astype(f32)

    width = 2 * D // parts
    grads = lambda depth, columns: shape((depth, columns // parts), f32)
    so, up, down, qkv, co, cq, ckv, gains, biases, modw, modb = pl.pallas_call(
        functools.partial(finish_kernel, parts),
        name="finish",
        out_shape=[
            grads(D, D), grads(D, ff), grads(ff, D), grads(D, 3 * D), grads(D, D), grads(D, D), grads(ctx_width, 2 * D),
            grads(3, D), grads(3, D), shape((3, cam_width, width), f32), grads(3, 2 * D),
        ],
        in_specs=[whole()] * 9,
        out_specs=[whole()] * 11,
        scratch_shapes=[VMEM((3, objects, width), f32)],
        compiler_params=params(),
    )(*[v.reshape(-1, lanes) for v in sums], small_all)
    return (
        mixed[None], tokens_grad[None], context_grad[None], cq, ckv, co, qkv, so, up, down, gains, biases, modw, modb,
    )


def solution(mesh):
    rows = P("obj", "blk", None)
    columns = P(None, "blk")
    return jax.shard_map(
        body,
        mesh=mesh,
        in_specs=(rows, P("obj", None, None), P("obj")) + (P(),) * 12 + (rows,),
        out_specs=(rows, rows, P("obj", None, None)) + (columns,) * 9
        + (P(None, None, "blk"), columns),
        check_vma=False,
    )
```

```python
import functools
import math

import jax
import jax.numpy as jnp
from jax import lax
from jax.experimental import pallas as pl
from jax.experimental.pallas import tpu as pltpu
from jax.sharding import PartitionSpec as P

D = 512
HEADS = 8
HEAD_DIM = 64
PAIRS = HEADS // 2
WIDE = 2 * HEAD_DIM
LOG2E = 1.4426950408889634
LN2 = 0.6931471805599453
QUERY_FACTOR = LOG2E * HEAD_DIM ** (-0.5)
SCORE_FACTOR = HEAD_DIM ** (-0.5)
SAFE_SQUARE = 60.0 ** 2
EPSILON = 1e-06
GELU_A = 0.7978845608028654
GELU_B = 0.044715
MIB = 2**20

f32 = jnp.float32
bf16 = jnp.bfloat16
VMEM = pltpu.VMEM


def nn(a, b):
    return lax.dot_general(a, b, (((1,), (0,)), ((), ())), preferred_element_type=f32)


def nt(a, b):
    return lax.dot_general(a, b, (((1,), (1,)), ((), ())), preferred_element_type=f32)


def tn(a, b):
    return lax.dot_general(a, b, (((0,), (0,)), ((), ())), preferred_element_type=f32)


def whole():
    return pl.BlockSpec(memory_space=VMEM)


def params(mib=60):
    return pltpu.CompilerParams(vmem_limit_bytes=mib * MIB)


def lower_half(shape):
    return lax.broadcasted_iota(jnp.int32, shape, 1) % WIDE < HEAD_DIM


def own_half(shape, odd):
    lower = lower_half(shape)
    return jnp.logical_not(lower) if odd else lower


def normalize(x):
    center = x - jnp.mean(x, -1, keepdims=True)
    inverse = lax.rsqrt(jnp.mean(center * center, -1, keepdims=True) + EPSILON)
    return center * inverse, inverse


def modulate(x, gain, bias, shift, scale):
    normed, _ = normalize(x)
    return (normed * gain + bias) * (1.0 + scale) + shift


def modulate_back(g, x, gain, bias, scale):
    normed, inverse = normalize(x)
    affine = normed * gain + bias
    shift_grad = jnp.sum(g, 0, keepdims=True)
    scale_grad = jnp.sum(g * affine, 0, keepdims=True)
    a = g * (1.0 + scale)
    gain_grad = jnp.sum(a * normed, 0, keepdims=True)
    bias_grad = jnp.sum(a, 0, keepdims=True)
    n = a * gain
    back = inverse * (
        n - jnp.mean(n, -1, keepdims=True) - normed * jnp.mean(n * normed, -1, keepdims=True)
    )
    return back, jnp.concatenate([shift_grad, scale_grad, gain_grad, bias_grad], 0)


def norm_rows(gain_ref, bias_ref, mod_ref, j):
    gain = gain_ref[j : j + 1, :].astype(f32)
    bias = bias_ref[j : j + 1, :].astype(f32)
    shift = mod_ref[j : j + 1, :D]
    scale = mod_ref[j : j + 1, D:]
    return gain, bias, shift, scale


def head_sums(values, sign):
    rows = lax.broadcasted_iota(jnp.int32, (WIDE, WIDE), 0)
    cols = lax.broadcasted_iota(jnp.int32, (WIDE, WIDE), 1)
    block = jnp.where((rows < HEAD_DIM) != (cols < HEAD_DIM), sign, 0.0).astype(bf16)
    high = values.astype(bf16)
    low = (values - high.astype(f32)).astype(bf16)
    return nn(high, block) + nn(low, block)


def delta_lanes(product):
    parts = []
    for p in range(PAIRS):
        total = head_sums(product[:, p * WIDE : (p + 1) * WIDE], -1.0)
        high = total.astype(bf16).astype(f32)
        low = total - high
        lane = lax.broadcasted_iota(jnp.int32, total.shape, 1) % HEAD_DIM
        parts.append(jnp.where(lane == 0, high, jnp.where(lane == 1, low, 0.0)).astype(bf16))
    return jnp.concatenate(parts, 1)


def norm_top(x):
    rows = lax.broadcasted_iota(jnp.int32, (WIDE, WIDE), 0)
    cols = lax.broadcasted_iota(jnp.int32, (WIDE, WIDE), 1)
    block = jnp.where((rows < HEAD_DIM) == (cols < HEAD_DIM), 1.0, 0.0).astype(bf16)
    top = None
    for p in range(PAIRS):
        part = x[:, p * WIDE : (p + 1) * WIDE].astype(f32)
        here = jnp.max(nn((part * part).astype(bf16), block), 0, keepdims=True)
        top = here if top is None else jnp.maximum(top, here)
    return jnp.max(top)


def bounded(q, k):
    return norm_top(q) * norm_top(k) < SAFE_SQUARE


def pair_columns(head, offset=0):
    return pl.ds(pl.multiple_of(offset + head // 2 * WIDE, WIDE), WIDE)


def head_rows(head, offset=0):
    return pl.ds(pl.multiple_of(offset + head * HEAD_DIM, HEAD_DIM), HEAD_DIM)


def owned(shape, head):
    lane = lax.broadcasted_iota(jnp.int32, shape, 1)
    return lane // HEAD_DIM == head % 2


def key_rows(kv, head):
    k = kv[:, pair_columns(head)]
    return jnp.where(owned(k.shape, head), k, jnp.zeros_like(k))


def value_rows(kv, head, real_keys):
    v = kv[:, pair_columns(head, D)]
    v = jnp.where(owned(v.shape, head), v, jnp.ones_like(v))
    if real_keys < v.shape[0]:
        row = lax.broadcasted_iota(jnp.int32, v.shape, 0)
        v = jnp.where(row < real_keys, v, jnp.zeros_like(v))
    return v


def attend(head, safe, q, kv, w_ref, acc, top, real_keys):
    count = q.shape[0]
    step = min(256, count)

    def blocks(shifted):
        k = key_rows(kv, head)
        v = value_rows(kv, head, real_keys)
        for r in range(0, count, step):
            rows = slice(r, r + step)
            s = nt(q[rows, pair_columns(head)], k)
            if shifted:
                most = jnp.max(s, -1, keepdims=True)
                s = s - most
            w = jnp.exp2(s).astype(bf16)
            w_ref[0, rows, :] = w
            acc[rows, :] = nn(w, v)
            if top is not None:
                top[rows, :] = jnp.broadcast_to(most, (step, WIDE)) if shifted else jnp.zeros((step, WIDE), f32)

    @pl.when(safe)
    def _():
        blocks(False)

    @pl.when(jnp.logical_not(safe))
    def _():
        blocks(True)


def paired(even, odd):
    lower = lower_half(even.shape)
    return jnp.where(lower, even, odd), pltpu.roll(jnp.where(lower, odd, even), HEAD_DIM, 1)


def attend_back(head, do, x, do_t, q_t, kv, w_ref, dq, dkvt, real_keys, chunk):
    left = jnp.where(owned((do.shape[0], WIDE), head), do[:, pair_columns(head)], x[:, pair_columns(head)])
    k = key_rows(kv, head)
    v = value_rows(kv, head, real_keys)
    keys = k.shape[0]
    chunk = chunk if keys % chunk == 0 else keys
    total = None
    for c in range(0, keys, chunk):
        cols = slice(c, c + chunk)
        w = w_ref[0, :, cols]
        dp = nt(left, v[cols])
        ds = (w.astype(f32) * dp).astype(bf16)
        part = nn(ds, k[cols])
        total = part if total is None else total + part
        dkvt[head_rows(head), cols] = (nn(q_t[head_rows(head), :], ds) * LN2).astype(bf16)
        dkvt[head_rows(head, D), cols] = nn(do_t[head_rows(head), :], w).astype(bf16)
    total = total * SCORE_FACTOR

    dq[:, pair_columns(head)] += total


def cross_kernel(
    context_count, tokens, context, wq, wkv, wo, gain, bias, mod,
    second_in, after_one, q_hbm, pair_hbm, w_out, att_out, inv_out, q, pair, att, acc, safe_ref, sems,
):
    h = pl.program_id(0)
    saves = [pltpu.make_async_copy(q, q_hbm, sems.at[0]), pltpu.make_async_copy(pair, pair_hbm, sems.at[1])]

    @pl.when(h == 0)
    def _():
        first_in = modulate(tokens[...].astype(f32), *norm_rows(gain, bias, mod, 0)).astype(bf16)
        q[...] = (nn(first_in, wq[...]) * QUERY_FACTOR).astype(bf16)
        pair[...] = nn(context[...], wkv[...]).astype(bf16)
        safe_ref[0] = bounded(q[...], pair[:, :D]).astype(jnp.int32)
        for save in saves:
            save.start()

    attend(h, safe_ref[0] == 1, q, pair, w_out, acc.at[h % 2], None, context_count)

    @pl.when(h % 2 == 1)
    def _():
        values, sums = paired(acc[0], acc[1])
        inverse = 1.0 / sums
        att_out[...] = values * inverse
        inv_out[...] = inverse
        att[:, pair_columns(h)] = att_out[...].astype(bf16)

    @pl.when(h == HEADS - 1)
    def _():
        one = tokens[...].astype(f32) + nn(att[...], wo[...])
        after_one[...] = one
        second_in[...] = modulate(one, *norm_rows(gain, bias, mod, 1)).astype(bf16)
        for save in saves:
            save.wait()


def project_keys(blocks, wqkv, kv):
    for i, block in enumerate(blocks):
        rows = block.shape[0]
        kv[i * rows : (i + 1) * rows, :] = nn(block[...], wqkv[:, D:]).astype(bf16)


def near_kernel(own, sibling, wqkv, w_out, q_hbm, kv_hbm, acc_out, top_out, q, kv, safe_ref, sems):
    h = pl.program_id(0)
    saves = [pltpu.make_async_copy(q, q_hbm, sems.at[0]), pltpu.make_async_copy(kv, kv_hbm, sems.at[1])]

    @pl.when(h == 0)
    def _():
        q[...] = (nn(own[...], wqkv[:, :D]) * QUERY_FACTOR).astype(bf16)
        project_keys([own, sibling], wqkv, kv)
        safe_ref[0] = bounded(q[...], kv[:, :D]).astype(jnp.int32)
        for save in saves:
            save.start()

    attend(h, safe_ref[0] == 1, q, kv, w_out, acc_out.at[0], top_out.at[0], kv.shape[0])

    @pl.when(h == HEADS - 1)
    def _():
        for save in saves:
            save.wait()


def far_kernel(count, *refs):
    blocks = refs[:count]
    (wqkv, q, acc_near, top_near, w_out, kv_hbm, blocks_hbm, att_out, inv_near, inv_far,
     kv, acc, top, safe_ref, sems) = refs[count:]
    h = pl.program_id(0)
    save = pltpu.make_async_copy(kv, kv_hbm, sems.at[count])
    keeps = [pltpu.make_async_copy(block, blocks_hbm.at[i], sems.at[i]) for i, block in enumerate(blocks)]

    @pl.when(h == 0)
    def _():
        for keep in keeps:
            keep.start()
        project_keys(blocks, wqkv, kv)
        safe_ref[0] = bounded(q[...], kv[:, :D]).astype(jnp.int32)
        save.start()

    attend(h, safe_ref[0] == 1, q, kv, w_out, acc.at[h % 2], top.at[h % 2], kv.shape[0])

    @pl.when(h % 2 == 1)
    def _():
        lower = lower_half(acc_near.shape[1:])
        values_near, sums_near = paired(acc_near[0], acc_near[1])
        values_far, sums_far = paired(acc[0], acc[1])
        taken_near = jnp.where(lower, top_near[0], top_near[1])
        taken_far = jnp.where(lower, top[0], top[1])
        most = jnp.maximum(taken_near, taken_far)
        near = jnp.exp2(taken_near - most)
        far = jnp.exp2(taken_far - most)
        inverse = 1.0 / (sums_near * near + sums_far * far)
        near, far = near * inverse, far * inverse
        att_out[...] = values_near * near + values_far * far
        inv_near[...] = near
        inv_far[...] = far

    @pl.when(h == HEADS - 1)
    def _():
        for copy in keeps + [save]:
            copy.wait()


def slab_rows(depth, columns, parts):
    return depth * columns // parts // WIDE


def padded_rows(rows, objects):
    unit = 16 * objects
    return max(2, -(-rows // unit)) * unit


def slab_pieces(depth, each):
    lanes = math.gcd(each, WIDE)
    deep = depth * lanes // WIDE
    return [
        (i * deep, k * lanes, k * deep, i * lanes, deep, lanes)
        for i in range(each // lanes)
        for k in range(WIDE // lanes)
    ]


def slabs(out_ref, base, grad):
    parts = out_ref.shape[0]
    depth, columns = grad.shape
    each = columns // parts
    grad = grad.astype(out_ref.dtype)
    for b in range(parts):
        for to_row, to_lane, row, col, deep, lanes in slab_pieces(depth, each):
            start = b * each + col
            out_ref[b, base + to_row : base + to_row + deep, to_lane : to_lane + lanes] = grad[
                row : row + deep, start : start + lanes
            ]


def loop(total, block, body):
    if total % block:
        block = total

    def turn(i, carry):
        body(pl.ds(pl.multiple_of(i * block, block), block))
        return carry

    lax.fori_loop(0, total // block, turn, 0)


def slabs_by_rows(out_ref, base, depth, columns, make, block=256):
    parts = out_ref.shape[0]
    each = columns // parts
    if each % WIDE:
        slabs(out_ref, base, make(pl.ds(0, depth)))
        return
    block = math.gcd(depth, block)

    def put(rows):
        grad = make(rows).astype(out_ref.dtype)
        for b in range(parts):
            for i in range(each // WIDE):
                start = b * each + i * WIDE
                at = pl.ds(pl.multiple_of(base + i * depth + rows.start, 16), block)
                out_ref[b, at, :] = grad[:, start : start + WIDE]

    loop(depth, block, put)


def clear_tail(out_ref, used):
    if used < out_ref.shape[1]:
        rest = out_ref.shape[1] - used
        out_ref[:, used:, :] = jnp.zeros((out_ref.shape[0], rest, WIDE), out_ref.dtype)


def mlp_kernel(
    self_att, after_one, wo, gain, bias, mod, up_hbm, cot_hbm, down_hbm, near_hbm, far_hbm,
    mixed, grad_two, do_near, x_near, do_far, x_far, modes, g_hbm,
    up, cotangent, down, inv_near, inv_far, g_out, two, final, norm_grad, third_in, active, hidden_grad,
    fetch_sems, save_sems,
):
    fetches = [
        Fetch([pair], fetch_sems.at[pl.ds(i, 1)])
        for i, pair in enumerate(
            [(up_hbm, up), (cot_hbm, cotangent), (down_hbm, down), (near_hbm, inv_near), (far_hbm, inv_far)]
        )
    ]
    for fetch in fetches:
        fetch.start()
    count = self_att.shape[0]
    ff = up.shape[1]
    parts = g_out.shape[0]
    rows3 = norm_rows(gain, bias, mod, 2)
    up_base = slab_rows(D, D, parts)
    down_base = up_base + slab_rows(D, ff, parts)

    def start(rows):
        value = after_one[rows, :] + nn(self_att[rows, :].astype(bf16), wo[...])
        two[rows, :] = value
        final[rows, :] = value
        third_in[rows, :] = modulate(value, *rows3).astype(bf16)
        norm_grad[rows, :] = jnp.zeros_like(value)

    loop(count, 384, start)
    for fetch in fetches[:3]:
        fetch.wait()
    step = active.shape[1]

    def columns_of(f, dynamic):
        cols = pl.ds(pl.multiple_of(f, step), step) if dynamic else slice(f, f + step)

        def rows_of(rows):
            hidden = nn(third_in[rows, :], up[:, cols])
            square = hidden * hidden
            t = jnp.tanh(GELU_A * hidden * (1.0 + GELU_B * square))
            half = 0.5 * (1.0 + t)
            low = (hidden * half).astype(bf16)
            slope = half + 0.5 * hidden * (1.0 - t * t) * (GELU_A * (1.0 + 3.0 * GELU_B * square))
            low_grad = (nt(cotangent[rows, :], down[cols, :]) * slope).astype(bf16)
            active[rows, :] = low
            hidden_grad[rows, :] = low_grad
            final[rows, :] += nn(low, down[cols, :])
            norm_grad[rows, :] += nt(low_grad, up[:, cols])

        loop(count, 768, rows_of)
        up_part = tn(third_in[...], hidden_grad[...]).astype(bf16)
        down_part = tn(active[...], cotangent[...]).astype(bf16)
        each = ff // parts
        for i in range(step // WIDE):
            col = f + i * WIDE
            base = up_base + col % each // WIDE * D
            at = pl.ds(pl.multiple_of(base, 16), D) if dynamic else slice(base, base + D)
            g_out[col // each, at, :] = up_part[:, i * WIDE : (i + 1) * WIDE]
        each = D // parts
        if dynamic:
            for b in range(parts):
                for i in range(each // WIDE):
                    start = b * each + i * WIDE
                    at = pl.ds(pl.multiple_of(down_base + i * ff + f, 16), step)
                    g_out[b, at, :] = down_part[:, start : start + WIDE]
            return
        for to_row, to_lane, row, col, deep, lanes in slab_pieces(ff, each):
            if row <= f < row + deep:
                at = down_base + to_row + f - row
                for b in range(parts):
                    g_out[b, at : at + step, to_lane : to_lane + lanes] = down_part[
                        :, b * each + col : b * each + col + lanes
                    ]

    if D // parts % WIDE == 0:
        def turn(i, carry):
            columns_of(i * step, True)
            return carry

        lax.fori_loop(0, ff // step, turn, 0)
    else:
        for f in range(0, ff, step):
            columns_of(f, False)
    clear_tail(g_out, down_base + slab_rows(ff, D, parts))
    saves = [
        pltpu.make_async_copy(g_out.at[:, rows], g_hbm.at[:, rows], save_sems.at[i])
        for i, rows in enumerate((slice(up_base, g_out.shape[1]), slice(0, up_base)))
    ]
    saves[0].start()
    for fetch in fetches[3:]:
        fetch.wait()
    modes[...] = jnp.zeros_like(modes)
    self_grad = third_in

    def end(rows):
        mixed[rows, :] = final[rows, :].astype(bf16)
        back, sums = modulate_back(norm_grad[rows, :], two[rows, :], rows3[0], rows3[1], rows3[3])
        modes[...] += sums
        grad = cotangent[rows, :].astype(f32) + back
        grad_two[rows, :] = grad
        low = grad.astype(bf16)
        self_grad[rows, :] = low
        att_grad = nt(low, wo[...])
        for inv, do_out, x_out in ((inv_near, do_near, x_near), (inv_far, do_far, x_far)):
            do = (att_grad * inv[rows, :]).astype(bf16)
            do_out[rows, :] = do
            x_out[rows, :] = delta_lanes(do.astype(f32) * self_att[rows, :])

    loop(count, 384, end)
    slabs_by_rows(g_out, 0, D, D, lambda rows: tn(self_att[:, rows].astype(bf16), self_grad[...]))
    saves[1].start()
    for save in saves:
        save.wait()


def project_back(dkvt, wqkv, part_out):
    count, rows, _ = part_out.shape
    for b in range(count):
        part = nn(wqkv[:, D:], dkvt[:, b * rows : (b + 1) * rows])
        part_out[b] = part.astype(bf16).T


class Mover:
    def __init__(self, send, recv):
        self.send, self.recv = send, recv
        self.copies = []
        place, obj = lax.axis_index("blk"), lax.axis_index("obj")
        self.chips = lax.axis_size("blk") // 2
        self.columns = lax.axis_size("obj") // 2
        self.core, self.chip = lax.rem(place, 2), place // 2
        self.side, self.column = lax.rem(obj, 2), obj // 2
        self.sibling = {"blk": self.chip * 2 + 1 - self.core}
        self.chip_ids = [lax.rem(self.chip + d, self.chips) for d in range(1, self.chips)]
        self.chip_peers = [{"blk": c * 2 + self.core} for c in self.chip_ids]
        self.across = {"obj": self.column * 2 + 1 - self.side}
        objects = lax.axis_size("obj")
        self.obj = obj
        self.object_ids = [lax.rem(obj + d, objects) for d in range(1, objects)]
        self.object_peers = [{"obj": o} for o in self.object_ids]
        self.column_ids = [lax.rem(self.column + d, self.columns) for d in range(1, self.columns)]
        self.column_peers = [{"obj": c * 2 + self.side} for c in self.column_ids]

    def barrier(self, all_objects=False):
        everyone = [self.sibling] + self.chip_peers
        everyone += self.object_peers if all_objects else [self.across] + self.column_peers
        semaphore = pltpu.get_barrier_semaphore()
        for target in everyone:
            pl.semaphore_signal(semaphore, inc=1, device_id=target, device_id_type=pl.DeviceIdType.MESH)
        pl.semaphore_wait(semaphore, len(everyone))

    def copy(self, src, dst, target):
        at = len(self.copies)
        made = pltpu.make_async_remote_copy(
            src_ref=src, dst_ref=dst, send_sem=self.send.at[at], recv_sem=self.recv.at[at],
            device_id=target, device_id_type=pl.DeviceIdType.MESH,
        )
        self.copies.append(made)
        return made

    def drain(self):
        for made in self.copies:
            made.wait_send()


def begin(copies):
    for made in copies:
        made.start()


def arrive(copies):
    for made in copies:
        made.wait_recv()


def added(*values):
    total = values[0].astype(f32)
    for value in values[1:]:
        total = total + value.astype(f32)
    return total.astype(bf16)


def cut(rows, objects):
    unit = 16 * objects
    first = (rows // unit + 1) // 2 * unit
    return first, rows - first


def in_groups(rows, objects, groups):
    return cut(rows, objects) if groups == 2 else (rows,)


class Gather:
    @staticmethod
    def scratch(chips, rows, objects, lanes):
        first, second = cut(rows, objects)
        return [
            VMEM((chips, rows, lanes), bf16),
            VMEM((max(chips - 1, 1), first, lanes), bf16), VMEM((2, first // 2, lanes), bf16), VMEM((first // 2, lanes), bf16),
            VMEM((chips, second // 2, lanes), bf16), VMEM((chips, second // 2, lanes), bf16),
            VMEM((max(chips - 1, 1), second // 2, lanes), bf16),
        ]

    @staticmethod
    def copies(chips):
        return 2 * chips + 2 * (chips - 1) + 1 + chips

    def __init__(self, mover, g, scratch, out_first, out_second):
        self.mover, self.g = mover, g
        self.mine, self.far0, self.flat0, self.across0, self.across1, self.mine1, self.far1 = scratch
        self.out0, self.out1 = out_first, out_second
        first, half1 = self.far0.shape[1], self.mine1.shape[1]
        m, chips = mover, mover.chips
        self.rows = (slice(0, first), slice(first, first + 2 * half1))
        other = 1 - m.core
        self.core = [
            [m.copy(g.at[2 * j + other, rows], self.mine.at[j, rows], m.sibling) for j in range(chips)]
            for rows in self.rows
        ]
        self.chip0 = [
            m.copy(self.mine.at[c, self.rows[0]], self.far0.at[d], peer)
            for d, (c, peer) in enumerate(zip(m.chip_ids, m.chip_peers))
        ]
        self.side0 = [m.copy(self.flat0.at[1 - m.side], self.across0, m.across)]
        away = pl.ds(pl.multiple_of(first + (1 - m.side) * half1, 16), half1)
        self.kept = pl.ds(pl.multiple_of(first + m.side * half1, 16), half1)
        self.side1 = [m.copy(self.mine.at[j, away], self.across1.at[j], m.across) for j in range(chips)]
        self.chip1 = [
            m.copy(self.mine1.at[c], self.far1.at[d], peer)
            for d, (c, peer) in enumerate(zip(m.chip_ids, m.chip_peers))
        ]

    def step0(self):
        begin(self.core[0] + self.core[1])

    def step1(self):
        for group, after in ((0, self.chip0), (1, self.side1)):
            arrive(self.core[group])
            rows = self.rows[group]
            for j in range(self.mover.chips):
                self.mine[j, rows] = added(self.g[2 * j + self.mover.core, rows], self.mine[j, rows])
            begin(after)

    def step2(self):
        m = self.mover
        arrive(self.chip0)
        total = added(self.mine[m.chip, self.rows[0]], *[self.far0[d] for d in range(m.chips - 1)])
        self.flat0[...] = total.reshape(self.flat0.shape)
        begin(self.side0)
        arrive(self.side1)
        for j in range(m.chips):
            self.mine1[j] = added(self.mine[j, self.kept], self.across1[j])
        begin(self.chip1)

    def step3(self):
        m = self.mover
        arrive(self.side0)
        self.out0[...] = added(self.flat0[m.side], self.across0[...])
        arrive(self.chip1)
        self.out1[...] = added(self.mine1[m.chip], *[self.far1[d] for d in range(m.chips - 1)])


class Spread:
    @staticmethod
    def scratch(objects, half, lanes):
        columns = objects // 2
        return VMEM((max(columns - 1, 1), half // columns, lanes), bf16)

    @staticmethod
    def copies(objects):
        return 2 * (objects // 2 - 1)

    def __init__(self, mover, half, taken, out):
        m = mover
        self.mover, self.half, self.taken, self.out = mover, half, taken, out
        piece = taken.shape[1]
        self.piece = pl.ds(pl.multiple_of(m.column * piece, 16), piece)
        self.sums = [
            m.copy(half.at[pl.ds(pl.multiple_of(c * piece, 16), piece)], taken.at[d], peer)
            for d, (c, peer) in enumerate(zip(m.column_ids, m.column_peers))
        ]
        own = out.at[m.column]
        self.shares = [m.copy(own, own, peer) for peer in m.column_peers]

    def step0(self):
        begin(self.sums)

    def step1(self):
        arrive(self.sums)
        m = self.mover
        self.out[m.column] = added(self.half[self.piece], *[self.taken[d] for d in range(m.columns - 1)])
        begin(self.shares)

    def step2(self):
        arrive(self.shares)


class Cross:
    def __init__(self, mover, own, other):
        self.own, self.other = own, other
        self.copies = [mover.copy(own, other, mover.across)]

    def start(self):
        begin(self.copies)

    def wait(self):
        arrive(self.copies)


def put_sides(mover, own, other, out):
    out[mover.side] = own[...]
    out[1 - mover.side] = other[...]


class Fetch:
    def __init__(self, pairs, sems):
        self.copies = [pltpu.make_async_copy(src, dst, sems.at[i]) for i, (src, dst) in enumerate(pairs)]

    def start(self):
        begin(self.copies)

    def wait(self):
        for made in self.copies:
            made.wait()


def self_back_kernel(
    count, do_far, x_far, do_near, x_near, q, kv_far, kv_near_hbm, w_far, w_near, wqkv_hbm, g_early, *refs
):
    late_hbm = refs[:2] + tuple(refs[2].at[i] for i in range(count))
    (norm_grad, g_out, out0, out1, dq, dkvt_far, dkvt_near, do_far_t, do_near_t, q_t, far_parts, near_parts,
     from_sibling, chip_sums, from_chips, near_sibling, half0, half1, taken0, taken1, sums0, sums1,
     kv_near, wqkv) = refs[3:27]
    late = refs[27 : count + 29]
    own, sibling, blocks = late[0], late[1], late[2:]
    gather_scratch, sems, moving = refs[count + 29 : -3], refs[-3], refs[-2:]
    h = pl.program_id(0)
    fetch = Fetch(list(zip((kv_near_hbm, wqkv_hbm) + tuple(late_hbm), (kv_near, wqkv) + tuple(late))), sems)
    m = Mover(*moving)
    gather = Gather(m, g_early, gather_scratch, half0, half1)
    spreads = [Spread(m, half0, taken0, sums0), Spread(m, half1, taken1, sums1)]
    chips = m.chips
    far_core = [m.copy(far_parts.at[2 * d + 1], from_sibling.at[d], m.sibling) for d in range(chips - 1)]
    back = [{"blk": lax.rem(m.chip + chips - d, chips) * 2 + m.core} for d in range(1, chips)]
    far_chip = [m.copy(chip_sums.at[d], from_chips.at[d], back[d]) for d in range(chips - 1)]
    near_core = [m.copy(near_parts.at[1], near_sibling, m.sibling)]

    @pl.when(h == 0)
    def _():
        m.barrier()
        gather.step0()
        fetch.start()
        do_far_t[...] = do_far[...].T
        q_t[...] = q[...].T
        dq[...] = jnp.zeros_like(dq)

    @pl.when(h == 1)
    def _():
        gather.step1()

    @pl.when(h == 6)
    def _():
        gather.step2()

    @pl.when(h == HEADS)
    def _():
        fetch.wait()
        project_back(dkvt_far, wqkv, far_parts)
        begin(far_core)
        gather.step3()
        for spread in spreads:
            spread.step0()
        do_near_t[...] = do_near[...].T

    @pl.when(h == HEADS + 1)
    def _():
        arrive(far_core)
        for d in range(chips - 1):
            chip_sums[d] = added(far_parts[2 * d], from_sibling[d])
        begin(far_chip)

    @pl.when(h == HEADS + 4)
    def _():
        spreads[0].step1()

    @pl.when(h == HEADS + 5)
    def _():
        spreads[1].step1()

    @pl.when(h < HEADS)
    def _():
        attend_back(h, do_far, x_far, do_far_t, q_t, kv_far, w_far, dq, dkvt_far, kv_far.shape[0], 512)

    @pl.when(h >= HEADS)
    def _():
        attend_back(h - HEADS, do_near, x_near, do_near_t, q_t, kv_near, w_near, dq, dkvt_near, kv_near.shape[0], 512)

    @pl.when(h == 2 * HEADS - 1)
    def _():
        project_back(dkvt_near, wqkv, near_parts)
        begin(near_core)
        dq_low = dq[...].astype(bf16)
        rows = own.shape[0]
        grad = nn(dkvt_near[:, :rows], own[...]) + nn(dkvt_near[:, rows:], sibling[...])
        for i, block in enumerate(blocks):
            grad = grad + nn(dkvt_far[:, i * rows : (i + 1) * rows], block[...])
        slabs(g_out, 0, jnp.concatenate([tn(own[...], dq_low), grad.T], 1))
        clear_tail(g_out, slab_rows(D, 3 * D, g_out.shape[0]))
        total = nt(dq_low, wqkv[:, :D]) + near_parts[0].astype(f32)
        arrive(far_chip)
        for d in range(chips - 1):
            total = total + from_chips[d].astype(f32)
        arrive(near_core)
        norm_grad[...] = total + near_sibling[...].astype(f32)
        for spread, out in zip(spreads, (out0, out1)):
            spread.step2()
            out[...] = spread.out[...]
        m.drain()


class Job:
    @staticmethod
    def scratch(chips, rows, objects, lanes, groups):
        made = [VMEM((chips, rows, lanes), bf16), VMEM((max(chips - 1, 1), rows, lanes), bf16)]
        for n in in_groups(rows, objects, groups):
            piece = n // objects
            made += [
                VMEM((objects, piece, lanes), bf16), VMEM((objects - 1, piece, lanes), bf16),
                VMEM((objects, piece, lanes), bf16),
            ]
        return made

    @staticmethod
    def copies(chips, objects, groups):
        return groups * (2 * chips - 1 + 2 * (objects - 1))

    def __init__(self, mover, g, scratch):
        m = mover
        self.mover, self.g = m, g
        self.mine, self.far = scratch[:2]
        self.groups = []
        start = 0
        for shard, taken, sums in (scratch[i : i + 3] for i in range(2, len(scratch), 3)):
            objects, piece, _ = shard.shape
            rows = slice(start, start + objects * piece)
            start += objects * piece
            core = [m.copy(g.at[2 * j + 1 - m.core, rows], self.mine.at[j, rows], m.sibling) for j in range(m.chips)]
            chip = [
                m.copy(self.mine.at[c, rows], self.far.at[d, rows], peer)
                for d, (c, peer) in enumerate(zip(m.chip_ids, m.chip_peers))
            ]
            pieces = [
                m.copy(shard.at[o], taken.at[d], peer) for d, (o, peer) in enumerate(zip(m.object_ids, m.object_peers))
            ]
            shares = [m.copy(sums.at[m.obj], sums.at[m.obj], peer) for peer in m.object_peers]
            self.groups.append((rows, shard, taken, sums, core, chip, pieces, shares))

    def step0(self):
        for group in self.groups:
            begin(group[4])

    def step1(self):
        m = self.mover
        for rows, _, _, _, core, chip, _, _ in self.groups:
            arrive(core)
            for j in range(m.chips):
                self.mine[j, rows] = added(self.g[2 * j + m.core, rows], self.mine[j, rows])
            begin(chip)

    def step2(self):
        m = self.mover
        for rows, shard, _, _, _, chip, pieces, _ in self.groups:
            arrive(chip)
            total = added(self.mine[m.chip, rows], *[self.far[d, rows] for d in range(m.chips - 1)])
            shard[...] = total.reshape(shard.shape)
            begin(pieces)

    def step3(self):
        m = self.mover
        for _, shard, taken, sums, _, _, pieces, shares in self.groups:
            arrive(pieces)
            sums[m.obj] = added(shard[m.obj], *[taken[d] for d in range(taken.shape[0])])
            begin(shares)

    def finish(self, outs):
        for group, out in zip(self.groups, outs):
            arrive(group[7])
            out[...] = group[3][...]


def cross_back_kernel(
    context_count, groups, norm_grad, grad_two, after_one, tokens, context, q, pair, w, att, inv,
    wq, wkv, wo, gain, bias, mod, g_middle, modes_three, lifted, own0, own1,
    tokens_grad, ctx_result, small_result, early0, early1, *rest
):
    outs, rest = rest[: sum(groups)], rest[sum(groups) :]
    mid_outs, out_outs, late_outs = outs[: groups[0]], outs[groups[0] : -groups[2]], outs[-groups[2] :]
    (dkvt, do, x, do_t, q_t, dq, g_out, g_late, small, ctx,
     ctx_half, ctx_mine, ctx_far, small_half, small_mine, small_far, ctx_out, small_out, other0, other1, *rest) = rest
    h = pl.program_id(0)
    m = Mover(*rest[-2:])
    chips = m.chips
    ends = [2 + 3 * groups[0], 4 + 3 * (groups[0] + groups[1]), 6 + 3 * sum(groups)]
    middle = Job(m, g_middle, rest[: ends[0]])
    outer = Job(m, g_out, rest[ends[0] : ends[1]])
    late = Job(m, g_late, rest[ends[1] : ends[2]])
    early = [Cross(m, own0, other0), Cross(m, own1, other1)]
    ctx_rows = ctx.shape[0] // 2
    ctx_own = pl.ds(pl.multiple_of(m.core * ctx_rows, 16), ctx_rows)
    ctx_other = pl.ds(pl.multiple_of((1 - m.core) * ctx_rows, 16), ctx_rows)
    ctx_core = [m.copy(ctx.at[ctx_other], ctx_half, m.sibling)]
    ctx_chip = [m.copy(ctx_mine, ctx_far.at[d], m.chip_peers[d]) for d in range(chips - 1)]
    ctx_back = [m.copy(ctx_out.at[ctx_own], ctx_out.at[ctx_own], m.sibling)]
    small_core = [m.copy(small, small_half, m.sibling)]
    small_chip = [m.copy(small_mine, small_far.at[d], m.chip_peers[d]) for d in range(chips - 1)]
    small_share = [m.copy(small_out.at[m.obj], small_out.at[m.obj], peer) for peer in m.object_peers]
    late_base = slab_rows(D, D, g_late.shape[0])

    @pl.when(h == 0)
    def _():
        m.barrier(True)
        middle.step0()
        rows = norm_rows(gain, bias, mod, 1)
        back, sums = modulate_back(norm_grad[...], after_one[...], rows[0], rows[1], rows[3])
        grad_one = grad_two[...] + back
        tokens_grad[...] = grad_one
        small[4:8, :] = sums
        small[8:12, :] = modes_three[...]
        for i in range(2):
            row = lifted[:, i * D : (i + 1) * D].astype(f32)
            small[12 + i : 13 + i, :] = row * (0.5 / chips)
        small[14:16, :] = jnp.zeros((2, D), f32)
        cross_grad = grad_one.astype(bf16)
        middle.step1()
        slabs(g_out, 0, tn(att[...].astype(bf16), cross_grad))
        clear_tail(g_out, slab_rows(D, D, g_out.shape[0]))
        outer.step0()
        do[...] = (nt(cross_grad, wo[...]) * inv[...]).astype(bf16)
        x[...] = delta_lanes(do[...].astype(f32) * att[...])
        do_t[...] = do[...].T
        q_t[...] = q[...].T
        dq[...] = jnp.zeros_like(dq)

    @pl.when(h == 1)
    def _():
        outer.step1()

    @pl.when(h == 4)
    def _():
        middle.step2()

    @pl.when(h == 5)
    def _():
        outer.step2()
        for cross in early:
            cross.start()

    attend_back(h, do, x, do_t, q_t, pair, w, dq, dkvt, context_count, pair.shape[0])

    @pl.when(h == HEADS - 1)
    def _():
        dq_low = dq[...].astype(bf16)
        first = tokens[...].astype(f32)
        rows = norm_rows(gain, bias, mod, 0)
        first_in = modulate(first, *rows).astype(bf16)
        slabs(g_late, 0, tn(first_in, dq_low))
        real = lax.broadcasted_iota(jnp.int32, dkvt.shape, 1) < context_count
        kept = jnp.where(real, dkvt[...], jnp.zeros_like(dkvt))
        slabs(g_late, late_base, nn(kept, context[...]).T)
        clear_tail(g_late, late_base + slab_rows(context.shape[1], 2 * D, g_late.shape[0]))
        late.step0()
        ctx[...] = tn(dkvt[...], wkv[...].T).astype(bf16)
        begin(ctx_core)
        late.step1()
        middle.step3()
        outer.step3()

        back, sums = modulate_back(nt(dq_low, wq[...]), first, rows[0], rows[1], rows[3])
        small[0:4, :] = sums
        begin(small_core)
        late.step2()
        arrive(ctx_core)
        ctx_mine[...] = added(ctx[ctx_own], ctx_half[...])
        begin(ctx_chip)
        arrive(small_core)
        small_mine[...] = small[...] + small_half[...]
        begin(small_chip)
        tokens_grad[...] = tokens_grad[...] + back
        for cross, own, out in zip(early, (own0, own1), (early0, early1)):
            cross.wait()
            put_sides(m, own, cross.other, out)
        arrive(small_chip)
        total = small_mine[...]
        for d in range(chips - 1):
            total = total + small_far[d]
        small_out[m.obj] = total
        begin(small_share)
        late.step3()
        arrive(ctx_chip)
        ctx_out[ctx_own] = added(ctx_mine[...], *[ctx_far[d] for d in range(chips - 1)])
        begin(ctx_back)
        middle.finish(mid_outs)
        outer.finish(out_outs)
        arrive(small_share)
        small_result[...] = small_out[...]
        arrive(ctx_back)
        ctx_result[...] = ctx_out[...]
        late.finish(late_outs)
        m.drain()


def finish_kernel(parts, groups, *refs):
    sums, refs = refs[: 2 + sum(groups)], refs[2 + sum(groups) :]
    small, ctx, tokens_in, gains, biases, modb, ctx_out, tokens_out = refs[:8]
    results, (so, up, down, qkv, co, cq, ckv, modw), mode, sems = refs[8:16], refs[16:24], refs[24], refs[25]
    saves = []

    def save(src, dst):
        made = pltpu.make_async_copy(src, dst, sems.at[len(saves)])
        made.start()
        saves.append(made)

    save(tokens_in, tokens_out)
    place = lax.axis_index("blk")
    width = 2 * D // parts
    each = D // parts

    def put(out, total, base):
        depth, columns = out.shape
        for to_row, to_lane, row, col, deep, lanes in slab_pieces(depth, columns):
            out[row : row + deep, col : col + lanes] = total[
                base + to_row : base + to_row + deep, to_lane : to_lane + lanes
            ].astype(f32)
        for scratch, result in zip((so, up, down, qkv, co, cq, ckv), results):
            if scratch is out:
                save(out, result)
        return base + slab_rows(depth, columns, 1)

    join = lambda start, count: jnp.concatenate([ref[...] for ref in sums[start : start + count]], 0)
    early = join(0, 2)
    base = put(so, early, 0)
    base = put(up, early, base)
    put(down, early, base)
    put(qkv, join(2, groups[0]), 0)
    put(co, join(2 + groups[0], groups[1]), 0)
    late = join(2 + groups[0] + groups[1], groups[2])
    base = put(cq, late, 0)
    put(ckv, late, base)
    lifted = jnp.concatenate([small[:, 12, :], small[:, 13, :]], 1)
    summed = jnp.sum(small[...], 0)
    for b in range(parts):
        @pl.when(place == b)
        def _():
            row, col = b * width // D, b * width % D
            for j in range(3):
                mode[j] = small[:, 4 * j + row, col : col + width]
                gains[j : j + 1, :] = summed[4 * j + 2 : 4 * j + 3, b * each : (b + 1) * each]
                biases[j : j + 1, :] = summed[4 * j + 3 : 4 * j + 4, b * each : (b + 1) * each]
    for j in range(3):
        modw[j] = lax.dot_general(
            lifted, mode[j], (((0,), (0,)), ((), ())), precision=lax.Precision.HIGHEST, preferred_element_type=f32
        )
        modb[j : j + 1, :] = jnp.sum(mode[j], 0, keepdims=True)
    save(modw, results[7])
    ctx_out[...] = ctx[: ctx_out.shape[0], :].astype(f32).reshape(ctx_out.shape)
    for made in saves:
        made.wait()


def shape(dims, dtype):
    return jax.ShapeDtypeStruct(tuple(dims), dtype)


def body(
    tokens, context, camera_groups, camera_table, cross_query, cross_kv, cross_out, self_qkv,
    self_out, mlp_up, mlp_down, norm_gain, norm_bias, mod_weight, mod_bias, cotangent,
):
    parts = lax.axis_size("blk")
    tokens = tokens[0]
    cotangent = cotangent[0]
    context_count = context.shape[1]
    rows = tokens.shape[0]
    length = rows * parts
    ff = mlp_up.shape[1]
    cam_width = mod_weight.shape[1]
    ctx_width = context.shape[2]
    padded = -(-context_count // 128) * 128
    context_rows = jnp.pad(context[0], ((0, padded - context_count), (0, 0)), mode="edge")

    picked = (
        camera_groups[:, None] == jnp.arange(camera_table.shape[0], dtype=jnp.int32)[None, :]
    ).astype(bf16)
    camera = jnp.dot(picked, camera_table, preferred_element_type=f32)
    lifted = jax.nn.silu(camera).astype(bf16)
    mod = (
        jnp.einsum("oc,jcm->ojm", lifted, mod_weight, preferred_element_type=f32)
        + mod_bias.astype(f32)
    )[0]

    def near_hop(block):
        return lax.ppermute(block, "blk", [(i, i ^ 1) for i in range(parts)])

    def chip_hop(block, distance):
        route = [(i, (i // 2 + distance) % chips * 2 + i % 2) for i in range(parts)]
        return lax.ppermute(block, "blk", route)

    chips = parts // 2
    objects = lax.axis_size("obj")
    full = lambda *dims: pl.BlockSpec(dims, lambda h: (0,) * len(dims))
    head = lambda keys: pl.BlockSpec((1, rows, keys), lambda h: (h, 0, 0))
    row_full = full(rows, D)
    row_f32, row_bf16 = shape((rows, D), f32), shape((rows, D), bf16)
    two_heads = VMEM((2, rows, WIDE), f32)
    flag = pltpu.SMEM((1,), jnp.int32)
    anywhere = pl.BlockSpec(memory_space=pl.ANY)
    pair_block = pl.BlockSpec((rows, WIDE), lambda h: (0, h // 2))
    head_block = pl.BlockSpec((1, rows, WIDE), lambda h: (h, 0, 0))
    heads_block = pl.BlockSpec((2, rows, WIDE), lambda h: (h // 2, 0, 0))
    sums_f32 = shape((HEADS, rows, WIDE), f32)
    transposed = [VMEM((D, rows), bf16), VMEM((D, rows), bf16)]
    norm_full = [full(3, D), full(3, D), full(3, 2 * D)]

    def call(kernel, name, us, outs, ins, out_specs, scratch=(), collective_id=None, mib=60, free=None, **more):
        if free is not None:
            outs = [item if i in free else pltpu.HBM(item.shape, item.dtype) for i, item in enumerate(outs)]
        return pl.pallas_call(
            kernel, name=name, out_shape=outs, in_specs=ins, out_specs=out_specs, scratch_shapes=list(scratch),
            cost_estimate=pl.CostEstimate(flops=int(us * 1.1e9), bytes_accessed=int(us * 3.6e6), transcendentals=0),
            compiler_params=params(mib) if collective_id is None else pltpu.CompilerParams(
                vmem_limit_bytes=62 * MIB, collective_id=collective_id, has_side_effects=True
            ), **more,
        )

    second_in, after_one, cross_q, cross_pair, cross_w, cross_att, cross_inv = call(
        functools.partial(cross_kernel, context_count), "cross_forward", 15,
        [row_bf16, row_f32, row_bf16, shape((padded, 2 * D), bf16), shape((HEADS, rows, padded), bf16), row_f32, row_f32],
        [row_full, full(padded, ctx_width), full(D, D), full(ctx_width, 2 * D), full(D, D)] + norm_full,
        [row_full, row_full, anywhere, anywhere, head(padded), pair_block, pair_block],
        [VMEM((rows, D), bf16), VMEM((padded, 2 * D), bf16), VMEM((rows, D), bf16), two_heads, flag,
         pltpu.SemaphoreType.DMA((2,))], grid=(HEADS,), mib=32, free=(0,),
    )(tokens, context_rows, cross_query, cross_kv, cross_out, norm_gain, norm_bias, mod)

    sibling_in = near_hop(second_in)
    chip_in = [chip_hop(second_in, d) for d in range(1, chips)]
    near_keys, far_keys = 2 * rows, 2 * rows * (chips - 1)
    near_w, self_q, near_kv, near_acc, near_top = call(
        near_kernel, "near_forward", 16,
        [shape((HEADS, rows, near_keys), bf16), row_bf16, shape((near_keys, 2 * D), bf16), sums_f32, sums_f32],
        [row_full, row_full, full(D, 3 * D)],
        [head(near_keys), anywhere, anywhere, head_block, head_block],
        [VMEM((rows, D), bf16), VMEM((near_keys, 2 * D), bf16), flag, pltpu.SemaphoreType.DMA((2,))], grid=(HEADS,), mib=32, free=(),
    )(second_in, sibling_in, self_qkv)
    chip_in, near_kv = lax.optimization_barrier((chip_in, near_kv))
    far_in = []
    for block in chip_in:
        far_in += [block, near_hop(block)]
    count = len(far_in)
    far_w, far_kv, far_rows, self_att, near_inv, far_inv = call(
        functools.partial(far_kernel, count), "far_forward", 16,
        [shape((HEADS, rows, far_keys), bf16), shape((far_keys, 2 * D), bf16), shape((count, rows, D), bf16),
         row_f32, row_f32, row_f32],
        [row_full] * count + [full(D, 3 * D), row_full, heads_block, heads_block],
        [head(far_keys), anywhere, anywhere, pair_block, pair_block, pair_block],
        [VMEM((far_keys, 2 * D), bf16), two_heads, two_heads, flag, pltpu.SemaphoreType.DMA((count + 1,))], grid=(HEADS,), mib=32, free=(),
    )(*far_in, self_qkv, *[pltpu.with_memory_space_constraint(v, pltpu.HBM) for v in (self_q, near_acc, near_top)])

    lanes = WIDE
    tall = lambda columns, depth: slab_rows(depth, columns, parts)
    early = padded_rows(tall(D, D) + tall(ff, D) + tall(D, ff), objects)
    mixed, grad_two, near_do, near_x, far_do, far_x, modes_three, g_early = call(
        mlp_kernel, "feed_forward", 20,
        [row_bf16, row_f32, row_bf16, row_bf16, row_bf16, row_bf16, shape((4, D), f32), shape((parts, early, lanes), bf16)],
        [whole()] * 6 + [anywhere] * 5, [whole()] * 7 + [anywhere],
        [VMEM((D, ff), bf16), VMEM((rows, D), bf16), VMEM((ff, D), bf16), VMEM((rows, D), f32), VMEM((rows, D), f32),
         VMEM((parts, early, lanes), bf16), VMEM((rows, D), f32), VMEM((rows, D), f32), VMEM((rows, D), f32),
         VMEM((rows, D), bf16), VMEM((rows, 512), bf16), VMEM((rows, 512), bf16),
         pltpu.SemaphoreType.DMA((5,)), pltpu.SemaphoreType.DMA((2,))],
    )(self_att, after_one, self_out, norm_gain, norm_bias, mod, mlp_up, cotangent, mlp_down, near_inv, far_inv)

    unit = objects // 2
    moving = lambda copies: [pltpu.SemaphoreType.DMA((copies,)), pltpu.SemaphoreType.DMA((copies,))]
    halves = lambda rows: [shape((n // 2, lanes), bf16) for n in cut(rows, objects)]
    half_vmem = lambda rows: [VMEM((n // 2, lanes), bf16) for n in cut(rows, objects)]
    spread_outs = lambda rows: [shape((2, unit, n // objects, lanes), bf16) for n in cut(rows, objects)]
    own_outs = lambda rows: [shape((unit, n // objects, lanes), bf16) for n in cut(rows, objects)]
    taken = lambda rows: [Spread.scratch(objects, n // 2, lanes) for n in cut(rows, objects)]
    in_vmem = lambda shapes: [VMEM(item.shape, item.dtype) for item in shapes]
    once = lambda *dims: pl.BlockSpec(dims, lambda h: (0,) * len(dims), pipeline_mode=pl.Buffered(1))
    like = lambda shapes: [once(*item.shape) for item in shapes]
    row_once = once(rows, D)

    middle = padded_rows(tall(3 * D, D), objects)
    own_shapes = own_outs(early)
    hops = VMEM((chips - 1, rows, D), bf16)
    row_vmem = VMEM((rows, D), bf16)
    norm_grad, g_middle, own0, own1 = call(
        functools.partial(self_back_kernel, count), "self_backward", 60,
        [row_f32, shape((parts, middle, lanes), bf16)] + own_shapes,
        [row_once] * 5 + [once(far_keys, 2 * D), anywhere,
         pl.BlockSpec((1, rows, far_keys), lambda h: (jnp.minimum(h, HEADS - 1), 0, 0)),
         pl.BlockSpec((1, rows, near_keys), lambda h: (jnp.maximum(h - HEADS, 0), 0, 0)),
         anywhere, once(parts, early, lanes)] + [anywhere] * 3,
        [row_once, once(parts, middle, lanes)] + like(own_shapes),
        [VMEM((rows, D), f32), VMEM((2 * D, far_keys), bf16), VMEM((2 * D, near_keys), bf16)]
        + [VMEM((D, rows), bf16)] * 3 + [VMEM((count, rows, D), bf16), VMEM((2, rows, D), bf16)]
        + [hops, hops, hops, row_vmem] + half_vmem(early) + taken(early) + in_vmem(own_shapes)
        + [VMEM((near_keys, 2 * D), bf16), VMEM((D, 3 * D), bf16)] + [row_vmem] * (2 + count)
        + Gather.scratch(chips, early, objects, lanes) + [pltpu.SemaphoreType.DMA((count + 4,))]
        + moving(Gather.copies(chips) + 2 * (chips - 1) + 1 + 2 * Spread.copies(objects)),
        grid=(2 * HEADS,), collective_id=1,
    )(far_do, far_x, near_do, near_x, self_q, far_kv, near_kv, far_w, near_w, self_qkv, g_early,
      second_in, sibling_in, far_rows)

    outer = padded_rows(tall(D, D), objects)
    groups = (1, 1, 1)
    late = padded_rows(tall(D, D) + tall(2 * D, ctx_width), objects)
    sums = spread_outs(early) + [
        shape((objects, n // objects, lanes), bf16) for total, n_groups in zip((middle, outer, late), groups) for n in in_groups(total, objects, n_groups)
    ]
    ctx_half = VMEM((padded // 2, ctx_width), bf16)
    small_vmem = VMEM((16, D), f32)
    tokens_grad, context_sum, small_all, *sums = call(
        functools.partial(cross_back_kernel, context_count, groups), "cross_backward", 20,
        [row_f32, shape((padded, ctx_width), bf16), shape((objects, 16, D), f32)] + sums,
        [row_once] * 4 + [once(padded, ctx_width), row_once, once(padded, 2 * D), head(padded), row_once, row_once,
         once(D, D), once(ctx_width, 2 * D), once(D, D)] + norm_full + [once(parts, middle, lanes), full(4, D), full(1, cam_width)]
        + like(own_shapes),
        [row_once, once(padded, ctx_width), once(objects, 16, D)] + like(sums),
        [VMEM((2 * D, padded), bf16), row_vmem, row_vmem] + transposed + [VMEM((rows, D), f32)]
        + [VMEM((parts, outer, lanes), bf16), VMEM((parts, late, lanes), bf16), small_vmem, VMEM((padded, ctx_width), bf16)]
        + [ctx_half, ctx_half, VMEM((chips - 1, padded // 2, ctx_width), bf16)]
        + [small_vmem, small_vmem, VMEM((chips - 1, 16, D), f32)]
        + [VMEM((padded, ctx_width), bf16), VMEM((objects, 16, D), f32)] + in_vmem(own_shapes)
        + Job.scratch(chips, middle, objects, lanes, groups[0]) + Job.scratch(chips, outer, objects, lanes, groups[1])
        + Job.scratch(chips, late, objects, lanes, groups[2])
        + moving(Job.copies(chips, objects, sum(groups)) + 2 + chips + 1 + chips + objects - 1),
        grid=(HEADS,), collective_id=2,
    )(
        norm_grad, grad_two, after_one, tokens, context_rows, cross_q, cross_pair, cross_w,
        cross_att, cross_inv, cross_query, cross_kv, cross_out, norm_gain, norm_bias, mod, g_middle, modes_three,
        lifted, own0, own1,
    )
    width = 2 * D // parts
    grads = lambda depth, columns: shape((depth, columns // parts), f32)
    large = [
        grads(D, D), grads(D, ff), grads(ff, D), grads(D, 3 * D), grads(D, D), grads(D, D), grads(ctx_width, 2 * D),
        shape((3, cam_width, width), f32),
    ]
    gains, biases, modb, context_grad, tokens_grad, so, up, down, qkv, co, cq, ckv, modw = pl.pallas_call(
        functools.partial(finish_kernel, parts, groups),
        name="finish",
        out_shape=[
            grads(3, D), grads(3, D), grads(3, 2 * D), shape((context_count, 1, ctx_width), f32), shape((rows, D), f32),
        ] + large,
        in_specs=[whole()] * (5 + sum(groups)),
        out_specs=[whole()] * 4 + [anywhere] * 9,
        scratch_shapes=in_vmem(large) + [VMEM((3, objects, width), f32), pltpu.SemaphoreType.DMA((9,))],
        compiler_params=params(),
    )(*[v.reshape(-1, lanes) for v in sums], small_all, context_sum, tokens_grad)
    return (
        mixed[None], tokens_grad[None], context_grad.reshape(1, context_count, ctx_width), cq, ckv, co, qkv, so, up, down, gains, biases, modw, modb,
    )


def solution(mesh):
    rows = P("obj", "blk", None)
    columns = P(None, "blk")
    return jax.shard_map(
        body,
        mesh=mesh,
        in_specs=(rows, P("obj", None, None), P("obj")) + (P(),) * 12 + (rows,),
        out_specs=(rows, rows, P("obj", None, None)) + (columns,) * 9
        + (P(None, None, "blk"), columns),
        check_vma=False,
    )
```

```python
import functools
import math

import jax
import jax.numpy as jnp
from jax import lax
from jax.experimental import pallas as pl
from jax.experimental.pallas import tpu as pltpu
from jax.sharding import PartitionSpec as P

D = 512
HEADS = 8
HEAD_DIM = 64
PAIRS = HEADS // 2
WIDE = 2 * HEAD_DIM
LOG2E = 1.4426950408889634
QUERY_FACTOR = LOG2E * HEAD_DIM ** (-0.5)
SCORE_FACTOR = HEAD_DIM ** (-0.5)
SAFE_SQUARE = (60.0 / QUERY_FACTOR) ** 2
EPSILON = 1e-06
GELU_A = 0.7978845608028654
GELU_B = 0.044715
MIB = 2**20

f32 = jnp.float32
bf16 = jnp.bfloat16
VMEM = pltpu.VMEM


def nn(a, b):
    return lax.dot_general(a, b, (((1,), (0,)), ((), ())), preferred_element_type=f32)


def nt(a, b):
    return lax.dot_general(a, b, (((1,), (1,)), ((), ())), preferred_element_type=f32)


def tn(a, b):
    return lax.dot_general(a, b, (((0,), (0,)), ((), ())), preferred_element_type=f32)


def whole():
    return pl.BlockSpec(memory_space=VMEM)


def params(mib=60):
    return pltpu.CompilerParams(vmem_limit_bytes=mib * MIB)


def lower_half(shape):
    return lax.broadcasted_iota(jnp.int32, shape, 1) % WIDE < HEAD_DIM


def own_half(shape, odd):
    lower = lower_half(shape)
    return jnp.logical_not(lower) if odd else lower


def normalize(x):
    center = x - jnp.mean(x, -1, keepdims=True)
    inverse = lax.rsqrt(jnp.mean(center * center, -1, keepdims=True) + EPSILON)
    return center * inverse, inverse


def modulate(x, gain, bias, shift, scale):
    normed, _ = normalize(x)
    return (normed * gain + bias) * (1.0 + scale) + shift


def modulate_back(g, x, gain, bias, scale):
    normed, inverse = normalize(x)
    affine = normed * gain + bias
    shift_grad = jnp.sum(g, 0, keepdims=True)
    scale_grad = jnp.sum(g * affine, 0, keepdims=True)
    a = g * (1.0 + scale)
    gain_grad = jnp.sum(a * normed, 0, keepdims=True)
    bias_grad = jnp.sum(a, 0, keepdims=True)
    n = a * gain
    back = inverse * (
        n - jnp.mean(n, -1, keepdims=True) - normed * jnp.mean(n * normed, -1, keepdims=True)
    )
    return back, jnp.concatenate([shift_grad, scale_grad, gain_grad, bias_grad], 0)


def norm_rows(gain_ref, bias_ref, mod_ref, j):
    gain = gain_ref[j : j + 1, :].astype(f32)
    bias = bias_ref[j : j + 1, :].astype(f32)
    shift = mod_ref[j : j + 1, :D]
    scale = mod_ref[j : j + 1, D:]
    return gain, bias, shift, scale


def head_sums(values, sign):
    rows = lax.broadcasted_iota(jnp.int32, (WIDE, WIDE), 0)
    cols = lax.broadcasted_iota(jnp.int32, (WIDE, WIDE), 1)
    block = jnp.where((rows < HEAD_DIM) != (cols < HEAD_DIM), sign, 0.0).astype(bf16)
    high = values.astype(bf16)
    low = (values - high.astype(f32)).astype(bf16)
    return nn(high, block) + nn(low, block)


def delta_lanes(product):
    parts = []
    for p in range(PAIRS):
        total = head_sums(product[:, p * WIDE : (p + 1) * WIDE], -1.0)
        high = total.astype(bf16).astype(f32)
        low = total - high
        lane = lax.broadcasted_iota(jnp.int32, total.shape, 1) % HEAD_DIM
        parts.append(jnp.where(lane == 0, high, jnp.where(lane == 1, low, 0.0)).astype(bf16))
    return jnp.concatenate(parts, 1)


def norm_top(x):
    rows = lax.broadcasted_iota(jnp.int32, (WIDE, WIDE), 0)
    cols = lax.broadcasted_iota(jnp.int32, (WIDE, WIDE), 1)
    block = jnp.where((rows < HEAD_DIM) == (cols < HEAD_DIM), 1.0, 0.0).astype(bf16)
    top = None
    for p in range(PAIRS):
        part = x[:, p * WIDE : (p + 1) * WIDE].astype(f32)
        here = jnp.max(nn((part * part).astype(bf16), block), 0, keepdims=True)
        top = here if top is None else jnp.maximum(top, here)
    return jnp.max(top)


def bounded(q, k):
    return norm_top(q) * norm_top(k) < SAFE_SQUARE


def pair_columns(head, offset=0):
    return pl.ds(pl.multiple_of(offset + head // 2 * WIDE, WIDE), WIDE)


def head_rows(head, offset=0):
    return pl.ds(pl.multiple_of(offset + head * HEAD_DIM, HEAD_DIM), HEAD_DIM)


def owned(shape, head):
    lane = lax.broadcasted_iota(jnp.int32, shape, 1)
    return lane // HEAD_DIM == head % 2


def key_rows(kv, head):
    k = kv[:, pair_columns(head)]
    return jnp.where(owned(k.shape, head), k, jnp.zeros_like(k))


def value_rows(kv, head, real_keys):
    v = kv[:, pair_columns(head, D)]
    v = jnp.where(owned(v.shape, head), v, jnp.ones_like(v))
    if real_keys < v.shape[0]:
        row = lax.broadcasted_iota(jnp.int32, v.shape, 0)
        v = jnp.where(row < real_keys, v, jnp.zeros_like(v))
    return v


def attend(head, safe, q, kv, w_ref, acc, top, real_keys):
    count = q.shape[0]
    step = min(256, count)

    def blocks(shifted):
        k = key_rows(kv, head)
        v = value_rows(kv, head, real_keys)
        for r in range(0, count, step):
            rows = slice(r, r + step)
            s = nt(q[rows, pair_columns(head)], k) * QUERY_FACTOR
            if shifted:
                most = jnp.max(s, -1, keepdims=True)
                s = s - most
            w = jnp.exp2(s).astype(bf16)
            w_ref[0, rows, :] = w
            acc[rows, :] = nn(w, v)
            if top is not None:
                top[rows, :] = jnp.broadcast_to(most, (step, WIDE)) if shifted else jnp.zeros((step, WIDE), f32)

    @pl.when(safe)
    def _():
        blocks(False)

    @pl.when(jnp.logical_not(safe))
    def _():
        blocks(True)


def paired(even, odd):
    lower = lower_half(even.shape)
    return jnp.where(lower, even, odd), pltpu.roll(jnp.where(lower, odd, even), HEAD_DIM, 1)


def attend_back(head, do, x, do_t, q_t, kv, w_ref, dq, dkvt, real_keys, chunk):
    left = jnp.where(owned((do.shape[0], WIDE), head), do[:, pair_columns(head)], x[:, pair_columns(head)])
    k = key_rows(kv, head)
    v = value_rows(kv, head, real_keys)
    keys = k.shape[0]
    chunk = chunk if keys % chunk == 0 else keys
    total = None
    for c in range(0, keys, chunk):
        cols = slice(c, c + chunk)
        w = w_ref[0, :, cols]
        dp = nt(left, v[cols])
        ds = (w.astype(f32) * dp).astype(bf16)
        part = nn(ds, k[cols])
        total = part if total is None else total + part
        dkvt[head_rows(head), cols] = (nn(q_t[head_rows(head), :], ds) * SCORE_FACTOR).astype(bf16)
        dkvt[head_rows(head, D), cols] = nn(do_t[head_rows(head), :], w).astype(bf16)
    total = total * SCORE_FACTOR

    dq[:, pair_columns(head)] += total


def cross_kernel(
    context_count, tokens, context, wq, wkv, wo, gain, bias, mod,
    second_in, after_one, q_hbm, pair_hbm, w_out, att_out, inv_out, q, pair, att, acc, safe_ref, sems,
):
    h = pl.program_id(0)
    saves = [pltpu.make_async_copy(q, q_hbm, sems.at[0]), pltpu.make_async_copy(pair, pair_hbm, sems.at[1])]

    @pl.when(h == 0)
    def _():
        first_in = modulate(tokens[...].astype(f32), *norm_rows(gain, bias, mod, 0)).astype(bf16)
        q[...] = nn(first_in, wq[...]).astype(bf16)
        pair[...] = nn(context[...], wkv[...]).astype(bf16)
        safe_ref[0] = bounded(q[...], pair[:, :D]).astype(jnp.int32)
        for save in saves:
            save.start()

    attend(h, safe_ref[0] == 1, q, pair, w_out, acc.at[h % 2], None, context_count)

    @pl.when(h % 2 == 1)
    def _():
        values, sums = paired(acc[0], acc[1])
        inverse = 1.0 / sums
        att_out[...] = values * inverse
        inv_out[...] = inverse
        att[:, pair_columns(h)] = att_out[...].astype(bf16)

    @pl.when(h == HEADS - 1)
    def _():
        one = tokens[...].astype(f32) + nn(att[...], wo[...])
        after_one[...] = one
        second_in[...] = modulate(one, *norm_rows(gain, bias, mod, 1)).astype(bf16)
        for save in saves:
            save.wait()


def project_keys(blocks, wqkv, kv):
    for i, block in enumerate(blocks):
        rows = block.shape[0]
        kv[i * rows : (i + 1) * rows, :] = nn(block[...], wqkv[:, D:]).astype(bf16)


def near_kernel(own, sibling, wqkv, w_out, q_hbm, kv_hbm, acc_out, top_out, q, kv, safe_ref, sems):
    h = pl.program_id(0)
    saves = [pltpu.make_async_copy(q, q_hbm, sems.at[0]), pltpu.make_async_copy(kv, kv_hbm, sems.at[1])]

    @pl.when(h == 0)
    def _():
        q[...] = nn(own[...], wqkv[:, :D]).astype(bf16)
        project_keys([own, sibling], wqkv, kv)
        safe_ref[0] = bounded(q[...], kv[:, :D]).astype(jnp.int32)
        for save in saves:
            save.start()

    attend(h, safe_ref[0] == 1, q, kv, w_out, acc_out.at[0], top_out.at[0], kv.shape[0])

    @pl.when(h == HEADS - 1)
    def _():
        for save in saves:
            save.wait()


def far_kernel(count, *refs):
    blocks = refs[:count]
    (wqkv, q, acc_near, top_near, w_out, kv_hbm, blocks_hbm, att_out, inv_near, inv_far,
     kv, acc, top, safe_ref, sems) = refs[count:]
    h = pl.program_id(0)
    save = pltpu.make_async_copy(kv, kv_hbm, sems.at[count])
    keeps = [pltpu.make_async_copy(block, blocks_hbm.at[i], sems.at[i]) for i, block in enumerate(blocks)]

    @pl.when(h == 0)
    def _():
        for keep in keeps:
            keep.start()
        project_keys(blocks, wqkv, kv)
        safe_ref[0] = bounded(q[...], kv[:, :D]).astype(jnp.int32)
        save.start()

    attend(h, safe_ref[0] == 1, q, kv, w_out, acc.at[h % 2], top.at[h % 2], kv.shape[0])

    @pl.when(h % 2 == 1)
    def _():
        lower = lower_half(acc_near.shape[1:])
        values_near, sums_near = paired(acc_near[0], acc_near[1])
        values_far, sums_far = paired(acc[0], acc[1])
        taken_near = jnp.where(lower, top_near[0], top_near[1])
        taken_far = jnp.where(lower, top[0], top[1])
        most = jnp.maximum(taken_near, taken_far)
        near = jnp.exp2(taken_near - most)
        far = jnp.exp2(taken_far - most)
        inverse = 1.0 / (sums_near * near + sums_far * far)
        near, far = near * inverse, far * inverse
        att_out[...] = values_near * near + values_far * far
        inv_near[...] = near
        inv_far[...] = far

    @pl.when(h == HEADS - 1)
    def _():
        for copy in keeps + [save]:
            copy.wait()


def slab_rows(depth, columns, parts):
    return depth * columns // parts // WIDE


def padded_rows(rows, objects):
    unit = 16 * objects
    return max(2, -(-rows // unit)) * unit


def slab_pieces(depth, each):
    lanes = math.gcd(each, WIDE)
    deep = depth * lanes // WIDE
    return [
        (i * deep, k * lanes, k * deep, i * lanes, deep, lanes)
        for i in range(each // lanes)
        for k in range(WIDE // lanes)
    ]


def slabs(out_ref, base, grad):
    parts = out_ref.shape[0]
    depth, columns = grad.shape
    each = columns // parts
    grad = grad.astype(out_ref.dtype)
    for b in range(parts):
        for to_row, to_lane, row, col, deep, lanes in slab_pieces(depth, each):
            start = b * each + col
            out_ref[b, base + to_row : base + to_row + deep, to_lane : to_lane + lanes] = grad[
                row : row + deep, start : start + lanes
            ]


def loop(total, block, body):
    if total % block:
        block = total

    def turn(i, carry):
        body(pl.ds(pl.multiple_of(i * block, block), block))
        return carry

    lax.fori_loop(0, total // block, turn, 0)


def slabs_by_rows(out_ref, base, depth, columns, make, block=256):
    parts = out_ref.shape[0]
    each = columns // parts
    if each % WIDE:
        slabs(out_ref, base, make(pl.ds(0, depth)))
        return
    block = math.gcd(depth, block)

    def put(rows):
        grad = make(rows).astype(out_ref.dtype)
        for b in range(parts):
            for i in range(each // WIDE):
                start = b * each + i * WIDE
                at = pl.ds(pl.multiple_of(base + i * depth + rows.start, 16), block)
                out_ref[b, at, :] = grad[:, start : start + WIDE]

    loop(depth, block, put)


def clear_tail(out_ref, used):
    if used < out_ref.shape[1]:
        rest = out_ref.shape[1] - used
        out_ref[:, used:, :] = jnp.zeros((out_ref.shape[0], rest, WIDE), out_ref.dtype)


def mlp_kernel(
    self_att, after_one, wo, gain, bias, mod, up_hbm, cot_hbm, down_hbm, near_hbm, far_hbm,
    mixed, grad_two, do_near, x_near, do_far, x_far, modes, g_hbm,
    up, cotangent, down, inv_near, inv_far, g_out, two, final, norm_grad, third_in, active, hidden_grad,
    fetch_sems, save_sems,
):
    fetches = [
        Fetch([pair], fetch_sems.at[pl.ds(i, 1)])
        for i, pair in enumerate(
            [(up_hbm, up), (cot_hbm, cotangent), (down_hbm, down), (near_hbm, inv_near), (far_hbm, inv_far)]
        )
    ]
    for fetch in fetches:
        fetch.start()
    count = self_att.shape[0]
    ff = up.shape[1]
    parts = g_out.shape[0]
    rows3 = norm_rows(gain, bias, mod, 2)
    up_base = slab_rows(D, D, parts)
    down_base = up_base + slab_rows(D, ff, parts)

    def start(rows):
        value = after_one[rows, :] + nn(self_att[rows, :].astype(bf16), wo[...])
        two[rows, :] = value
        final[rows, :] = value
        third_in[rows, :] = modulate(value, *rows3).astype(bf16)
        norm_grad[rows, :] = jnp.zeros_like(value)

    loop(count, 384, start)
    for fetch in fetches[:3]:
        fetch.wait()
    step = active.shape[1]

    def columns_of(f, dynamic):
        cols = pl.ds(pl.multiple_of(f, step), step) if dynamic else slice(f, f + step)

        def rows_of(rows):
            hidden = nn(third_in[rows, :], up[:, cols])
            square = hidden * hidden
            t = jnp.tanh(GELU_A * hidden * (1.0 + GELU_B * square))
            half = 0.5 * (1.0 + t)
            low = (hidden * half).astype(bf16)
            slope = half + 0.5 * hidden * (1.0 - t * t) * (GELU_A * (1.0 + 3.0 * GELU_B * square))
            low_grad = (nt(cotangent[rows, :], down[cols, :]) * slope).astype(bf16)
            active[rows, :] = low
            hidden_grad[rows, :] = low_grad
            final[rows, :] += nn(low, down[cols, :])
            norm_grad[rows, :] += nt(low_grad, up[:, cols])

        loop(count, 768, rows_of)
        up_part = tn(third_in[...], hidden_grad[...]).astype(bf16)
        down_part = tn(active[...], cotangent[...]).astype(bf16)
        each = ff // parts
        for i in range(step // WIDE):
            col = f + i * WIDE
            base = up_base + col % each // WIDE * D
            at = pl.ds(pl.multiple_of(base, 16), D) if dynamic else slice(base, base + D)
            g_out[col // each, at, :] = up_part[:, i * WIDE : (i + 1) * WIDE]
        each = D // parts
        if dynamic:
            for b in range(parts):
                for i in range(each // WIDE):
                    start = b * each + i * WIDE
                    at = pl.ds(pl.multiple_of(down_base + i * ff + f, 16), step)
                    g_out[b, at, :] = down_part[:, start : start + WIDE]
            return
        for to_row, to_lane, row, col, deep, lanes in slab_pieces(ff, each):
            if row <= f < row + deep:
                at = down_base + to_row + f - row
                for b in range(parts):
                    g_out[b, at : at + step, to_lane : to_lane + lanes] = down_part[
                        :, b * each + col : b * each + col + lanes
                    ]

    if D // parts % WIDE == 0:
        def turn(i, carry):
            columns_of(i * step, True)
            return carry

        lax.fori_loop(0, ff // step, turn, 0)
    else:
        for f in range(0, ff, step):
            columns_of(f, False)
    clear_tail(g_out, down_base + slab_rows(ff, D, parts))
    saves = [
        pltpu.make_async_copy(g_out.at[:, rows], g_hbm.at[:, rows], save_sems.at[i])
        for i, rows in enumerate((slice(up_base, g_out.shape[1]), slice(0, up_base)))
    ]
    saves[0].start()
    for fetch in fetches[3:]:
        fetch.wait()
    modes[...] = jnp.zeros_like(modes)
    self_grad = third_in

    def end(rows):
        mixed[rows, :] = final[rows, :].astype(bf16)
        back, sums = modulate_back(norm_grad[rows, :], two[rows, :], rows3[0], rows3[1], rows3[3])
        modes[...] += sums
        grad = cotangent[rows, :].astype(f32) + back
        grad_two[rows, :] = grad
        low = grad.astype(bf16)
        self_grad[rows, :] = low
        att_grad = nt(low, wo[...])
        for inv, do_out, x_out in ((inv_near, do_near, x_near), (inv_far, do_far, x_far)):
            do = (att_grad * inv[rows, :]).astype(bf16)
            do_out[rows, :] = do
            x_out[rows, :] = delta_lanes(do.astype(f32) * self_att[rows, :])

    loop(count, 384, end)
    slabs_by_rows(g_out, 0, D, D, lambda rows: tn(self_att[:, rows].astype(bf16), self_grad[...]))
    saves[1].start()
    for save in saves:
        save.wait()


def project_back(dkvt, wqkv, part_out):
    count, rows, _ = part_out.shape
    for b in range(count):
        part = nn(wqkv[:, D:], dkvt[:, b * rows : (b + 1) * rows])
        part_out[b] = part.astype(bf16).T


class Mover:
    def __init__(self, send, recv):
        self.send, self.recv = send, recv
        self.copies = []
        place, obj = lax.axis_index("blk"), lax.axis_index("obj")
        self.chips = lax.axis_size("blk") // 2
        self.columns = lax.axis_size("obj") // 2
        self.core, self.chip = lax.rem(place, 2), place // 2
        self.side, self.column = lax.rem(obj, 2), obj // 2
        self.sibling = {"blk": self.chip * 2 + 1 - self.core}
        self.chip_ids = [lax.rem(self.chip + d, self.chips) for d in range(1, self.chips)]
        self.chip_peers = [{"blk": c * 2 + self.core} for c in self.chip_ids]
        self.across = {"obj": self.column * 2 + 1 - self.side}
        objects = lax.axis_size("obj")
        self.obj = obj
        self.object_ids = [lax.rem(obj + d, objects) for d in range(1, objects)]
        self.object_peers = [{"obj": o} for o in self.object_ids]
        self.column_ids = [lax.rem(self.column + d, self.columns) for d in range(1, self.columns)]
        self.column_peers = [{"obj": c * 2 + self.side} for c in self.column_ids]

    def barrier(self, all_objects=False):
        everyone = [self.sibling] + self.chip_peers
        everyone += self.object_peers if all_objects else [self.across] + self.column_peers
        semaphore = pltpu.get_barrier_semaphore()
        for target in everyone:
            pl.semaphore_signal(semaphore, inc=1, device_id=target, device_id_type=pl.DeviceIdType.MESH)
        pl.semaphore_wait(semaphore, len(everyone))

    def copy(self, src, dst, target):
        at = len(self.copies)
        made = pltpu.make_async_remote_copy(
            src_ref=src, dst_ref=dst, send_sem=self.send.at[at], recv_sem=self.recv.at[at],
            device_id=target, device_id_type=pl.DeviceIdType.MESH,
        )
        self.copies.append(made)
        return made

    def drain(self):
        for made in self.copies:
            made.wait_send()


def begin(copies):
    for made in copies:
        made.start()


def arrive(copies):
    for made in copies:
        made.wait_recv()


def added(*values):
    total = values[0].astype(f32)
    for value in values[1:]:
        total = total + value.astype(f32)
    return total.astype(bf16)


def cut(rows, objects):
    unit = 16 * objects
    first = (rows // unit + 1) // 2 * unit
    return first, rows - first


def in_groups(rows, objects, groups):
    return cut(rows, objects) if groups == 2 else (rows,)


class Gather:
    @staticmethod
    def scratch(chips, rows, objects, lanes):
        first, second = cut(rows, objects)
        return [
            VMEM((chips, rows, lanes), bf16),
            VMEM((max(chips - 1, 1), first, lanes), bf16), VMEM((2, first // 2, lanes), bf16), VMEM((first // 2, lanes), bf16),
            VMEM((chips, second // 2, lanes), bf16), VMEM((chips, second // 2, lanes), bf16),
            VMEM((max(chips - 1, 1), second // 2, lanes), bf16),
        ]

    @staticmethod
    def copies(chips):
        return 2 * chips + 2 * (chips - 1) + 1 + chips

    def __init__(self, mover, g, scratch, out_first, out_second):
        self.mover, self.g = mover, g
        self.mine, self.far0, self.flat0, self.across0, self.across1, self.mine1, self.far1 = scratch
        self.out0, self.out1 = out_first, out_second
        first, half1 = self.far0.shape[1], self.mine1.shape[1]
        m, chips = mover, mover.chips
        self.rows = (slice(0, first), slice(first, first + 2 * half1))
        other = 1 - m.core
        self.core = [
            [m.copy(g.at[2 * j + other, rows], self.mine.at[j, rows], m.sibling) for j in range(chips)]
            for rows in self.rows
        ]
        self.chip0 = [
            m.copy(self.mine.at[c, self.rows[0]], self.far0.at[d], peer)
            for d, (c, peer) in enumerate(zip(m.chip_ids, m.chip_peers))
        ]
        self.side0 = [m.copy(self.flat0.at[1 - m.side], self.across0, m.across)]
        away = pl.ds(pl.multiple_of(first + (1 - m.side) * half1, 16), half1)
        self.kept = pl.ds(pl.multiple_of(first + m.side * half1, 16), half1)
        self.side1 = [m.copy(self.mine.at[j, away], self.across1.at[j], m.across) for j in range(chips)]
        self.chip1 = [
            m.copy(self.mine1.at[c], self.far1.at[d], peer)
            for d, (c, peer) in enumerate(zip(m.chip_ids, m.chip_peers))
        ]

    def step0(self):
        begin(self.core[0] + self.core[1])

    def step1(self):
        for group, after in ((0, self.chip0), (1, self.side1)):
            arrive(self.core[group])
            rows = self.rows[group]
            for j in range(self.mover.chips):
                self.mine[j, rows] = added(self.g[2 * j + self.mover.core, rows], self.mine[j, rows])
            begin(after)

    def step2(self):
        m = self.mover
        arrive(self.chip0)
        total = added(self.mine[m.chip, self.rows[0]], *[self.far0[d] for d in range(m.chips - 1)])
        self.flat0[...] = total.reshape(self.flat0.shape)
        begin(self.side0)
        arrive(self.side1)
        for j in range(m.chips):
            self.mine1[j] = added(self.mine[j, self.kept], self.across1[j])
        begin(self.chip1)

    def step3(self):
        m = self.mover
        arrive(self.side0)
        self.out0[...] = added(self.flat0[m.side], self.across0[...])
        arrive(self.chip1)
        self.out1[...] = added(self.mine1[m.chip], *[self.far1[d] for d in range(m.chips - 1)])


class Spread:
    @staticmethod
    def scratch(objects, half, lanes):
        columns = objects // 2
        return VMEM((max(columns - 1, 1), half // columns, lanes), bf16)

    @staticmethod
    def copies(objects):
        return 2 * (objects // 2 - 1)

    def __init__(self, mover, half, taken, out):
        m = mover
        self.mover, self.half, self.taken, self.out = mover, half, taken, out
        piece = taken.shape[1]
        self.piece = pl.ds(pl.multiple_of(m.column * piece, 16), piece)
        self.sums = [
            m.copy(half.at[pl.ds(pl.multiple_of(c * piece, 16), piece)], taken.at[d], peer)
            for d, (c, peer) in enumerate(zip(m.column_ids, m.column_peers))
        ]
        own = out.at[m.column]
        self.shares = [m.copy(own, own, peer) for peer in m.column_peers]

    def step0(self):
        begin(self.sums)

    def step1(self):
        arrive(self.sums)
        m = self.mover
        self.out[m.column] = added(self.half[self.piece], *[self.taken[d] for d in range(m.columns - 1)])
        begin(self.shares)

    def step2(self):
        arrive(self.shares)


class Cross:
    def __init__(self, mover, own, other):
        self.own, self.other = own, other
        self.copies = [mover.copy(own, other, mover.across)]

    def start(self):
        begin(self.copies)

    def wait(self):
        arrive(self.copies)


def put_sides(mover, own, other, out):
    out[mover.side] = own[...]
    out[1 - mover.side] = other[...]


class Fetch:
    def __init__(self, pairs, sems):
        self.copies = [pltpu.make_async_copy(src, dst, sems.at[i]) for i, (src, dst) in enumerate(pairs)]

    def start(self):
        begin(self.copies)

    def wait(self):
        for made in self.copies:
            made.wait()


def self_back_kernel(
    count, do_far, x_far, do_near, x_near, q, kv_far, kv_near_hbm, w_far, w_near, wqkv_hbm, g_early, *refs
):
    late_hbm = refs[:2] + tuple(refs[2].at[i] for i in range(count))
    (norm_grad, g_out, out0, out1, dq, dkvt_far, dkvt_near, do_far_t, do_near_t, q_t, far_parts, near_parts,
     from_sibling, chip_sums, from_chips, near_sibling, half0, half1, taken0, taken1, sums0, sums1,
     kv_near, wqkv) = refs[3:27]
    late = refs[27 : count + 29]
    own, sibling, blocks = late[0], late[1], late[2:]
    gather_scratch, sems, moving = refs[count + 29 : -3], refs[-3], refs[-2:]
    h = pl.program_id(0)
    fetch = Fetch(list(zip((kv_near_hbm, wqkv_hbm) + tuple(late_hbm), (kv_near, wqkv) + tuple(late))), sems)
    m = Mover(*moving)
    gather = Gather(m, g_early, gather_scratch, half0, half1)
    spreads = [Spread(m, half0, taken0, sums0), Spread(m, half1, taken1, sums1)]
    chips = m.chips
    far_core = [m.copy(far_parts.at[2 * d + 1], from_sibling.at[d], m.sibling) for d in range(chips - 1)]
    back = [{"blk": lax.rem(m.chip + chips - d, chips) * 2 + m.core} for d in range(1, chips)]
    far_chip = [m.copy(chip_sums.at[d], from_chips.at[d], back[d]) for d in range(chips - 1)]
    near_core = [m.copy(near_parts.at[1], near_sibling, m.sibling)]

    @pl.when(h == 0)
    def _():
        m.barrier()
        gather.step0()
        fetch.start()
        do_far_t[...] = do_far[...].T
        q_t[...] = q[...].T
        dq[...] = jnp.zeros_like(dq)

    @pl.when(h == 1)
    def _():
        gather.step1()

    @pl.when(h == 6)
    def _():
        gather.step2()

    @pl.when(h == HEADS)
    def _():
        fetch.wait()
        project_back(dkvt_far, wqkv, far_parts)
        begin(far_core)
        gather.step3()
        for spread in spreads:
            spread.step0()
        do_near_t[...] = do_near[...].T

    @pl.when(h == HEADS + 1)
    def _():
        arrive(far_core)
        for d in range(chips - 1):
            chip_sums[d] = added(far_parts[2 * d], from_sibling[d])
        begin(far_chip)

    @pl.when(h == HEADS + 4)
    def _():
        spreads[0].step1()

    @pl.when(h == HEADS + 5)
    def _():
        spreads[1].step1()

    @pl.when(h < HEADS)
    def _():
        attend_back(h, do_far, x_far, do_far_t, q_t, kv_far, w_far, dq, dkvt_far, kv_far.shape[0], 512)

    @pl.when(h >= HEADS)
    def _():
        attend_back(h - HEADS, do_near, x_near, do_near_t, q_t, kv_near, w_near, dq, dkvt_near, kv_near.shape[0], 512)

    @pl.when(h == 2 * HEADS - 1)
    def _():
        project_back(dkvt_near, wqkv, near_parts)
        begin(near_core)
        dq_low = dq[...].astype(bf16)
        rows = own.shape[0]
        grad = nn(dkvt_near[:, :rows], own[...]) + nn(dkvt_near[:, rows:], sibling[...])
        for i, block in enumerate(blocks):
            grad = grad + nn(dkvt_far[:, i * rows : (i + 1) * rows], block[...])
        slabs(g_out, 0, jnp.concatenate([tn(own[...], dq_low), grad.T], 1))
        clear_tail(g_out, slab_rows(D, 3 * D, g_out.shape[0]))
        total = nt(dq_low, wqkv[:, :D]) + near_parts[0].astype(f32)
        arrive(far_chip)
        for d in range(chips - 1):
            total = total + from_chips[d].astype(f32)
        arrive(near_core)
        norm_grad[...] = total + near_sibling[...].astype(f32)
        for spread, out in zip(spreads, (out0, out1)):
            spread.step2()
            out[...] = spread.out[...]
        m.drain()


class Job:
    @staticmethod
    def scratch(chips, rows, objects, lanes, groups):
        made = [VMEM((chips, rows, lanes), bf16), VMEM((max(chips - 1, 1), rows, lanes), bf16)]
        for n in in_groups(rows, objects, groups):
            piece = n // objects
            made += [
                VMEM((objects, piece, lanes), bf16), VMEM((objects - 1, piece, lanes), bf16),
                VMEM((objects, piece, lanes), bf16),
            ]
        return made

    @staticmethod
    def copies(chips, objects, groups):
        return groups * (2 * chips - 1 + 2 * (objects - 1))

    def __init__(self, mover, g, scratch):
        m = mover
        self.mover, self.g = m, g
        self.mine, self.far = scratch[:2]
        self.groups = []
        start = 0
        for shard, taken, sums in (scratch[i : i + 3] for i in range(2, len(scratch), 3)):
            objects, piece, _ = shard.shape
            rows = slice(start, start + objects * piece)
            start += objects * piece
            core = [m.copy(g.at[2 * j + 1 - m.core, rows], self.mine.at[j, rows], m.sibling) for j in range(m.chips)]
            chip = [
                m.copy(self.mine.at[c, rows], self.far.at[d, rows], peer)
                for d, (c, peer) in enumerate(zip(m.chip_ids, m.chip_peers))
            ]
            pieces = [
                m.copy(shard.at[o], taken.at[d], peer) for d, (o, peer) in enumerate(zip(m.object_ids, m.object_peers))
            ]
            shares = [m.copy(sums.at[m.obj], sums.at[m.obj], peer) for peer in m.object_peers]
            self.groups.append((rows, shard, taken, sums, core, chip, pieces, shares))

    def step0(self):
        for group in self.groups:
            begin(group[4])

    def step1(self):
        m = self.mover
        for rows, _, _, _, core, chip, _, _ in self.groups:
            arrive(core)
            for j in range(m.chips):
                self.mine[j, rows] = added(self.g[2 * j + m.core, rows], self.mine[j, rows])
            begin(chip)

    def step2(self):
        m = self.mover
        for rows, shard, _, _, _, chip, pieces, _ in self.groups:
            arrive(chip)
            total = added(self.mine[m.chip, rows], *[self.far[d, rows] for d in range(m.chips - 1)])
            shard[...] = total.reshape(shard.shape)
            begin(pieces)

    def step3(self):
        m = self.mover
        for _, shard, taken, sums, _, _, pieces, shares in self.groups:
            arrive(pieces)
            sums[m.obj] = added(shard[m.obj], *[taken[d] for d in range(taken.shape[0])])
            begin(shares)

    def finish(self, outs):
        for group, out in zip(self.groups, outs):
            arrive(group[7])
            out[...] = group[3][...]


def cross_back_kernel(
    context_count, groups, norm_grad, grad_two, after_one, tokens, context, q, pair, w, att, inv,
    wq, wkv, wo, gain, bias, mod, g_middle, modes_three, lifted, own0, own1,
    tokens_grad, ctx_result, small_result, early0, early1, *rest
):
    outs, rest = rest[: sum(groups)], rest[sum(groups) :]
    mid_outs, out_outs, late_outs = outs[: groups[0]], outs[groups[0] : -groups[2]], outs[-groups[2] :]
    (dkvt, do, x, do_t, q_t, dq, g_out, g_late, small, ctx,
     ctx_half, ctx_mine, ctx_far, small_half, small_mine, small_far, ctx_out, small_out, other0, other1, *rest) = rest
    h = pl.program_id(0)
    m = Mover(*rest[-2:])
    chips = m.chips
    ends = [2 + 3 * groups[0], 4 + 3 * (groups[0] + groups[1]), 6 + 3 * sum(groups)]
    middle = Job(m, g_middle, rest[: ends[0]])
    outer = Job(m, g_out, rest[ends[0] : ends[1]])
    late = Job(m, g_late, rest[ends[1] : ends[2]])
    early = [Cross(m, own0, other0), Cross(m, own1, other1)]
    ctx_rows = ctx.shape[0] // 2
    ctx_own = pl.ds(pl.multiple_of(m.core * ctx_rows, 16), ctx_rows)
    ctx_other = pl.ds(pl.multiple_of((1 - m.core) * ctx_rows, 16), ctx_rows)
    ctx_core = [m.copy(ctx.at[ctx_other], ctx_half, m.sibling)]
    ctx_chip = [m.copy(ctx_mine, ctx_far.at[d], m.chip_peers[d]) for d in range(chips - 1)]
    ctx_back = [m.copy(ctx_out.at[ctx_own], ctx_out.at[ctx_own], m.sibling)]
    small_core = [m.copy(small, small_half, m.sibling)]
    small_chip = [m.copy(small_mine, small_far.at[d], m.chip_peers[d]) for d in range(chips - 1)]
    small_share = [m.copy(small_out.at[m.obj], small_out.at[m.obj], peer) for peer in m.object_peers]
    late_base = slab_rows(D, D, g_late.shape[0])

    @pl.when(h == 0)
    def _():
        m.barrier(True)
        middle.step0()
        rows = norm_rows(gain, bias, mod, 1)
        back, sums = modulate_back(norm_grad[...], after_one[...], rows[0], rows[1], rows[3])
        grad_one = grad_two[...] + back
        tokens_grad[...] = grad_one
        small[4:8, :] = sums
        small[8:12, :] = modes_three[...]
        for i in range(2):
            row = lifted[:, i * D : (i + 1) * D].astype(f32)
            small[12 + i : 13 + i, :] = row * (0.5 / chips)
        small[14:16, :] = jnp.zeros((2, D), f32)
        cross_grad = grad_one.astype(bf16)
        middle.step1()
        slabs(g_out, 0, tn(att[...].astype(bf16), cross_grad))
        clear_tail(g_out, slab_rows(D, D, g_out.shape[0]))
        outer.step0()
        do[...] = (nt(cross_grad, wo[...]) * inv[...]).astype(bf16)
        x[...] = delta_lanes(do[...].astype(f32) * att[...])
        do_t[...] = do[...].T
        q_t[...] = q[...].T
        dq[...] = jnp.zeros_like(dq)

    @pl.when(h == 1)
    def _():
        outer.step1()

    @pl.when(h == 4)
    def _():
        middle.step2()

    @pl.when(h == 5)
    def _():
        outer.step2()
        for cross in early:
            cross.start()

    attend_back(h, do, x, do_t, q_t, pair, w, dq, dkvt, context_count, pair.shape[0])

    @pl.when(h == HEADS - 1)
    def _():
        dq_low = dq[...].astype(bf16)
        first = tokens[...].astype(f32)
        rows = norm_rows(gain, bias, mod, 0)
        first_in = modulate(first, *rows).astype(bf16)
        slabs(g_late, 0, tn(first_in, dq_low))
        real = lax.broadcasted_iota(jnp.int32, dkvt.shape, 1) < context_count
        kept = jnp.where(real, dkvt[...], jnp.zeros_like(dkvt))
        slabs(g_late, late_base, nn(kept, context[...]).T)
        clear_tail(g_late, late_base + slab_rows(context.shape[1], 2 * D, g_late.shape[0]))
        late.step0()
        ctx[...] = tn(dkvt[...], wkv[...].T).astype(bf16)
        begin(ctx_core)
        late.step1()
        middle.step3()
        outer.step3()

        back, sums = modulate_back(nt(dq_low, wq[...]), first, rows[0], rows[1], rows[3])
        small[0:4, :] = sums
        begin(small_core)
        late.step2()
        arrive(ctx_core)
        ctx_mine[...] = added(ctx[ctx_own], ctx_half[...])
        begin(ctx_chip)
        arrive(small_core)
        small_mine[...] = small[...] + small_half[...]
        begin(small_chip)
        tokens_grad[...] = tokens_grad[...] + back
        for cross, own, out in zip(early, (own0, own1), (early0, early1)):
            cross.wait()
            put_sides(m, own, cross.other, out)
        arrive(small_chip)
        total = small_mine[...]
        for d in range(chips - 1):
            total = total + small_far[d]
        small_out[m.obj] = total
        begin(small_share)
        late.step3()
        arrive(ctx_chip)
        ctx_out[ctx_own] = added(ctx_mine[...], *[ctx_far[d] for d in range(chips - 1)])
        begin(ctx_back)
        middle.finish(mid_outs)
        outer.finish(out_outs)
        arrive(small_share)
        small_result[...] = small_out[...]
        arrive(ctx_back)
        ctx_result[...] = ctx_out[...]
        late.finish(late_outs)
        m.drain()


def finish_kernel(parts, groups, *refs):
    sums, refs = refs[: 2 + sum(groups)], refs[2 + sum(groups) :]
    small, ctx, tokens_in, gains, biases, modb, ctx_out, tokens_out = refs[:8]
    results, (so, up, down, qkv, co, cq, ckv, modw), mode, sems = refs[8:16], refs[16:24], refs[24], refs[25]
    saves = []

    def save(src, dst):
        made = pltpu.make_async_copy(src, dst, sems.at[len(saves)])
        made.start()
        saves.append(made)

    save(tokens_in, tokens_out)
    place = lax.axis_index("blk")
    width = 2 * D // parts
    each = D // parts

    def put(out, total, base):
        depth, columns = out.shape
        for to_row, to_lane, row, col, deep, lanes in slab_pieces(depth, columns):
            out[row : row + deep, col : col + lanes] = total[
                base + to_row : base + to_row + deep, to_lane : to_lane + lanes
            ].astype(f32)
        for scratch, result in zip((so, up, down, qkv, co, cq, ckv), results):
            if scratch is out:
                save(out, result)
        return base + slab_rows(depth, columns, 1)

    join = lambda start, count: jnp.concatenate([ref[...] for ref in sums[start : start + count]], 0)
    early = join(0, 2)
    base = put(so, early, 0)
    base = put(up, early, base)
    put(down, early, base)
    put(qkv, join(2, groups[0]), 0)
    put(co, join(2 + groups[0], groups[1]), 0)
    late = join(2 + groups[0] + groups[1], groups[2])
    base = put(cq, late, 0)
    put(ckv, late, base)
    lifted = jnp.concatenate([small[:, 12, :], small[:, 13, :]], 1)
    summed = jnp.sum(small[...], 0)
    for b in range(parts):
        @pl.when(place == b)
        def _():
            row, col = b * width // D, b * width % D
            for j in range(3):
                mode[j] = small[:, 4 * j + row, col : col + width]
                gains[j : j + 1, :] = summed[4 * j + 2 : 4 * j + 3, b * each : (b + 1) * each]
                biases[j : j + 1, :] = summed[4 * j + 3 : 4 * j + 4, b * each : (b + 1) * each]
    for j in range(3):
        modw[j] = lax.dot_general(
            lifted, mode[j], (((0,), (0,)), ((), ())), precision=lax.Precision.HIGHEST, preferred_element_type=f32
        )
        modb[j : j + 1, :] = jnp.sum(mode[j], 0, keepdims=True)
    save(modw, results[7])
    ctx_out[...] = ctx[: ctx_out.shape[0], :].astype(f32).reshape(ctx_out.shape)
    for made in saves:
        made.wait()


def shape(dims, dtype):
    return jax.ShapeDtypeStruct(tuple(dims), dtype)


def body(
    tokens, context, camera_groups, camera_table, cross_query, cross_kv, cross_out, self_qkv,
    self_out, mlp_up, mlp_down, norm_gain, norm_bias, mod_weight, mod_bias, cotangent,
):
    parts = lax.axis_size("blk")
    tokens = tokens[0]
    cotangent = cotangent[0]
    context_count = context.shape[1]
    rows = tokens.shape[0]
    length = rows * parts
    ff = mlp_up.shape[1]
    cam_width = mod_weight.shape[1]
    ctx_width = context.shape[2]
    padded = -(-context_count // 128) * 128
    context_rows = jnp.pad(context[0], ((0, padded - context_count), (0, 0)), mode="edge")

    picked = (
        camera_groups[:, None] == jnp.arange(camera_table.shape[0], dtype=jnp.int32)[None, :]
    ).astype(bf16)
    camera = jnp.dot(picked, camera_table, preferred_element_type=f32)
    lifted = jax.nn.silu(camera).astype(bf16)
    mod = (
        jnp.einsum("oc,jcm->ojm", lifted, mod_weight, preferred_element_type=f32)
        + mod_bias.astype(f32)
    )[0]

    def near_hop(block):
        return lax.ppermute(block, "blk", [(i, i ^ 1) for i in range(parts)])

    def chip_hop(block, distance):
        route = [(i, (i // 2 + distance) % chips * 2 + i % 2) for i in range(parts)]
        return lax.ppermute(block, "blk", route)

    chips = parts // 2
    objects = lax.axis_size("obj")
    full = lambda *dims: pl.BlockSpec(dims, lambda h: (0,) * len(dims))
    head = lambda keys: pl.BlockSpec((1, rows, keys), lambda h: (h, 0, 0))
    row_full = full(rows, D)
    row_f32, row_bf16 = shape((rows, D), f32), shape((rows, D), bf16)
    two_heads = VMEM((2, rows, WIDE), f32)
    flag = pltpu.SMEM((1,), jnp.int32)
    anywhere = pl.BlockSpec(memory_space=pl.ANY)
    pair_block = pl.BlockSpec((rows, WIDE), lambda h: (0, h // 2))
    head_block = pl.BlockSpec((1, rows, WIDE), lambda h: (h, 0, 0))
    heads_block = pl.BlockSpec((2, rows, WIDE), lambda h: (h // 2, 0, 0))
    sums_f32 = shape((HEADS, rows, WIDE), f32)
    transposed = [VMEM((D, rows), bf16), VMEM((D, rows), bf16)]
    norm_full = [full(3, D), full(3, D), full(3, 2 * D)]

    def call(kernel, name, us, outs, ins, out_specs, scratch=(), collective_id=None, mib=60, free=None, **more):
        if free is not None:
            outs = [item if i in free else pltpu.HBM(item.shape, item.dtype) for i, item in enumerate(outs)]
        return pl.pallas_call(
            kernel, name=name, out_shape=outs, in_specs=ins, out_specs=out_specs, scratch_shapes=list(scratch),
            cost_estimate=pl.CostEstimate(flops=int(us * 1.1e9), bytes_accessed=int(us * 3.6e6), transcendentals=0),
            compiler_params=params(mib) if collective_id is None else pltpu.CompilerParams(
                vmem_limit_bytes=62 * MIB, collective_id=collective_id, has_side_effects=True
            ), **more,
        )

    second_in, after_one, cross_q, cross_pair, cross_w, cross_att, cross_inv = call(
        functools.partial(cross_kernel, context_count), "cross_forward", 15,
        [row_bf16, row_f32, row_bf16, shape((padded, 2 * D), bf16), shape((HEADS, rows, padded), bf16), row_f32, row_f32],
        [row_full, full(padded, ctx_width), full(D, D), full(ctx_width, 2 * D), full(D, D)] + norm_full,
        [row_full, row_full, anywhere, anywhere, head(padded), pair_block, pair_block],
        [VMEM((rows, D), bf16), VMEM((padded, 2 * D), bf16), VMEM((rows, D), bf16), two_heads, flag,
         pltpu.SemaphoreType.DMA((2,))], grid=(HEADS,), mib=32, free=(0,),
    )(tokens, context_rows, cross_query, cross_kv, cross_out, norm_gain, norm_bias, mod)

    sibling_in = near_hop(second_in)
    chip_in = [chip_hop(second_in, d) for d in range(1, chips)]
    near_keys, far_keys = 2 * rows, 2 * rows * (chips - 1)
    near_w, self_q, near_kv, near_acc, near_top = call(
        near_kernel, "near_forward", 16,
        [shape((HEADS, rows, near_keys), bf16), row_bf16, shape((near_keys, 2 * D), bf16), sums_f32, sums_f32],
        [row_full, row_full, full(D, 3 * D)],
        [head(near_keys), anywhere, anywhere, head_block, head_block],
        [VMEM((rows, D), bf16), VMEM((near_keys, 2 * D), bf16), flag, pltpu.SemaphoreType.DMA((2,))], grid=(HEADS,), mib=32, free=(),
    )(second_in, sibling_in, self_qkv)
    chip_in, near_kv = lax.optimization_barrier((chip_in, near_kv))
    far_in = []
    for block in chip_in:
        far_in += [block, near_hop(block)]
    count = len(far_in)
    far_w, far_kv, far_rows, self_att, near_inv, far_inv = call(
        functools.partial(far_kernel, count), "far_forward", 16,
        [shape((HEADS, rows, far_keys), bf16), shape((far_keys, 2 * D), bf16), shape((count, rows, D), bf16),
         row_f32, row_f32, row_f32],
        [row_full] * count + [full(D, 3 * D), row_full, heads_block, heads_block],
        [head(far_keys), anywhere, anywhere, pair_block, pair_block, pair_block],
        [VMEM((far_keys, 2 * D), bf16), two_heads, two_heads, flag, pltpu.SemaphoreType.DMA((count + 1,))], grid=(HEADS,), mib=32, free=(),
    )(*far_in, self_qkv, *[pltpu.with_memory_space_constraint(v, pltpu.HBM) for v in (self_q, near_acc, near_top)])

    lanes = WIDE
    tall = lambda columns, depth: slab_rows(depth, columns, parts)
    early = padded_rows(tall(D, D) + tall(ff, D) + tall(D, ff), objects)
    mixed, grad_two, near_do, near_x, far_do, far_x, modes_three, g_early = call(
        mlp_kernel, "feed_forward", 20,
        [row_bf16, row_f32, row_bf16, row_bf16, row_bf16, row_bf16, shape((4, D), f32), shape((parts, early, lanes), bf16)],
        [whole()] * 6 + [anywhere] * 5, [whole()] * 7 + [anywhere],
        [VMEM((D, ff), bf16), VMEM((rows, D), bf16), VMEM((ff, D), bf16), VMEM((rows, D), f32), VMEM((rows, D), f32),
         VMEM((parts, early, lanes), bf16), VMEM((rows, D), f32), VMEM((rows, D), f32), VMEM((rows, D), f32),
         VMEM((rows, D), bf16), VMEM((rows, 512), bf16), VMEM((rows, 512), bf16),
         pltpu.SemaphoreType.DMA((5,)), pltpu.SemaphoreType.DMA((2,))],
    )(self_att, after_one, self_out, norm_gain, norm_bias, mod, mlp_up, cotangent, mlp_down, near_inv, far_inv)

    unit = objects // 2
    moving = lambda copies: [pltpu.SemaphoreType.DMA((copies,)), pltpu.SemaphoreType.DMA((copies,))]
    halves = lambda rows: [shape((n // 2, lanes), bf16) for n in cut(rows, objects)]
    half_vmem = lambda rows: [VMEM((n // 2, lanes), bf16) for n in cut(rows, objects)]
    spread_outs = lambda rows: [shape((2, unit, n // objects, lanes), bf16) for n in cut(rows, objects)]
    own_outs = lambda rows: [shape((unit, n // objects, lanes), bf16) for n in cut(rows, objects)]
    taken = lambda rows: [Spread.scratch(objects, n // 2, lanes) for n in cut(rows, objects)]
    in_vmem = lambda shapes: [VMEM(item.shape, item.dtype) for item in shapes]
    once = lambda *dims: pl.BlockSpec(dims, lambda h: (0,) * len(dims), pipeline_mode=pl.Buffered(1))
    like = lambda shapes: [once(*item.shape) for item in shapes]
    row_once = once(rows, D)

    middle = padded_rows(tall(3 * D, D), objects)
    own_shapes = own_outs(early)
    hops = VMEM((chips - 1, rows, D), bf16)
    row_vmem = VMEM((rows, D), bf16)
    norm_grad, g_middle, own0, own1 = call(
        functools.partial(self_back_kernel, count), "self_backward", 60,
        [row_f32, shape((parts, middle, lanes), bf16)] + own_shapes,
        [row_once] * 5 + [once(far_keys, 2 * D), anywhere,
         pl.BlockSpec((1, rows, far_keys), lambda h: (jnp.minimum(h, HEADS - 1), 0, 0)),
         pl.BlockSpec((1, rows, near_keys), lambda h: (jnp.maximum(h - HEADS, 0), 0, 0)),
         anywhere, once(parts, early, lanes)] + [anywhere] * 3,
        [row_once, once(parts, middle, lanes)] + like(own_shapes),
        [VMEM((rows, D), f32), VMEM((2 * D, far_keys), bf16), VMEM((2 * D, near_keys), bf16)]
        + [VMEM((D, rows), bf16)] * 3 + [VMEM((count, rows, D), bf16), VMEM((2, rows, D), bf16)]
        + [hops, hops, hops, row_vmem] + half_vmem(early) + taken(early) + in_vmem(own_shapes)
        + [VMEM((near_keys, 2 * D), bf16), VMEM((D, 3 * D), bf16)] + [row_vmem] * (2 + count)
        + Gather.scratch(chips, early, objects, lanes) + [pltpu.SemaphoreType.DMA((count + 4,))]
        + moving(Gather.copies(chips) + 2 * (chips - 1) + 1 + 2 * Spread.copies(objects)),
        grid=(2 * HEADS,), collective_id=1,
    )(far_do, far_x, near_do, near_x, self_q, far_kv, near_kv, far_w, near_w, self_qkv, g_early,
      second_in, sibling_in, far_rows)

    outer = padded_rows(tall(D, D), objects)
    groups = (1, 1, 1)
    late = padded_rows(tall(D, D) + tall(2 * D, ctx_width), objects)
    sums = spread_outs(early) + [
        shape((objects, n // objects, lanes), bf16) for total, n_groups in zip((middle, outer, late), groups) for n in in_groups(total, objects, n_groups)
    ]
    ctx_half = VMEM((padded // 2, ctx_width), bf16)
    small_vmem = VMEM((16, D), f32)
    tokens_grad, context_sum, small_all, *sums = call(
        functools.partial(cross_back_kernel, context_count, groups), "cross_backward", 20,
        [row_f32, shape((padded, ctx_width), bf16), shape((objects, 16, D), f32)] + sums,
        [row_once] * 4 + [once(padded, ctx_width), row_once, once(padded, 2 * D), head(padded), row_once, row_once,
         once(D, D), once(ctx_width, 2 * D), once(D, D)] + norm_full + [once(parts, middle, lanes), full(4, D), full(1, cam_width)]
        + like(own_shapes),
        [row_once, once(padded, ctx_width), once(objects, 16, D)] + like(sums),
        [VMEM((2 * D, padded), bf16), row_vmem, row_vmem] + transposed + [VMEM((rows, D), f32)]
        + [VMEM((parts, outer, lanes), bf16), VMEM((parts, late, lanes), bf16), small_vmem, VMEM((padded, ctx_width), bf16)]
        + [ctx_half, ctx_half, VMEM((chips - 1, padded // 2, ctx_width), bf16)]
        + [small_vmem, small_vmem, VMEM((chips - 1, 16, D), f32)]
        + [VMEM((padded, ctx_width), bf16), VMEM((objects, 16, D), f32)] + in_vmem(own_shapes)
        + Job.scratch(chips, middle, objects, lanes, groups[0]) + Job.scratch(chips, outer, objects, lanes, groups[1])
        + Job.scratch(chips, late, objects, lanes, groups[2])
        + moving(Job.copies(chips, objects, sum(groups)) + 2 + chips + 1 + chips + objects - 1),
        grid=(HEADS,), collective_id=2,
    )(
        norm_grad, grad_two, after_one, tokens, context_rows, cross_q, cross_pair, cross_w,
        cross_att, cross_inv, cross_query, cross_kv, cross_out, norm_gain, norm_bias, mod, g_middle, modes_three,
        lifted, own0, own1,
    )
    width = 2 * D // parts
    grads = lambda depth, columns: shape((depth, columns // parts), f32)
    large = [
        grads(D, D), grads(D, ff), grads(ff, D), grads(D, 3 * D), grads(D, D), grads(D, D), grads(ctx_width, 2 * D),
        shape((3, cam_width, width), f32),
    ]
    gains, biases, modb, context_grad, tokens_grad, so, up, down, qkv, co, cq, ckv, modw = pl.pallas_call(
        functools.partial(finish_kernel, parts, groups),
        name="finish",
        out_shape=[
            grads(3, D), grads(3, D), grads(3, 2 * D), shape((context_count, 1, ctx_width), f32), shape((rows, D), f32),
        ] + large,
        in_specs=[whole()] * (5 + sum(groups)),
        out_specs=[whole()] * 4 + [anywhere] * 9,
        scratch_shapes=in_vmem(large) + [VMEM((3, objects, width), f32), pltpu.SemaphoreType.DMA((9,))],
        compiler_params=params(),
    )(*[v.reshape(-1, lanes) for v in sums], small_all, context_sum, tokens_grad)
    return (
        mixed[None], tokens_grad[None], context_grad.reshape(1, context_count, ctx_width), cq, ckv, co, qkv, so, up, down, gains, biases, modw, modb,
    )


def solution(mesh):
    rows = P("obj", "blk", None)
    columns = P(None, "blk")
    return jax.shard_map(
        body,
        mesh=mesh,
        in_specs=(rows, P("obj", None, None), P("obj")) + (P(),) * 12 + (rows,),
        out_specs=(rows, rows, P("obj", None, None)) + (columns,) * 9
        + (P(None, None, "blk"), columns),
        check_vma=False,
    )
```
